128 devices in a mesh: tok: 8 (over x_lo, y), layer: 16 (over x_hi, z, core).
Axes of the slice: x: 4 (x_hi: 2, x_lo: 2; x = x_hi * 2 + x_lo), y: 4, z: 4, core: 2. Of those that a mesh axis runs over, the one named last changes fastest.
Arguments:
- cache_in: bfloat16 [64, 128, 2304], P('tok', None, 'layer'), may hold values from -6 to 6
- cache_out: bfloat16 [64, 128, 2304], P('tok', None, 'layer'), may hold values from -6 to 6
- read_list: int32 [8, 8], P('tok'), may hold values from 0 to 7, each once within a row
- live_blocks: int32 [8, 2], P('tok'), may hold values from 1 to 4, as said below
- encoder: bfloat16 [2, 2304, 8192], P(None, None, 'layer'), may hold values from -0.125 to 0.125
- enc_bias: float32 [2, 8192], P(None, 'layer'), may hold values from -4 to 4
- decoder: bfloat16 [3, 8192, 2304], P(None, 'layer'), may hold values from -0.046875 to 0.046875
Outputs:
- grad_encoder: float32 [2, 2304, 8192], P(None, 'tok', 'layer')
- grad_bias: float32 [2, 16, 512], P(None, 'layer', 'tok')
- grad_decoder: float32 [3, 8192, 2304], P(None, 'layer', 'tok')
The draws below stay inside these ranges and needn't reach their ends.
Inputs may be any that keep to these rules, and one draw needn't show every extreme that they name: `read_list`: in each group every one of the 8 cached blocks is named exactly once. `live_blocks`: each group has exactly one layer with all 4 blocks live; the other layers have fewer.
All inputs are finite; a program needn't handle non-finite values.
Results may differ from the reference program's by a relative error of at most 0.024.
Values may be sent and summed in bfloat16 or wider, within the bound.
No kernel may reach another device: no remote copies, remote signals or barrier semaphores. Data moves between devices by JAX's collectives and lax.ppermute only.
A program may use at most 128 MiB of HBM per device.

```python
import math
import jax
import jax.numpy as jnp
from jax import lax

D = 2304
FEATS = 8192
LAYERS = 2
BLK = 128
TB = 4
F_DEV = 512
PAIRS = 3
GROUPS = 8
BLOCKS = 8
TOK = 512
TOKENS = 4096


def draw_live_blocks(key, part):
    key = jax.random.fold_in(key, 7)
    first_key, second_key = jax.random.split(key)
    counts = jax.random.randint(first_key, (GROUPS, LAYERS), 1, TB)
    full_layer = jax.random.randint(second_key, (GROUPS, 1), 0, LAYERS)
    layer_ids = jnp.arange(LAYERS)[None, :]
    group_ids = jnp.arange(GROUPS)[:, None]
    counts = jnp.where(layer_ids == full_layer, TB, counts)
    single_layer = (full_layer[0, 0] + 1) % LAYERS
    counts = jnp.where((group_ids == 0) & (layer_ids == single_layer), 1, counts)
    return counts.astype(jnp.int32)


def levels(key, dims, cuts, least, high):
    def one(dim, blocks):
        steps = jax.random.uniform(jax.random.fold_in(jax.random.fold_in(key, 6), dim), (blocks,), jnp.float32, least / len(cuts), high / len(cuts))
        return jnp.repeat(jnp.exp(steps), dims[dim] // blocks).reshape((-1,) + (1,) * (len(dims) - dim - 1))

    factor_of = one(*cuts[0])
    for cut in cuts[1:]:
        factor_of = factor_of * one(*cut)
    return factor_of


def gaussian(key, dims, spread, reach, cuts=(), kind=jnp.bfloat16):
    array = jax.random.normal(key, dims, jnp.float32) * spread
    if len(cuts) > 0:
        array = levels(key, dims, cuts, -0.22, 0.18) * array
    return jnp.clip(array, min=-reach, max=reach).astype(kind)


def setup_inputs(seed: int = 0) -> dict:
    keys = jax.random.split(jax.random.key(seed), 8)
    return {
        "cache_in": gaussian(keys[0], (GROUPS * BLOCKS, BLK, D), 1.0, 6.0, ((0, 8), (2, 16))),
        "cache_out": gaussian(keys[1], (GROUPS * BLOCKS, BLK, D), 1.0, 6.0, ((0, 8), (2, 16))),
        "read_list": jax.vmap(lambda own: jax.random.permutation(own, BLOCKS))(jax.random.split(keys[2], GROUPS)).reshape((GROUPS, BLOCKS)).astype(jnp.int32),
        "live_blocks": draw_live_blocks(jax.random.fold_in(keys[7], 71), 0),
        "encoder": gaussian(keys[4], (LAYERS, D, FEATS), D ** -0.5, 0.125, ((2, 16),)),
        "enc_bias": gaussian(keys[5], (LAYERS, FEATS), 1.0, 4.0, ((1, 16),), jnp.float32),
        "decoder": gaussian(keys[6], (PAIRS, FEATS, D), (2 * FEATS) ** -0.5, 0.046875, ((1, 16),)),
    }


def activation_slope(pre_act):
    sigma = jax.nn.sigmoid(pre_act)
    return sigma + pre_act * sigma * (1.0 - sigma)

def rounded_sum(total, term):
    return total + lax.optimization_barrier(term.astype(jnp.bfloat16)).astype(jnp.float32)

def pair_slot(source, target):
    return target * (target + 1) // 2 + source

def reference(cache_in, cache_out, read_list, live_blocks, encoder, enc_bias, decoder):
    error_scale = 1.0 / math.sqrt(TOKENS)
    inputs_all = cache_in.reshape(GROUPS, BLOCKS, BLK, D)
    targets_all = cache_out.reshape(GROUPS, BLOCKS, BLK, D)
    row_blocks = jnp.arange(TOK, dtype=jnp.int32) // BLK

    def group_step(running, group_index):
        block_ids = read_list[group_index].astype(jnp.int32)
        inputs = jnp.take(inputs_all[group_index], block_ids, axis=0).reshape(LAYERS, TOK, D)
        targets = jnp.take(targets_all[group_index], block_ids, axis=0).reshape(LAYERS, TOK, D)
        live = (row_blocks[None, :] < live_blocks[group_index][:, None]).astype(jnp.float32)
        pre_list = []
        feat_list = []
        for layer in range(LAYERS):
            pre_act = jnp.dot(inputs[layer], encoder[layer], preferred_element_type=jnp.float32) + enc_bias[layer][None, :]
            pre_list.append(pre_act)
            feat_list.append((jax.nn.silu(pre_act) * live[layer][:, None]).astype(jnp.bfloat16))
        err_list = []
        for target in range(LAYERS):
            recon = jnp.zeros((TOK, D), jnp.float32)
            for source in range(target + 1):
                recon = recon + jnp.dot(feat_list[source], decoder[pair_slot(source, target)], preferred_element_type=jnp.float32)
            err_list.append(((recon - targets[target].astype(jnp.float32)) * live[target][:, None] * error_scale).astype(jnp.bfloat16))
        dec_terms = []
        gfeat_list = [jnp.zeros((TOK, FEATS), jnp.float32) for layer in range(LAYERS)]
        for target in range(LAYERS):
            for source in range(target + 1):
                weights = decoder[pair_slot(source, target)]
                dec_terms.append(lax.dot_general(feat_list[source], err_list[target], (((0,), (0,)), ((), ())), preferred_element_type=jnp.float32))
                gfeat_list[source] = gfeat_list[source] + lax.dot_general(err_list[target], weights, (((1,), (1,)), ((), ())), preferred_element_type=jnp.float32)
        enc_terms = []
        bias_terms = []
        for layer in range(LAYERS):
            gpre = (gfeat_list[layer] * live[layer][:, None] * activation_slope(pre_list[layer])).astype(jnp.bfloat16)
            enc_terms.append(lax.dot_general(inputs[layer], gpre, (((0,), (0,)), ((), ())), preferred_element_type=jnp.float32))
            bias_terms.append(lax.optimization_barrier(jnp.sum(gpre.astype(jnp.float32), axis=0)))
        updated = (rounded_sum(running[0], jnp.stack(enc_terms)), rounded_sum(running[1], jnp.stack(bias_terms)), rounded_sum(running[2], jnp.stack(dec_terms)))
        return (updated, None)
    start_sums = (jnp.zeros((LAYERS, D, FEATS), jnp.float32), jnp.zeros((LAYERS, FEATS), jnp.float32), jnp.zeros((PAIRS, FEATS, D), jnp.float32))
    sums, unused = lax.scan(group_step, start_sums, jnp.arange(GROUPS, dtype=jnp.int32))
    grad_bias = sums[1].reshape(LAYERS, FEATS // F_DEV, F_DEV)
    return (sums[0], grad_bias, sums[2])
```

```python
import functools
import math

import jax
import jax.numpy as jnp
from jax import lax
from jax.experimental import pallas as pl
from jax.experimental.pallas import tpu as pltpu
from jax.sharding import PartitionSpec as P

AXES = ("tok", "layer")
BF = jnp.bfloat16
F32 = jnp.float32
ROWS = 512
COLS = 144
HALF = 256
WIDE = 8 * COLS


def device_index(x, y, z, c):
    return ((x % 2) * 4 + y) * 16 + (x // 2) * 8 + z * 2 + c


def pairs_of(partner):
    out = []
    for x in range(4):
        for y in range(4):
            for z in range(4):
                for c in range(2):
                    out.append((device_index(x, y, z, c), device_index(*partner(x, y, z, c))))
    return out


def mask(step, c):
    return 1 if (step + c) % 2 == 0 else 3


def exchange(value, axis, step):
    def partner(x, y, z, c):
        m = mask(step, c)
        return {"x": (x ^ m, y, z, c), "y": (x, y ^ m, z, c), "z": (x, y, z ^ m, c)}[axis]

    return lax.ppermute(value, AXES, pairs_of(partner))


def to_other_core(value):
    return lax.ppermute(value, AXES, pairs_of(lambda x, y, z, c: (x, y, z, 1 - c)))


def to_mate(value, flip):
    return lax.ppermute(value, AXES, pairs_of(lambda x, y, z, c: (x ^ 1, y, z, c ^ flip)))


def activation_slope(pre_act):
    sigma = jax.nn.sigmoid(pre_act)
    return sigma + pre_act * sigma * (1.0 - sigma)


def mm(a, b, ca, cb):
    return lax.dot_general(a, b, (((ca,), (cb,)), ((), ())), preferred_element_type=F32)


def at(array, index, dim=0):
    starts = [jnp.int32(0)] * array.ndim
    starts[dim] = index
    sizes = list(array.shape)
    sizes[dim] = 1
    piece = lax.dynamic_slice(array, starts, sizes, allow_negative_indices=False)
    return piece.reshape(array.shape[:dim] + array.shape[dim + 1 :])


def slot_of(apart, core):
    on_core0 = apart ^ (apart >> 1)
    on_core1 = (on_core0 & 1) * 2 + (on_core0 >> 1)
    return jnp.where(core == 0, on_core0, on_core1)


def after(value, *others):
    return lax.optimization_barrier((value,) + others)


def order_kernel(turn, where_ref, w_ref, dep_ref, own_ref, give_ref):
    block = w_ref[0].T if turn else w_ref[0]
    core = where_ref[2]
    for zz in range(4):
        even = block[2 * zz * COLS : (2 * zz + 1) * COLS]
        odd = block[(2 * zz + 1) * COLS : (2 * zz + 2) * COLS]
        apart = zz ^ where_ref[3]
        own_ref[0, 0, slot_of(apart, core)] = jnp.where(core == 0, even, odd)
        give_ref[0, 0, slot_of(apart, 1 - core)] = jnp.where(core == 0, odd, even)


def ordered_weights(weights, where, dep, turn):
    count = weights.shape[0]
    if turn:
        in_spec = pl.BlockSpec((1, HALF, WIDE), lambda i, h, s: (i, s[0], h))
    else:
        in_spec = pl.BlockSpec((1, WIDE, HALF), lambda i, h, s: (i, h, s[0]))
    out_spec = pl.BlockSpec((1, 1, 4, COLS, HALF), lambda i, h, s: (i, (h + s[1]) % 2, 0, 0, 0))
    shape = jax.ShapeDtypeStruct((count, 2, 4, COLS, HALF), BF)
    return pl.pallas_call(
        functools.partial(order_kernel, turn),
        grid_spec=pltpu.PrefetchScalarGridSpec(
            num_scalar_prefetch=1,
            grid=(count, 2),
            in_specs=[in_spec, pl.BlockSpec(memory_space=pl.ANY)],
            out_specs=[out_spec, out_spec],
        ),
        out_shape=[shape, shape],
        compiler_params=pltpu.CompilerParams(vmem_limit_bytes=24 * 1024 * 1024),
        cost_estimate=pl.CostEstimate(flops=0, bytes_accessed=4 * count * WIDE * 2 * HALF, transcendentals=0),
    )(where, weights, dep)


def join_kernel(own_ref, got_ref, dep_ref, out_ref):
    first = pl.program_id(0) == 0
    for hi in range(2):
        for slot in range(4):
            chunk = jnp.where(first, slot * 2 + hi, hi * 4 + slot)
            out_ref[0, chunk, :, :HALF] = own_ref[0, hi, slot]
            out_ref[0, chunk, :, HALF:] = got_ref[0, hi, slot]


def joined_weights(own, got, dep):
    count = own.shape[0]
    in_spec = pl.BlockSpec((1, 2, 4, COLS, HALF), lambda i: (i, 0, 0, 0, 0))
    out = pl.pallas_call(
        join_kernel,
        grid=(count,),
        in_specs=[in_spec, in_spec, pl.BlockSpec(memory_space=pl.ANY)],
        out_specs=pl.BlockSpec((1, 8, COLS, 2 * HALF), lambda i: (i, 0, 0, 0)),
        out_shape=jax.ShapeDtypeStruct((count, 8, COLS, 2 * HALF), BF),
        compiler_params=pltpu.CompilerParams(vmem_limit_bytes=24 * 1024 * 1024),
        cost_estimate=pl.CostEstimate(flops=0, bytes_accessed=8 * count * WIDE * HALF, transcendentals=0),
    )(own, got, dep)
    return out.reshape(count, WIDE, 2 * HALF)


def pick_kernel(ids_ref, cache_ref, dep_ref, out_ref):
    out_ref[0] = cache_ref[0].T


def picked_after(cache, block_ids, dep):
    return pl.pallas_call(
        pick_kernel,
        grid_spec=pltpu.PrefetchScalarGridSpec(
            num_scalar_prefetch=1,
            grid=(8,),
            in_specs=[
                pl.BlockSpec((1, 128, COLS), lambda i, ids: (ids[i], 0, 0)),
                pl.BlockSpec(memory_space=pl.ANY),
            ],
            out_specs=pl.BlockSpec((1, COLS, 128), lambda i, ids: (i // 4, 0, i % 4)),
        ),
        out_shape=jax.ShapeDtypeStruct((2, COLS, ROWS), BF),
        cost_estimate=pl.CostEstimate(flops=0, bytes_accessed=4 * 2 * COLS * ROWS, transcendentals=0),
    )(block_ids, cache, dep)


def silu_kernel(part_ref, got_ref, live_ref, pre_ref, feat_ref):
    pre = part_ref[...] + got_ref[...].astype(F32)
    pre_ref[...] = pre
    feat_ref[...] = (jax.nn.silu(pre) * live_ref[...]).astype(BF)


def slope_kernel(part_ref, got_ref, live_ref, pre_ref, out_ref):
    grad = part_ref[...] + got_ref[...].astype(F32)
    out_ref[...] = (grad * live_ref[...] * activation_slope(pre_ref[...])).astype(BF)


def with_other_core(kernel, part, got, live, extra, outs):
    tile = 128
    count = 2 * HALF // tile
    own = pl.BlockSpec((tile, 2 * ROWS), lambda i: (i, 0))
    swapped = pl.BlockSpec((tile, 2 * ROWS), lambda i: ((i + count // 2) % count, 0))
    return pl.pallas_call(
        kernel,
        grid=(count,),
        in_specs=[own, swapped, pl.BlockSpec((1, 2 * ROWS), lambda i: (0, 0))] + [own] * len(extra),
        out_specs=[own] * len(outs),
        out_shape=[jax.ShapeDtypeStruct((2 * HALF, 2 * ROWS), kind) for kind in outs],
        compiler_params=pltpu.CompilerParams(vmem_limit_bytes=24 * 1024 * 1024),
        cost_estimate=pl.CostEstimate(
            flops=20 * HALF * ROWS, bytes_accessed=24 * HALF * ROWS, transcendentals=4 * HALF * ROWS
        ),
    )(part, got, live, *extra)


def per_device(cache_in, cache_out, read_list, live_blocks, encoder, enc_bias, decoder):
    t = lax.axis_index("tok")
    l = lax.axis_index("layer")
    x_lo, y = t // 4, t % 4
    x_hi, z, core = l // 8, (l // 2) % 4, l % 2
    is_core0 = core == 0
    block_ids = read_list[0]

    def picked(cache):
        rows = cache.at[block_ids].get(mode="promise_in_bounds")
        return rows.reshape(2, ROWS, COLS).transpose(0, 2, 1)

    def gather_both(one, two, steps=None):
        got1, got2 = after(exchange(one, "x", 0), exchange(two, "z", 0))
        if steps is not None:
            steps.append(got2)
        pair2 = jnp.stack([two, got2])
        more1, more2 = after(exchange(jnp.stack([one, got1]), "x", 1), exchange(pair2, "z", 1))
        near = jnp.where(is_core0, got1, more1[0])
        away = jnp.where(is_core0, more1[0], got1)
        block1 = jnp.stack(
            [jnp.concatenate([one, near], axis=1), jnp.concatenate([more1[1], away], axis=1)]
        )
        block2 = jnp.concatenate([pair2, more2])
        if steps is not None:
            steps.append(more2)
        got1, got2 = after(exchange(block1, "z", 0), exchange(block2, "x", 0))
        if steps is not None:
            steps.append(got2)
        more1 = [exchange(block1, "z", 1), exchange(got1, "z", 1)]
        more2 = [exchange(block2, "x", 1), exchange(got2, "x", 1)]
        near = jnp.where(is_core0, got2, more2[0])
        away = jnp.where(is_core0, more2[0], got2)

        def rows(*parts):
            return tuple(p.reshape(WIDE // 4, 2 * ROWS) for p in parts)

        return (
            rows(block1, got1, *more1),
            (
                jnp.concatenate([block2, near], axis=2).reshape(WIDE // 2, 2 * ROWS),
                jnp.concatenate([more2[1], away], axis=2).reshape(WIDE // 2, 2 * ROWS),
            ),
        )

    own_in = picked(cache_in)
    steps = []
    in0, in1 = gather_both(own_in[0], own_in[1], steps)
    where = jnp.stack([x_lo, x_hi, core, z]).astype(jnp.int32)
    enc_own, enc_give = ordered_weights(encoder, where, steps[0], False)
    dec_own, dec_give = ordered_weights(decoder, where, steps[1], True)
    enc_w = joined_weights(enc_own, to_other_core(enc_give), steps[2])
    dec_w = joined_weights(dec_own, to_other_core(dec_give), steps[2])
    own_out = picked_after(cache_out, block_ids, steps[2])

    live_other = to_mate(live_blocks, 0)
    row_blocks = jnp.arange(ROWS, dtype=jnp.int32) // 128
    own_live = (row_blocks[None, :] < live_blocks[0][:, None]).astype(F32)
    other_live = (row_blocks[None, :] < live_other[0][:, None]).astype(F32)
    live = jnp.concatenate([own_live, other_live], axis=1)[:, None, :]
    own_live = own_live[:, None, :]
    bias_half = lax.dynamic_slice(
        enc_bias, (jnp.int32(0), x_lo * HALF), (2, HALF), allow_negative_indices=False
    )
    bias_mine = jnp.concatenate([bias_half, jnp.zeros_like(bias_half)], axis=1)[:, :, None]

    inputs = (in0, in1)
    mid = WIDE // 2

    def over_width(mat, parts):
        size = WIDE // len(parts)
        total = mm(mat[:size], parts[0], 0, 0)
        for i in range(1, len(parts)):
            total = total + mm(mat[i * size : (i + 1) * size], parts[i], 0, 0)
        return total

    def encode(k):
        total = over_width(enc_w[k], inputs[k]) + bias_mine[k]
        other = to_other_core(total.astype(BF))
        return with_other_core(silu_kernel, total, other, live[k], (), (F32, BF))

    pre_act, feats = zip(*[encode(k) for k in range(2)])

    low = mid // 2
    dec_hi = [dec_w[k].reshape(2, mid, 2 * HALF) for k in (1, 2)]

    def slot_term(k):
        return mm(dec_w[0][k * low : (k + 1) * low], feats[0], 1, 0)

    def quarter(hi, first):
        total = mm(at(dec_hi[0], hi), feats[0][:, first : first + ROWS], 1, 0)
        return total + mm(at(dec_hi[1], hi), feats[1][:, first : first + ROWS], 1, 0)

    got = [
        exchange(slot_term(3).astype(BF), "z", 1),
        exchange(quarter(1, 0).astype(BF), "x", 1),
        exchange(slot_term(2).astype(BF), "z", 1),
        exchange(quarter(1 - core, ROWS).astype(BF), "x", 1),
    ]
    got = after(*got)
    give1 = (slot_term(1) + got[0].astype(F32)).astype(BF)
    give2 = (quarter(core, ROWS) + got[1].astype(F32)).astype(BF)
    block1 = (slot_term(0) + got[2].astype(F32)).reshape(2, COLS, 2 * ROWS)
    block2 = (quarter(0, 0) + got[3].astype(F32)).reshape(4, COLS, ROWS)
    got1, got2 = after(exchange(give1, "z", 0), exchange(give2, "x", 0))
    block1 = block1 + got1.reshape(2, COLS, 2 * ROWS).astype(F32)
    block2 = block2 + got2.reshape(4, COLS, ROWS).astype(F32)
    own0, own1 = block1[0, :, :ROWS], block1[1, :, :ROWS]
    oth0, oth1 = block1[0, :, ROWS:], block1[1, :, ROWS:]
    give1 = jnp.stack([jnp.where(is_core0, oth1, oth0), own1]).astype(BF)
    got1, got2 = after(exchange(give1, "x", 1), exchange(block2[2:].astype(BF), "z", 1))
    give1 = (jnp.where(is_core0, oth0, oth1) + got1[1].astype(F32)).astype(BF)
    give2 = (block2[1] + got2[1].astype(F32)).astype(BF)
    more1, more2 = after(exchange(give1, "x", 0), exchange(give2, "z", 0))
    recon0 = own0 + got1[0].astype(F32) + more1.astype(F32)
    recon1 = block2[0] + got2[0].astype(F32) + more2.astype(F32)

    err_scale = 1.0 / math.sqrt(4096)

    def error(k, recon):
        return ((recon - own_out[k].astype(F32)) * own_live[k] * err_scale).astype(BF)

    err0, err1 = gather_both(error(0, recon0), error(1, recon1))

    def width_grad(halves, other, hi_first):
        term = mm(jnp.concatenate(halves), other, 1, 1).astype(BF)
        if hi_first:
            return term.reshape(2, 4, COLS, 2 * HALF).transpose(1, 0, 2, 3)
        return term.reshape(4, 2, COLS, 2 * HALF)

    m_first = jnp.where(is_core0, 1, 3)
    m_second = jnp.where(is_core0, 3, 1)
    slot_own, slot_first, slot_second, slot_far = [slot_of(z ^ y ^ m, core) for m in (0, m_first, m_second, 2)]

    def sum_over_y(terms, joined=False):
        def chunk(slot):
            return jnp.stack([at(term, slot) for term in terms])

        if joined:
            got, far = exchange(jnp.stack([chunk(slot_second), chunk(slot_far)]), "y", 1)
        else:
            far = exchange(chunk(slot_far), "y", 1)
            got = exchange(chunk(slot_second), "y", 1)
        near = chunk(slot_first).astype(F32) + far.astype(F32)
        return chunk(slot_own).astype(F32) + got.astype(F32) + exchange(near.astype(BF), "y", 0).astype(F32)

    def to_owners(mine):
        def part(lo, first):
            return at(mine, lo ^ x_hi, 1)[:, :, first : first + HALF]

        same = part(x_lo, 0)
        from_core = to_other_core(part(x_lo, HALF).astype(BF)).astype(F32)
        from_mate = to_mate(part(1 - x_lo, 0).astype(BF), 0).astype(F32)
        from_both = to_mate(part(1 - x_lo, HALF).astype(BF), 1).astype(F32)

        def pair(flag, own, other, axis):
            return jnp.where(
                flag, jnp.concatenate([own, other], axis=axis), jnp.concatenate([other, own], axis=axis)
            )

        return pair(is_core0, pair(x_lo == 0, same, from_mate, 2), pair(x_lo == 0, from_core, from_both, 2), 1)

    def backward(k, total):
        other = to_other_core(total.astype(BF))
        return with_other_core(slope_kernel, total, other, live[k], (pre_act[k],), (BF,))[0]

    sums_a = sum_over_y([width_grad(err1, feats[0], True), width_grad(err1, feats[1], True)])
    gpre1 = backward(1, over_width(dec_w[2], err1))
    sums_b = sum_over_y([width_grad(err0, feats[0], False), width_grad(in1, gpre1, True)])
    gpre0 = backward(0, over_width(dec_w[1], err1) + over_width(dec_w[0], err0))
    sums_c = sum_over_y([width_grad(in0, gpre0, False)], True)

    bias_sum = jnp.stack([jnp.sum(g[:HALF].astype(F32), axis=1) for g in (gpre0, gpre1)])
    bias_sum = bias_sum.astype(BF).astype(F32).reshape(2, 4, 64)
    give = jnp.stack([at(bias_sum, y ^ m_second, 1), at(bias_sum, y ^ 2, 1)])
    got = exchange(give, "y", 1)
    near = at(bias_sum, y ^ m_first, 1) + got[1]
    bias_out = at(bias_sum, y, 1) + got[0] + exchange(near, "y", 0)

    done_a = to_owners(sums_a)
    done_b = to_owners(sums_b)
    done_c = to_owners(sums_c)
    dec_out = jnp.stack([done_b[0], done_a[0], done_a[1]]).transpose(0, 2, 1)
    enc_out = jnp.stack([done_c[0], done_b[1]])
    return (enc_out, bias_out[:, None, :], dec_out)


def solution(mesh):
    return jax.shard_map(
        per_device,
        mesh=mesh,
        in_specs=(
            P("tok", None, "layer"),
            P("tok", None, "layer"),
            P("tok", None),
            P("tok", None),
            P(None, None, "layer"),
            P(None, "layer"),
            P(None, "layer", None),
        ),
        out_specs=(P(None, "tok", "layer"), P(None, "layer", "tok"), P(None, "layer", "tok")),
        check_vma=False,
    )
```

```python
import functools
import math

import jax
import jax.numpy as jnp
from jax import lax
from jax.experimental import pallas as pl
from jax.experimental.pallas import tpu as pltpu
from jax.sharding import PartitionSpec as P

AXES = ("tok", "layer")
BF = jnp.bfloat16
F32 = jnp.float32
ROWS = 512
COLS = 144
HALF = 256
WIDE = 8 * COLS
SMALL = 16 * 1024 * 1024


def device_index(x, y, z, c):
    return ((x % 2) * 4 + y) * 16 + (x // 2) * 8 + z * 2 + c


def pairs_of(partner):
    out = []
    for x in range(4):
        for y in range(4):
            for z in range(4):
                for c in range(2):
                    out.append((device_index(x, y, z, c), device_index(*partner(x, y, z, c))))
    return out


def mask(step, c):
    return 1 if (step + c) % 2 == 0 else 3


def exchange(value, axis, step):
    def partner(x, y, z, c):
        m = mask(step, c)
        return {"x": (x ^ m, y, z, c), "y": (x, y ^ m, z, c), "z": (x, y, z ^ m, c)}[axis]

    return lax.ppermute(value, AXES, pairs_of(partner))


def exchange_far(value, axis):
    def partner(x, y, z, c):
        return {"x": (x ^ 2, y, z, c), "z": (x, y, z ^ 2, c)}[axis]

    return lax.ppermute(value, AXES, pairs_of(partner))


def to_other_core(value):
    return lax.ppermute(value, AXES, pairs_of(lambda x, y, z, c: (x, y, z, 1 - c)))


def to_mate(value, flip):
    return lax.ppermute(value, AXES, pairs_of(lambda x, y, z, c: (x ^ 1, y, z, c ^ flip)))


def activation_slope(pre_act):
    sigma = jax.nn.sigmoid(pre_act)
    return sigma + pre_act * sigma * (1.0 - sigma)


def mm(a, b, ca, cb):
    return lax.dot_general(a, b, (((ca,), (cb,)), ((), ())), preferred_element_type=F32)


def at(array, index, dim=0):
    starts = [jnp.int32(0)] * array.ndim
    starts[dim] = index
    sizes = list(array.shape)
    sizes[dim] = 1
    piece = lax.dynamic_slice(array, starts, sizes, allow_negative_indices=False)
    return piece.reshape(array.shape[:dim] + array.shape[dim + 1 :])


def slot_of(apart, core):
    on_core0 = apart ^ (apart >> 1)
    on_core1 = (on_core0 & 1) * 2 + (on_core0 >> 1)
    return jnp.where(core == 0, on_core0, on_core1)


def order_spec(array):
    return pl.BlockSpec((1,) * (array.ndim - 2) + (16, 128), lambda *args: (0,) * array.ndim)


def order_kernel(turn, where_ref, w_ref, dep_ref, own_ref, give_ref):
    block = w_ref[0].T if turn else w_ref[0]
    core = where_ref[2]
    for zz in range(4):
        even = block[2 * zz * COLS : (2 * zz + 1) * COLS]
        odd = block[(2 * zz + 1) * COLS : (2 * zz + 2) * COLS]
        apart = zz ^ where_ref[3]
        own_ref[0, 0, slot_of(apart, core)] = jnp.where(core == 0, even, odd)
        give_ref[0, 0, slot_of(apart, 1 - core)] = jnp.where(core == 0, odd, even)


def ordered_weights(weights, where, dep, turn):
    count = weights.shape[0]
    if turn:
        in_spec = pl.BlockSpec((1, HALF, WIDE), lambda i, h, s: (i, s[0], h))
    else:
        in_spec = pl.BlockSpec((1, WIDE, HALF), lambda i, h, s: (i, h, s[0]))
    out_spec = pl.BlockSpec((1, 1, 4, COLS, HALF), lambda i, h, s: (i, (h + s[1]) % 2, 0, 0, 0))
    shape = jax.ShapeDtypeStruct((count, 2, 4, COLS, HALF), BF)
    return pl.pallas_call(
        functools.partial(order_kernel, turn),
        grid_spec=pltpu.PrefetchScalarGridSpec(
            num_scalar_prefetch=1,
            grid=(count, 2),
            in_specs=[in_spec, order_spec(dep)],
            out_specs=[out_spec, out_spec],
        ),
        out_shape=[shape, shape],
        compiler_params=pltpu.CompilerParams(vmem_limit_bytes=24 * 1024 * 1024),
        cost_estimate=pl.CostEstimate(flops=0, bytes_accessed=4 * count * WIDE * 2 * HALF, transcendentals=0),
    )(where, weights, dep)


def join_kernel(own_ref, got_ref, dep_ref, out_ref):
    first = pl.program_id(0) == 0
    for hi in range(2):
        for slot in range(4):
            chunk = jnp.where(first, slot * 2 + hi, hi * 4 + slot)
            out_ref[0, chunk, :, :HALF] = own_ref[0, hi, slot]
            out_ref[0, chunk, :, HALF:] = got_ref[0, hi, slot]


def joined_weights(own, got, dep):
    count = own.shape[0]
    in_spec = pl.BlockSpec((1, 2, 4, COLS, HALF), lambda i: (i, 0, 0, 0, 0))
    out = pl.pallas_call(
        join_kernel,
        grid=(count,),
        in_specs=[in_spec, in_spec, order_spec(dep)],
        out_specs=pl.BlockSpec((1, 8, COLS, 2 * HALF), lambda i: (i, 0, 0, 0)),
        out_shape=jax.ShapeDtypeStruct((count, 8, COLS, 2 * HALF), BF),
        compiler_params=pltpu.CompilerParams(vmem_limit_bytes=24 * 1024 * 1024),
        cost_estimate=pl.CostEstimate(flops=0, bytes_accessed=8 * count * WIDE * HALF, transcendentals=0),
    )(own, got, dep)
    return out.reshape(count, WIDE, 2 * HALF)


def pass_on(value, dep):
    def kernel(value_ref, dep_ref, out_ref):
        out_ref[...] = value_ref[...]

    parts = value.shape[0]
    whole = pl.BlockSpec((1,) + value.shape[1:], lambda i: (i,) + (0,) * (value.ndim - 1))
    return pl.pallas_call(
        kernel,
        grid=(parts,),
        in_specs=[whole, order_spec(dep)],
        out_specs=whole,
        out_shape=jax.ShapeDtypeStruct(value.shape, value.dtype),
        compiler_params=pltpu.CompilerParams(vmem_limit_bytes=SMALL),
        cost_estimate=pl.CostEstimate(flops=0, bytes_accessed=8 * value.size, transcendentals=0),
    )(value, dep)


def pack_x(core, own, first, second, far, deps):
    def kernel(core_ref, own_ref, first_ref, second_ref, far_ref, *rest):
        out_ref = rest[-1]
        swap = core_ref[0] != 0
        out_ref[0, :, :ROWS] = own_ref[...]
        out_ref[1, :, :ROWS] = far_ref[...]
        out_ref[0, :, ROWS:] = jnp.where(swap, second_ref[...], first_ref[...])
        out_ref[1, :, ROWS:] = jnp.where(swap, first_ref[...], second_ref[...])

    return pl.pallas_call(
        kernel,
        grid=(1,),
        in_specs=[pl.BlockSpec(memory_space=pltpu.SMEM)]
        + [pl.BlockSpec(memory_space=pltpu.VMEM)] * 4
        + [order_spec(dep) for dep in deps],
        out_specs=pl.BlockSpec(memory_space=pltpu.VMEM),
        out_shape=jax.ShapeDtypeStruct((2, COLS, 2 * ROWS), BF),
        compiler_params=pltpu.CompilerParams(vmem_limit_bytes=SMALL),
        cost_estimate=pl.CostEstimate(flops=0, bytes_accessed=16 * COLS * ROWS, transcendentals=0),
    )(core, own, first, second, far, *deps)


def pack_z(pieces, deps):
    def kernel(*refs):
        for k in range(4):
            refs[-1][k] = refs[k][...]

    return pl.pallas_call(
        kernel,
        grid=(1,),
        in_specs=[pl.BlockSpec(memory_space=pltpu.VMEM)] * 4 + [order_spec(dep) for dep in deps],
        out_specs=pl.BlockSpec(memory_space=pltpu.VMEM),
        out_shape=jax.ShapeDtypeStruct((4, COLS, ROWS), BF),
        compiler_params=pltpu.CompilerParams(vmem_limit_bytes=SMALL),
        cost_estimate=pl.CostEstimate(flops=0, bytes_accessed=16 * COLS * ROWS, transcendentals=0),
    )(*pieces, *deps)


def sum_kernel(core_ref, own_ref, oth_ref, got_own_ref, got_oth_ref, two_ref, got_two_ref, *outs):
    own = own_ref[...] + got_own_ref[...].astype(F32)
    oth = oth_ref[...] + got_oth_ref[...].astype(F32)
    two = two_ref[...] + got_two_ref[...].astype(F32)
    swap = core_ref[0] != 0
    keep1_ref, first1_ref, second1_ref, far1_ref, keep2_ref, first2_ref, second2_ref, far2_ref = outs
    keep1_ref[...] = own[0]
    first1_ref[...] = jnp.where(swap, oth[1], oth[0]).astype(BF)
    second1_ref[...] = jnp.where(swap, oth[0], oth[1]).astype(BF)
    far1_ref[...] = own[1].astype(BF)
    keep2_ref[...] = two[0]
    first2_ref[...] = two[1].astype(BF)
    second2_ref[...] = two[2].astype(BF)
    far2_ref[...] = two[3].astype(BF)


def heavy_sum(core, one, got1, two, got2):
    def spec(lead, shift):
        return pl.BlockSpec((lead, COLS, 128), lambda j, c: (0, 0, j + shift))

    kept = jax.ShapeDtypeStruct((COLS, ROWS), F32)
    give = jax.ShapeDtypeStruct((COLS, ROWS), BF)
    out = pl.pallas_call(
        sum_kernel,
        grid_spec=pltpu.PrefetchScalarGridSpec(
            num_scalar_prefetch=1,
            grid=(4,),
            in_specs=[spec(2, 0), spec(2, 4), spec(2, 0), spec(2, 4), spec(4, 0), spec(4, 0)],
            out_specs=[pl.BlockSpec((COLS, 128), lambda j, c: (0, j))] * 8,
        ),
        out_shape=[kept, give, give, give] * 2,
        compiler_params=pltpu.CompilerParams(vmem_limit_bytes=SMALL),
        cost_estimate=pl.CostEstimate(flops=0, bytes_accessed=36 * COLS * ROWS, transcendentals=0),
    )(core, one, one, got1, got1, two, got2)
    return out[:4], out[4:]


def error_kernel(ids_ref, counts_ref, *refs):
    block = pl.program_id(0)
    scale = 1.0 / math.sqrt(4096)
    for k in range(2):
        recon = refs[4 * k][...]
        for got in refs[4 * k + 1 : 4 * k + 4]:
            recon = recon + got[...].astype(F32)
        live = jnp.where(block < counts_ref[k], 1.0, 0.0).astype(F32)
        refs[10 + k][...] = ((recon - refs[8 + k][0].astype(F32)) * live * scale).astype(BF)


def errors(ids, counts, one, two, targets):
    part = pl.BlockSpec((COLS, 128), lambda j, ids, counts: (0, j))
    out = jax.ShapeDtypeStruct((COLS, ROWS), BF)
    return pl.pallas_call(
        error_kernel,
        grid_spec=pltpu.PrefetchScalarGridSpec(
            num_scalar_prefetch=2,
            grid=(4,),
            in_specs=[part] * 8
            + [
                pl.BlockSpec((1, COLS, 128), lambda j, ids, counts: (ids[j], 0, 0)),
                pl.BlockSpec((1, COLS, 128), lambda j, ids, counts: (ids[4 + j], 0, 0)),
            ],
            out_specs=[part] * 2,
        ),
        out_shape=[out, out],
        compiler_params=pltpu.CompilerParams(vmem_limit_bytes=SMALL),
        cost_estimate=pl.CostEstimate(flops=0, bytes_accessed=28 * COLS * ROWS, transcendentals=0),
    )(ids, counts, *one, *two, targets, targets)


def silu_kernel(part_ref, got_ref, live_ref, pre_ref, feat_ref):
    pre = part_ref[...] + got_ref[...].astype(F32)
    pre_ref[...] = pre
    feat_ref[...] = (jax.nn.silu(pre) * live_ref[...]).astype(BF)


def slope_kernel(part_ref, got_ref, live_ref, pre_ref, out_ref):
    grad = part_ref[...] + got_ref[...].astype(F32)
    out_ref[...] = (grad * live_ref[...] * activation_slope(pre_ref[...])).astype(BF)


def with_other_core(kernel, part, got, live, extra, outs):
    tile = 128
    count = 2 * HALF // tile
    own = pl.BlockSpec((tile, 2 * ROWS), lambda i: (i, 0))
    swapped = pl.BlockSpec((tile, 2 * ROWS), lambda i: ((i + count // 2) % count, 0))
    return pl.pallas_call(
        kernel,
        grid=(count,),
        in_specs=[own, swapped, pl.BlockSpec((1, 2 * ROWS), lambda i: (0, 0))] + [own] * len(extra),
        out_specs=[own] * len(outs),
        out_shape=[jax.ShapeDtypeStruct((2 * HALF, 2 * ROWS), kind) for kind in outs],
        compiler_params=pltpu.CompilerParams(vmem_limit_bytes=24 * 1024 * 1024),
        cost_estimate=pl.CostEstimate(
            flops=20 * HALF * ROWS, bytes_accessed=24 * HALF * ROWS, transcendentals=4 * HALF * ROWS
        ),
    )(part, got, live, *extra)


def term_views(terms):
    return [term.reshape((2, 4, COLS, 2 * HALF) if hi_first else (4, 2, COLS, 2 * HALF)) for term, hi_first in terms]


def term_specs(terms, place):
    def one(hi_first):
        def index(*args):
            hi, slot = place(*args)
            return (hi, slot, 0, 0) if hi_first else (slot, hi, 0, 0)

        return pl.BlockSpec((1, 1, COLS, 2 * HALF), index)

    return [one(hi_first) for _, hi_first in terms]


def y_give(scalars, terms, deps=()):
    count = len(terms)

    def kernel(s_ref, *refs):
        for k in range(count):
            refs[-1][0, k, 0] = refs[k][0, 0]

    return pl.pallas_call(
        kernel,
        grid_spec=pltpu.PrefetchScalarGridSpec(
            num_scalar_prefetch=1,
            grid=(2, 2),
            in_specs=term_specs(terms, lambda i, hi, s: (hi, s[2 + i]))
            + [order_spec(dep) for dep in deps],
            out_specs=pl.BlockSpec((1, count, 1, COLS, 2 * HALF), lambda i, hi, s: (i, 0, hi, 0, 0)),
        ),
        out_shape=jax.ShapeDtypeStruct((2, count, 2, COLS, 2 * HALF), BF),
        compiler_params=pltpu.CompilerParams(vmem_limit_bytes=SMALL),
        cost_estimate=pl.CostEstimate(flops=0, bytes_accessed=32 * count * COLS * HALF, transcendentals=0),
    )(scalars, *term_views(terms), *deps)


def y_near(scalars, terms, got, deps=()):
    count = len(terms)

    def kernel(s_ref, *refs):
        for k in range(count):
            first = refs[k][0, 0].astype(F32) + refs[2 * count][1, k, 0].astype(F32)
            refs[-2][k, 0] = first.astype(BF)
            refs[-1][k, 0] = refs[count + k][0, 0].astype(F32) + refs[2 * count][0, k, 0].astype(F32)

    out = pl.BlockSpec((count, 1, COLS, 2 * HALF), lambda hi, s: (0, hi, 0, 0))
    shape = (count, 2, COLS, 2 * HALF)
    return pl.pallas_call(
        kernel,
        grid_spec=pltpu.PrefetchScalarGridSpec(
            num_scalar_prefetch=1,
            grid=(2,),
            in_specs=term_specs(terms, lambda hi, s: (hi, s[1]))
            + term_specs(terms, lambda hi, s: (hi, s[0]))
            + [pl.BlockSpec((2, count, 1, COLS, 2 * HALF), lambda hi, s: (0, 0, hi, 0, 0))]
            + [order_spec(dep) for dep in deps],
            out_specs=[out, out],
        ),
        out_shape=[jax.ShapeDtypeStruct(shape, BF), jax.ShapeDtypeStruct(shape, F32)],
        compiler_params=pltpu.CompilerParams(vmem_limit_bytes=SMALL),
        cost_estimate=pl.CostEstimate(flops=0, bytes_accessed=48 * count * COLS * HALF, transcendentals=0),
    )(scalars, *term_views(terms), *term_views(terms), got, *deps)


def y_quarters(scalars, groups, deps=()):
    sizes = [keep.shape[0] for keep, _ in groups]
    count = sum(sizes)

    def kernel(s_ref, *refs):
        same_ref, core_ref, mate_ref, both_ref = refs[-4:]
        totals = []
        for n, size in enumerate(sizes):
            for k in range(size):
                totals.append(refs[2 * n][k, 0] + refs[2 * n + 1][k, 0].astype(F32))

        @pl.when(pl.program_id(0) == 0)
        def _():
            for k, total in enumerate(totals):
                same_ref[k] = total[:, :HALF]
                core_ref[k] = total[:, HALF:].astype(BF)

        @pl.when(pl.program_id(0) == 1)
        def _():
            for k, total in enumerate(totals):
                mate_ref[k] = total[:, :HALF].astype(BF)
                both_ref[k] = total[:, HALF:].astype(BF)

    def hi_of(i, s):
        return (i + s[4]) % 2

    in_specs, operands = [], []
    for size, group in zip(sizes, groups):
        in_specs += [pl.BlockSpec((size, 1, COLS, 2 * HALF), lambda i, s: (0, hi_of(i, s), 0, 0))] * 2
        operands += group
    out = pl.BlockSpec((count, COLS, HALF), lambda i, s: (0, 0, 0))
    sent = jax.ShapeDtypeStruct((count, COLS, HALF), BF)
    same, core, mate, both = pl.pallas_call(
        kernel,
        grid_spec=pltpu.PrefetchScalarGridSpec(
            num_scalar_prefetch=1,
            grid=(2,),
            in_specs=in_specs + [order_spec(dep) for dep in deps],
            out_specs=[out] * 4,
        ),
        out_shape=[jax.ShapeDtypeStruct((count, COLS, HALF), F32), sent, sent, sent],
        compiler_params=pltpu.CompilerParams(vmem_limit_bytes=SMALL),
        cost_estimate=pl.CostEstimate(flops=0, bytes_accessed=32 * count * COLS * HALF, transcendentals=0),
    )(scalars, *operands, *deps)
    return same, to_other_core(core), to_mate(mate, 0), to_mate(both, 1)


def write_out(place, groups, picks):
    def kernel(place_ref, *refs):
        core, x_lo = place_ref[0], place_ref[1]
        for n, (group, k) in enumerate(picks):
            same, from_core, from_mate, from_both = [ref[k].astype(F32) for ref in refs[4 * group : 4 * group + 4]]

            def side(own, mate):
                return jnp.where(
                    x_lo == 0, jnp.concatenate([own, mate], axis=1), jnp.concatenate([mate, own], axis=1)
                )

            refs[-1][n, pl.ds(pl.multiple_of(core * COLS, 8), COLS), :] = side(same, from_mate)
            refs[-1][n, pl.ds(pl.multiple_of((1 - core) * COLS, 8), COLS), :] = side(from_core, from_both)

    flat = [array for group in groups for array in group]
    return pl.pallas_call(
        kernel,
        in_specs=[pl.BlockSpec(memory_space=pltpu.SMEM)] + [pl.BlockSpec(memory_space=pltpu.VMEM)] * len(flat),
        out_specs=pl.BlockSpec(memory_space=pltpu.VMEM),
        out_shape=jax.ShapeDtypeStruct((len(picks), 2 * COLS, 2 * HALF), F32),
        compiler_params=pltpu.CompilerParams(vmem_limit_bytes=SMALL),
        cost_estimate=pl.CostEstimate(flops=0, bytes_accessed=28 * len(picks) * COLS * HALF, transcendentals=0),
    )(place, *flat)


def per_device(cache_in, cache_out, read_list, live_blocks, encoder, enc_bias, decoder):
    t = lax.axis_index("tok")
    l = lax.axis_index("layer")
    x_lo, y = t // 4, t % 4
    x_hi, z, core = l // 8, (l // 2) % 4, l % 2
    is_core0 = core == 0
    block_ids = read_list[0]

    def picked(cache):
        rows = cache.at[block_ids].get(mode="promise_in_bounds")
        return rows.reshape(2, ROWS, COLS).transpose(0, 2, 1)

    core_ref = core.reshape(1)

    def gather_both(one, two, steps=None):
        got2 = exchange(two, "z", 0), exchange(two, "z", 1), exchange_far(two, "z")
        got1 = exchange(one, "x", 0), exchange(one, "x", 1), exchange_far(one, "x")
        block2 = pack_z((two,) + got2, got1)
        block1 = pack_x(core_ref, one, *got1, got2)
        got1, got2 = exchange(block1, "z", 0), exchange(block2, "x", 0)
        if steps is not None:
            steps.append(got2)
        more1 = [exchange(block1, "z", 1), exchange(got1, "z", 1)]
        more2 = [exchange(block2, "x", 1), exchange(got2, "x", 1)]
        near = jnp.where(is_core0, got2, more2[0])
        away = jnp.where(is_core0, more2[0], got2)

        def rows(*parts):
            return tuple(p.reshape(WIDE // 4, 2 * ROWS) for p in parts)

        return (
            rows(block1, got1, *more1),
            (
                jnp.concatenate([block2, near], axis=2).reshape(WIDE // 2, 2 * ROWS),
                jnp.concatenate([more2[1], away], axis=2).reshape(WIDE // 2, 2 * ROWS),
            ),
        )

    own_in = picked(cache_in)
    steps = []
    in0, in1 = gather_both(own_in[0], own_in[1], steps)
    where = jnp.stack([x_lo, x_hi, core, z]).astype(jnp.int32)
    enc_own, enc_give = ordered_weights(encoder, where, steps[0], False)
    dec_own, dec_give = ordered_weights(decoder, where, steps[0], True)
    enc_w = joined_weights(enc_own, to_other_core(enc_give), steps[0])
    dec_w = joined_weights(dec_own, to_other_core(dec_give), steps[0])
    live_other = to_mate(live_blocks, 0)
    row_blocks = jnp.arange(ROWS, dtype=jnp.int32) // 128
    own_live = (row_blocks[None, :] < live_blocks[0][:, None]).astype(F32)
    other_live = (row_blocks[None, :] < live_other[0][:, None]).astype(F32)
    live = jnp.concatenate([own_live, other_live], axis=1)[:, None, :]
    bias_half = lax.dynamic_slice(
        enc_bias, (jnp.int32(0), x_lo * HALF), (2, HALF), allow_negative_indices=False
    )
    bias_mine = jnp.concatenate([bias_half, jnp.zeros_like(bias_half)], axis=1)[:, :, None]

    inputs = (in0, in1)
    mid = WIDE // 2

    def over_width(mat, parts):
        size = WIDE // len(parts)
        total = mm(mat[:size], parts[0], 0, 0)
        for i in range(1, len(parts)):
            total = total + mm(mat[i * size : (i + 1) * size], parts[i], 0, 0)
        return total

    def encode(k):
        total = over_width(enc_w[k], inputs[k]) + bias_mine[k]
        other = to_other_core(total.astype(BF))
        return with_other_core(silu_kernel, total, other, live[k], (), (F32, BF))

    pre_act, feats = zip(*[encode(k) for k in range(2)])

    low = mid // 2
    dec_hi = [dec_w[k].reshape(2, mid, 2 * HALF) for k in (1, 2)]

    def slot_term(k):
        return mm(dec_w[0][k * low : (k + 1) * low], feats[0], 1, 0)

    def quarter(hi, first):
        total = mm(at(dec_hi[0], hi), feats[0][:, first : first + ROWS], 1, 0)
        return total + mm(at(dec_hi[1], hi), feats[1][:, first : first + ROWS], 1, 0)

    got = [
        exchange(slot_term(3).astype(BF), "z", 1),
        exchange(quarter(1, 0).astype(BF), "x", 1),
        exchange(slot_term(2).astype(BF), "z", 1),
        exchange(quarter(1 - core, ROWS).astype(BF), "x", 1),
    ]
    give1 = (slot_term(1) + got[0].astype(F32)).astype(BF)
    give2 = (quarter(core, ROWS) + got[1].astype(F32)).astype(BF)
    block1 = (slot_term(0) + got[2].astype(F32)).reshape(2, COLS, 2 * ROWS)
    block2 = (quarter(0, 0) + got[3].astype(F32)).reshape(4, COLS, ROWS)
    got1, got2 = exchange(give1, "z", 0), exchange(give2, "x", 0)
    one, two = heavy_sum(
        core_ref, block1, got1.reshape(2, COLS, 2 * ROWS), block2, got2.reshape(4, COLS, ROWS)
    )
    got2 = exchange(two[1], "z", 0), exchange(two[2], "z", 1), exchange_far(two[3], "z")
    got1 = exchange(one[1], "x", 0), exchange(one[2], "x", 1), exchange_far(one[3], "x")
    own_err = errors(
        block_ids, live_blocks[0], (one[0],) + got1, (two[0],) + got2, cache_out.transpose(0, 2, 1)
    )

    err0, err1 = gather_both(*own_err)

    def width_grad(parts, other, hi_first):
        return mm(jnp.concatenate(parts), other, 1, 1).astype(BF), hi_first

    m_first = jnp.where(is_core0, 1, 3)
    m_second = jnp.where(is_core0, 3, 1)
    scalars = jnp.stack([slot_of(z ^ y ^ m, core) for m in (0, m_first, m_second, 2)] + [x_lo ^ x_hi])
    scalars = scalars.astype(jnp.int32)
    place = jnp.stack([core, x_lo]).astype(jnp.int32)

    def backward(k, total):
        other = to_other_core(total.astype(BF))
        return with_other_core(slope_kernel, total, other, live[k], (pre_act[k],), (BF,))[0]

    terms_a = [width_grad(err1, feats[0], True), width_grad(err1, feats[1], True)]
    give_a = y_give(scalars, terms_a)
    got_a = exchange(give_a, "y", 1)
    back_w = pass_on(dec_w, give_a)
    gpre1 = backward(1, over_width(back_w[2], err1))
    terms_b = [width_grad(err0, feats[0], False), width_grad(in1, gpre1, True)]
    got_b = exchange(y_give(scalars, terms_b), "y", 1)
    gpre0 = backward(0, over_width(back_w[1], err1) + over_width(back_w[0], err0))
    terms_c = [width_grad(in0, gpre0, False)]
    give_c = y_give(scalars, terms_c)
    got_c = exchange(give_c, "y", 1)
    near_a, keep_a = y_near(scalars, terms_a, got_a, (give_c,))
    last_a = exchange(near_a, "y", 0)
    near_b, keep_b = y_near(scalars, terms_b, got_b, (near_a,))
    last_b = exchange(near_b, "y", 0)
    near_c, keep_c = y_near(scalars, terms_c, got_c, (near_b,))
    last_c = exchange(near_c, "y", 0)
    done_a = y_quarters(scalars, [(keep_a, last_a)], (near_c,))
    done_bc = y_quarters(scalars, [(keep_b, last_b), (keep_c, last_c)], done_a[1:])

    bias_sum = jnp.stack([jnp.sum(g[:HALF].astype(F32), axis=1) for g in (gpre0, gpre1)])
    bias_sum = bias_sum.astype(BF).astype(F32).reshape(2, 4, 64)
    give = pass_on(jnp.stack([at(bias_sum, y ^ m_second, 1), at(bias_sum, y ^ 2, 1)]), near_c)
    got = exchange(give, "y", 1)
    near = at(bias_sum, y ^ m_first, 1) + got[1]
    bias_out = at(bias_sum, y, 1) + got[0] + exchange(near, "y", 0)

    dec_out = write_out(place, (done_a, done_bc), ((1, 0), (0, 0), (0, 1))).transpose(0, 2, 1)
    enc_out = write_out(place, (done_bc,), ((0, 2), (0, 1)))
    return (enc_out, bias_out[:, None, :], dec_out)


def solution(mesh):
    return jax.shard_map(
        per_device,
        mesh=mesh,
        in_specs=(
            P("tok", None, "layer"),
            P("tok", None, "layer"),
            P("tok", None),
            P("tok", None),
            P(None, None, "layer"),
            P(None, "layer"),
            P(None, "layer", None),
        ),
        out_specs=(P(None, "tok", "layer"), P(None, "layer", "tok"), P(None, "layer", "tok")),
        check_vma=False,
    )
```

```python
import functools
import math

import jax
import jax.numpy as jnp
from jax import lax
from jax.experimental import pallas as pl
from jax.experimental.pallas import tpu as pltpu
from jax.sharding import PartitionSpec as P

AXES = ("tok", "layer")
BF = jnp.bfloat16
F32 = jnp.float32
ROWS = 512
COLS = 144
HALF = 256
WIDE = 8 * COLS
SMALL = 8 * 1024 * 1024


def device_index(x, y, z, c):
    return ((x % 2) * 4 + y) * 16 + (x // 2) * 8 + z * 2 + c


def pairs_of(partner):
    out = []
    for x in range(4):
        for y in range(4):
            for z in range(4):
                for c in range(2):
                    out.append((device_index(x, y, z, c), device_index(*partner(x, y, z, c))))
    return out


def mask(step, c):
    return 1 if (step + c) % 2 == 0 else 3


def exchange(value, axis, step):
    def partner(x, y, z, c):
        m = mask(step, c)
        return {"x": (x ^ m, y, z, c), "y": (x, y ^ m, z, c), "z": (x, y, z ^ m, c)}[axis]

    return lax.ppermute(value, AXES, pairs_of(partner))


def exchange_far(value, axis):
    def partner(x, y, z, c):
        return {"x": (x ^ 2, y, z, c), "z": (x, y, z ^ 2, c)}[axis]

    return lax.ppermute(value, AXES, pairs_of(partner))


def to_other_core(value):
    return lax.ppermute(value, AXES, pairs_of(lambda x, y, z, c: (x, y, z, 1 - c)))


def to_mate(value, flip):
    return lax.ppermute(value, AXES, pairs_of(lambda x, y, z, c: (x ^ 1, y, z, c ^ flip)))


def activation_slope(pre_act):
    sigma = jax.nn.sigmoid(pre_act)
    return sigma + pre_act * sigma * (1.0 - sigma)


def mm(a, b, ca, cb):
    return lax.dot_general(a, b, (((ca,), (cb,)), ((), ())), preferred_element_type=F32)


def at(array, index, dim=0):
    starts = [jnp.int32(0)] * array.ndim
    starts[dim] = index
    sizes = list(array.shape)
    sizes[dim] = 1
    piece = lax.dynamic_slice(array, starts, sizes, allow_negative_indices=False)
    return piece.reshape(array.shape[:dim] + array.shape[dim + 1 :])


def slot_of(apart, core):
    on_core0 = apart ^ (apart >> 1)
    on_core1 = (on_core0 & 1) * 2 + (on_core0 >> 1)
    return jnp.where(core == 0, on_core0, on_core1)


def order_spec(array):
    tile = (min(16, array.shape[-2]), min(128, array.shape[-1]))
    return pl.BlockSpec((1,) * (array.ndim - 2) + tile, lambda *args: (0,) * array.ndim)


def order_kernel(turn, where_ref, w_ref, dep_ref, own_ref, give_ref):
    block = w_ref[0].T if turn else w_ref[0]
    core = where_ref[2]
    for zz in range(4):
        even = block[2 * zz * COLS : (2 * zz + 1) * COLS]
        odd = block[(2 * zz + 1) * COLS : (2 * zz + 2) * COLS]
        apart = zz ^ where_ref[3]
        own_ref[0, 0, slot_of(apart, core)] = jnp.where(core == 0, even, odd)
        give_ref[0, 0, slot_of(apart, 1 - core)] = jnp.where(core == 0, odd, even)


def ordered_weights(weights, where, dep, turn):
    count = weights.shape[0]
    if turn:
        in_spec = pl.BlockSpec((1, HALF, WIDE), lambda i, h, s: (i, s[0], h))
    else:
        in_spec = pl.BlockSpec((1, WIDE, HALF), lambda i, h, s: (i, h, s[0]))
    out_spec = pl.BlockSpec((1, 1, 4, COLS, HALF), lambda i, h, s: (i, (h + s[1]) % 2, 0, 0, 0))
    shape = jax.ShapeDtypeStruct((count, 2, 4, COLS, HALF), BF)
    return pl.pallas_call(
        functools.partial(order_kernel, turn),
        grid_spec=pltpu.PrefetchScalarGridSpec(
            num_scalar_prefetch=1,
            grid=(count, 2),
            in_specs=[in_spec, order_spec(dep)],
            out_specs=[out_spec, out_spec],
        ),
        out_shape=[shape, shape],
        compiler_params=pltpu.CompilerParams(vmem_limit_bytes=SMALL),
        cost_estimate=pl.CostEstimate(flops=0, bytes_accessed=4 * count * WIDE * 2 * HALF, transcendentals=0),
    )(where, weights, dep)


def join_kernel(own_ref, got_ref, dep_ref, out_ref):
    first = pl.program_id(0) == 0
    for hi in range(2):
        for slot in range(4):
            chunk = jnp.where(first, slot * 2 + hi, hi * 4 + slot)
            out_ref[0, chunk, :, :HALF] = own_ref[0, hi, slot]
            out_ref[0, chunk, :, HALF:] = got_ref[0, hi, slot]


def joined_weights(own, got, dep):
    count = own.shape[0]
    in_spec = pl.BlockSpec((1, 2, 4, COLS, HALF), lambda i: (i, 0, 0, 0, 0))
    out = pl.pallas_call(
        join_kernel,
        grid=(count,),
        in_specs=[in_spec, in_spec, order_spec(dep)],
        out_specs=pl.BlockSpec((1, 8, COLS, 2 * HALF), lambda i: (i, 0, 0, 0)),
        out_shape=jax.ShapeDtypeStruct((count, 8, COLS, 2 * HALF), BF),
        compiler_params=pltpu.CompilerParams(vmem_limit_bytes=12 * 1024 * 1024),
        cost_estimate=pl.CostEstimate(flops=0, bytes_accessed=8 * count * WIDE * HALF, transcendentals=0),
    )(own, got, dep)
    return out.reshape(count, WIDE, 2 * HALF)


def pass_on(value, first, count, *deps):
    def kernel(value_ref, *refs):
        refs[-1][...] = value_ref[...]

    block = (1,) + value.shape[1:]
    return pl.pallas_call(
        kernel,
        grid=(count,),
        in_specs=[pl.BlockSpec(block, lambda i: (first + i,) + (0,) * (value.ndim - 1))]
        + [order_spec(dep) for dep in deps],
        out_specs=pl.BlockSpec(block, lambda i: (i,) + (0,) * (value.ndim - 1)),
        out_shape=jax.ShapeDtypeStruct((count,) + value.shape[1:], value.dtype),
        compiler_params=pltpu.CompilerParams(vmem_limit_bytes=SMALL),
        cost_estimate=pl.CostEstimate(flops=0, bytes_accessed=4 * count * WIDE * HALF, transcendentals=0),
    )(value, *deps)


def pack_x(core, own, first, second, far, deps):
    def kernel(core_ref, own_ref, first_ref, second_ref, far_ref, *rest):
        out_ref = rest[-1]
        swap = core_ref[0] != 0
        out_ref[0, :, :ROWS] = own_ref[...]
        out_ref[1, :, :ROWS] = far_ref[...]
        out_ref[0, :, ROWS:] = jnp.where(swap, second_ref[...], first_ref[...])
        out_ref[1, :, ROWS:] = jnp.where(swap, first_ref[...], second_ref[...])

    return pl.pallas_call(
        kernel,
        grid=(1,),
        in_specs=[pl.BlockSpec(memory_space=pltpu.SMEM)]
        + [pl.BlockSpec(memory_space=pltpu.VMEM)] * 4
        + [order_spec(dep) for dep in deps],
        out_specs=pl.BlockSpec(memory_space=pltpu.VMEM),
        out_shape=jax.ShapeDtypeStruct((2, COLS, 2 * ROWS), BF),
        compiler_params=pltpu.CompilerParams(vmem_limit_bytes=SMALL),
        cost_estimate=pl.CostEstimate(flops=0, bytes_accessed=16 * COLS * ROWS, transcendentals=0),
    )(core, own, first, second, far, *deps)


def pack_z(pieces, deps):
    def kernel(*refs):
        for k in range(4):
            refs[-1][k] = refs[k][...]

    return pl.pallas_call(
        kernel,
        grid=(1,),
        in_specs=[pl.BlockSpec(memory_space=pltpu.VMEM)] * 4 + [order_spec(dep) for dep in deps],
        out_specs=pl.BlockSpec(memory_space=pltpu.VMEM),
        out_shape=jax.ShapeDtypeStruct((4, COLS, ROWS), BF),
        compiler_params=pltpu.CompilerParams(vmem_limit_bytes=SMALL),
        cost_estimate=pl.CostEstimate(flops=0, bytes_accessed=16 * COLS * ROWS, transcendentals=0),
    )(*pieces, *deps)


def sum_kernel(core_ref, own_ref, oth_ref, got_own_ref, got_oth_ref, two_ref, got_two_ref, *outs):
    own = own_ref[...] + got_own_ref[...].astype(F32)
    oth = oth_ref[...] + got_oth_ref[...].astype(F32)
    two = two_ref[...] + got_two_ref[...].astype(F32)
    swap = core_ref[0] != 0
    keep1_ref, first1_ref, second1_ref, far1_ref, keep2_ref, first2_ref, second2_ref, far2_ref = outs
    keep1_ref[...] = own[0]
    first1_ref[...] = jnp.where(swap, oth[1], oth[0]).astype(BF)
    second1_ref[...] = jnp.where(swap, oth[0], oth[1]).astype(BF)
    far1_ref[...] = own[1].astype(BF)
    keep2_ref[...] = two[0]
    first2_ref[...] = two[1].astype(BF)
    second2_ref[...] = two[2].astype(BF)
    far2_ref[...] = two[3].astype(BF)


def heavy_sum(core, one, got1, two, got2):
    def spec(lead, shift):
        return pl.BlockSpec((lead, COLS, 128), lambda j, c: (0, 0, j + shift))

    kept = jax.ShapeDtypeStruct((COLS, ROWS), F32)
    give = jax.ShapeDtypeStruct((COLS, ROWS), BF)
    out = pl.pallas_call(
        sum_kernel,
        grid_spec=pltpu.PrefetchScalarGridSpec(
            num_scalar_prefetch=1,
            grid=(4,),
            in_specs=[spec(2, 0), spec(2, 4), spec(2, 0), spec(2, 4), spec(4, 0), spec(4, 0)],
            out_specs=[pl.BlockSpec((COLS, 128), lambda j, c: (0, j))] * 8,
        ),
        out_shape=[kept, give, give, give] * 2,
        compiler_params=pltpu.CompilerParams(vmem_limit_bytes=SMALL),
        cost_estimate=pl.CostEstimate(flops=0, bytes_accessed=36 * COLS * ROWS, transcendentals=0),
    )(core, one, one, got1, got1, two, got2)
    return out[:4], out[4:]


def error_kernel(ids_ref, counts_ref, *refs):
    block = pl.program_id(0)
    scale = 1.0 / math.sqrt(4096)
    for k in range(2):
        recon = refs[4 * k][...]
        for got in refs[4 * k + 1 : 4 * k + 4]:
            recon = recon + got[...].astype(F32)
        live = jnp.where(block < counts_ref[k], 1.0, 0.0).astype(F32)
        refs[10 + k][...] = ((recon - refs[8 + k][0].astype(F32)) * live * scale).astype(BF)


def errors(ids, counts, one, two, targets):
    part = pl.BlockSpec((COLS, 128), lambda j, ids, counts: (0, j))
    out = jax.ShapeDtypeStruct((COLS, ROWS), BF)
    return pl.pallas_call(
        error_kernel,
        grid_spec=pltpu.PrefetchScalarGridSpec(
            num_scalar_prefetch=2,
            grid=(4,),
            in_specs=[part] * 8
            + [
                pl.BlockSpec((1, COLS, 128), lambda j, ids, counts: (ids[j], 0, 0)),
                pl.BlockSpec((1, COLS, 128), lambda j, ids, counts: (ids[4 + j], 0, 0)),
            ],
            out_specs=[part] * 2,
        ),
        out_shape=[out, out],
        compiler_params=pltpu.CompilerParams(vmem_limit_bytes=SMALL),
        cost_estimate=pl.CostEstimate(flops=0, bytes_accessed=28 * COLS * ROWS, transcendentals=0),
    )(ids, counts, *one, *two, targets, targets)


def silu_kernel(part_ref, got_ref, live_ref, pre_ref, feat_ref):
    pre = part_ref[...] + got_ref[...].astype(F32)
    pre_ref[...] = pre
    feat_ref[...] = (jax.nn.silu(pre) * live_ref[...]).astype(BF)


def slope_kernel(part_ref, got_ref, live_ref, pre_ref, out_ref):
    grad = part_ref[...] + got_ref[...].astype(F32)
    out_ref[...] = (grad * live_ref[...] * activation_slope(pre_ref[...])).astype(BF)


def with_other_core(kernel, part, got, live, extra, outs):
    tile = 128
    count = 2 * HALF // tile
    own = pl.BlockSpec((tile, 2 * ROWS), lambda i: (i, 0))
    swapped = pl.BlockSpec((tile, 2 * ROWS), lambda i: ((i + count // 2) % count, 0))
    return pl.pallas_call(
        kernel,
        grid=(count,),
        in_specs=[own, swapped, pl.BlockSpec((1, 2 * ROWS), lambda i: (0, 0))] + [own] * len(extra),
        out_specs=[own] * len(outs),
        out_shape=[jax.ShapeDtypeStruct((2 * HALF, 2 * ROWS), kind) for kind in outs],
        compiler_params=pltpu.CompilerParams(vmem_limit_bytes=SMALL),
        cost_estimate=pl.CostEstimate(
            flops=20 * HALF * ROWS, bytes_accessed=24 * HALF * ROWS, transcendentals=4 * HALF * ROWS
        ),
    )(part, got, live, *extra)


def term_views(terms):
    return [term.reshape((2, 4, COLS, 2 * HALF) if hi_first else (4, 2, COLS, 2 * HALF)) for term, hi_first in terms]


def term_specs(terms, place):
    def one(hi_first):
        def index(*args):
            hi, slot = place(*args)
            return (hi, slot, 0, 0) if hi_first else (slot, hi, 0, 0)

        return pl.BlockSpec((1, 1, COLS, 2 * HALF), index)

    return [one(hi_first) for _, hi_first in terms]


def y_give(scalars, terms, deps=()):
    count = len(terms)

    def kernel(s_ref, *refs):
        for k in range(count):
            refs[-1][0, k, 0] = refs[k][0, 0]

    return pl.pallas_call(
        kernel,
        grid_spec=pltpu.PrefetchScalarGridSpec(
            num_scalar_prefetch=1,
            grid=(2, 2),
            in_specs=term_specs(terms, lambda i, hi, s: (hi, s[2 + i]))
            + [order_spec(dep) for dep in deps],
            out_specs=pl.BlockSpec((1, count, 1, COLS, 2 * HALF), lambda i, hi, s: (i, 0, hi, 0, 0)),
        ),
        out_shape=jax.ShapeDtypeStruct((2, count, 2, COLS, 2 * HALF), BF),
        compiler_params=pltpu.CompilerParams(vmem_limit_bytes=SMALL),
        cost_estimate=pl.CostEstimate(flops=0, bytes_accessed=32 * count * COLS * HALF, transcendentals=0),
    )(scalars, *term_views(terms), *deps)


def y_near(scalars, terms, got, deps=()):
    count = len(terms)

    def kernel(s_ref, *refs):
        for k in range(count):
            first = refs[k][0, 0].astype(F32) + refs[2 * count][1, k, 0].astype(F32)
            refs[-2][k, 0] = first.astype(BF)
            keep = refs[count + k][0, 0].astype(F32) + refs[2 * count][0, k, 0].astype(F32)
            refs[-1][k, 0] = keep.astype(BF)

    out = pl.BlockSpec((count, 1, COLS, 2 * HALF), lambda hi, s: (0, hi, 0, 0))
    shape = (count, 2, COLS, 2 * HALF)
    return pl.pallas_call(
        kernel,
        grid_spec=pltpu.PrefetchScalarGridSpec(
            num_scalar_prefetch=1,
            grid=(2,),
            in_specs=term_specs(terms, lambda hi, s: (hi, s[1]))
            + term_specs(terms, lambda hi, s: (hi, s[0]))
            + [pl.BlockSpec((2, count, 1, COLS, 2 * HALF), lambda hi, s: (0, 0, hi, 0, 0))]
            + [order_spec(dep) for dep in deps],
            out_specs=[out, out],
        ),
        out_shape=[jax.ShapeDtypeStruct(shape, BF)] * 2,
        compiler_params=pltpu.CompilerParams(vmem_limit_bytes=SMALL),
        cost_estimate=pl.CostEstimate(flops=0, bytes_accessed=48 * count * COLS * HALF, transcendentals=0),
    )(scalars, *term_views(terms), *term_views(terms), got, *deps)


def y_quarters(scalars, groups, deps=()):
    sizes = [keep.shape[0] for keep, _ in groups]
    count = sum(sizes)

    def kernel(s_ref, *refs):
        same_ref, core_ref, mate_ref, both_ref = refs[-4:]
        totals = []
        for n, size in enumerate(sizes):
            for k in range(size):
                totals.append(refs[2 * n][k, 0].astype(F32) + refs[2 * n + 1][k, 0].astype(F32))

        @pl.when(pl.program_id(0) == 0)
        def _():
            for k, total in enumerate(totals):
                same_ref[k] = total[:, :HALF]
                core_ref[k] = total[:, HALF:].astype(BF)

        @pl.when(pl.program_id(0) == 1)
        def _():
            for k, total in enumerate(totals):
                mate_ref[k] = total[:, :HALF].astype(BF)
                both_ref[k] = total[:, HALF:].astype(BF)

    def hi_of(i, s):
        return (i + s[4]) % 2

    in_specs, operands = [], []
    for size, group in zip(sizes, groups):
        in_specs += [pl.BlockSpec((size, 1, COLS, 2 * HALF), lambda i, s: (0, hi_of(i, s), 0, 0))] * 2
        operands += group
    out = pl.BlockSpec((count, COLS, HALF), lambda i, s: (0, 0, 0))
    sent = jax.ShapeDtypeStruct((count, COLS, HALF), BF)
    same, core, mate, both = pl.pallas_call(
        kernel,
        grid_spec=pltpu.PrefetchScalarGridSpec(
            num_scalar_prefetch=1,
            grid=(2,),
            in_specs=in_specs + [order_spec(dep) for dep in deps],
            out_specs=[out] * 4,
        ),
        out_shape=[jax.ShapeDtypeStruct((count, COLS, HALF), F32), sent, sent, sent],
        compiler_params=pltpu.CompilerParams(vmem_limit_bytes=SMALL),
        cost_estimate=pl.CostEstimate(flops=0, bytes_accessed=32 * count * COLS * HALF, transcendentals=0),
    )(scalars, *operands, *deps)
    return same, to_other_core(core), to_mate(mate, 0), to_mate(both, 1)


def write_out(place, groups, picks):
    def kernel(place_ref, *refs):
        core, x_lo = place_ref[0], place_ref[1]
        for n, (group, k) in enumerate(picks):
            same, from_core, from_mate, from_both = [ref[k].astype(F32) for ref in refs[4 * group : 4 * group + 4]]

            def side(own, mate):
                return jnp.where(
                    x_lo == 0, jnp.concatenate([own, mate], axis=1), jnp.concatenate([mate, own], axis=1)
                )

            refs[-1][n, pl.ds(pl.multiple_of(core * COLS, 8), COLS), :] = side(same, from_mate)
            refs[-1][n, pl.ds(pl.multiple_of((1 - core) * COLS, 8), COLS), :] = side(from_core, from_both)

    flat = [array for group in groups for array in group]
    return pl.pallas_call(
        kernel,
        in_specs=[pl.BlockSpec(memory_space=pltpu.SMEM)] + [pl.BlockSpec(memory_space=pltpu.VMEM)] * len(flat),
        out_specs=pl.BlockSpec(memory_space=pltpu.VMEM),
        out_shape=jax.ShapeDtypeStruct((len(picks), 2 * COLS, 2 * HALF), F32),
        compiler_params=pltpu.CompilerParams(vmem_limit_bytes=SMALL),
        cost_estimate=pl.CostEstimate(flops=0, bytes_accessed=28 * len(picks) * COLS * HALF, transcendentals=0),
    )(place, *flat)


def per_device(cache_in, cache_out, read_list, live_blocks, encoder, enc_bias, decoder):
    t = lax.axis_index("tok")
    l = lax.axis_index("layer")
    x_lo, y = t // 4, t % 4
    x_hi, z, core = l // 8, (l // 2) % 4, l % 2
    is_core0 = core == 0
    block_ids = read_list[0]

    def picked(cache):
        rows = cache.at[block_ids].get(mode="promise_in_bounds")
        return rows.reshape(2, ROWS, COLS).transpose(0, 2, 1)

    core_ref = core.reshape(1)

    def gather_both(one, two, steps=None):
        got2 = exchange(two, "z", 0), exchange(two, "z", 1), exchange_far(two, "z")
        got1 = exchange(one, "x", 0), exchange(one, "x", 1), exchange_far(one, "x")
        arrived = got2[0]
        block2 = pack_z((two,) + got2, got1)
        block1 = pack_x(core_ref, one, *got1, got2)
        got1, got2 = exchange(block1, "z", 0), exchange(block2, "x", 0)
        if steps is not None:
            steps.extend([arrived, block1, got2])
        more1 = [exchange(block1, "z", 1), exchange(got1, "z", 1)]
        more2 = [exchange(block2, "x", 1), exchange(got2, "x", 1)]
        near = jnp.where(is_core0, got2, more2[0])
        away = jnp.where(is_core0, more2[0], got2)

        def rows(*parts):
            return tuple(p.reshape(WIDE // 4, 2 * ROWS) for p in parts)

        return (
            rows(block1, got1, *more1),
            (
                jnp.concatenate([block2, near], axis=2).reshape(WIDE // 2, 2 * ROWS),
                jnp.concatenate([more2[1], away], axis=2).reshape(WIDE // 2, 2 * ROWS),
            ),
        )

    own_in = picked(cache_in)
    steps = []
    in0, in1 = gather_both(own_in[0], own_in[1], steps)
    where = jnp.stack([x_lo, x_hi, core, z]).astype(jnp.int32)
    enc_own, enc_give = ordered_weights(encoder, where, steps[0], False)
    dec_own, dec_give = ordered_weights(decoder, where, steps[1], True)
    enc_w = joined_weights(enc_own, to_other_core(enc_give), steps[2])
    dec_w = joined_weights(dec_own, to_other_core(dec_give), steps[2])
    live_other = to_mate(live_blocks, 0)
    row_blocks = jnp.arange(ROWS, dtype=jnp.int32) // 128
    own_live = (row_blocks[None, :] < live_blocks[0][:, None]).astype(F32)
    other_live = (row_blocks[None, :] < live_other[0][:, None]).astype(F32)
    live = jnp.concatenate([own_live, other_live], axis=1)[:, None, :]
    bias_half = lax.dynamic_slice(
        enc_bias, (jnp.int32(0), x_lo * HALF), (2, HALF), allow_negative_indices=False
    )
    bias_mine = jnp.concatenate([bias_half, jnp.zeros_like(bias_half)], axis=1)[:, :, None]

    inputs = (in0, in1)
    mid = WIDE // 2

    def over_width(mat, parts):
        size = WIDE // len(parts)
        total = mm(mat[:size], parts[0], 0, 0)
        for i in range(1, len(parts)):
            total = total + mm(mat[i * size : (i + 1) * size], parts[i], 0, 0)
        return total

    def encode(k):
        total = over_width(enc_w[k], inputs[k]) + bias_mine[k]
        other = to_other_core(total.astype(BF))
        return with_other_core(silu_kernel, total, other, live[k], (), (F32, BF))

    pre_act, feats = zip(*[encode(k) for k in range(2)])

    low = mid // 2
    dec_hi = [dec_w[k].reshape(2, mid, 2 * HALF) for k in (1, 2)]

    def slot_term(k):
        return mm(dec_w[0][k * low : (k + 1) * low], feats[0], 1, 0)

    def quarter(hi, first):
        total = mm(at(dec_hi[0], hi), feats[0][:, first : first + ROWS], 1, 0)
        return total + mm(at(dec_hi[1], hi), feats[1][:, first : first + ROWS], 1, 0)

    got = [
        exchange(slot_term(3).astype(BF), "z", 1),
        exchange(quarter(1, 0).astype(BF), "x", 1),
        exchange(slot_term(2).astype(BF), "z", 1),
        exchange(quarter(1 - core, ROWS).astype(BF), "x", 1),
    ]
    give1 = (slot_term(1) + got[0].astype(F32)).astype(BF)
    give2 = (quarter(core, ROWS) + got[1].astype(F32)).astype(BF)
    block1 = (slot_term(0) + got[2].astype(F32)).reshape(2, COLS, 2 * ROWS)
    block2 = (quarter(0, 0) + got[3].astype(F32)).reshape(4, COLS, ROWS)
    got1, got2 = exchange(give1, "z", 0), exchange(give2, "x", 0)
    one, two = heavy_sum(
        core_ref, block1, got1.reshape(2, COLS, 2 * ROWS), block2, got2.reshape(4, COLS, ROWS)
    )
    got2 = exchange(two[1], "z", 0), exchange(two[2], "z", 1), exchange_far(two[3], "z")
    got1 = exchange(one[1], "x", 0), exchange(one[2], "x", 1), exchange_far(one[3], "x")
    own_err = errors(
        block_ids, live_blocks[0], (one[0],) + got1, (two[0],) + got2, cache_out.transpose(0, 2, 1)
    )

    err0, err1 = gather_both(*own_err)

    err0, err1 = jnp.concatenate(err0), jnp.concatenate(err1)

    def width_grad(whole, other, hi_first):
        return mm(whole, other, 1, 1).astype(BF), hi_first

    m_first = jnp.where(is_core0, 1, 3)
    m_second = jnp.where(is_core0, 3, 1)
    scalars = jnp.stack([slot_of(z ^ y ^ m, core) for m in (0, m_first, m_second, 2)] + [x_lo ^ x_hi])
    scalars = scalars.astype(jnp.int32)
    place = jnp.stack([core, x_lo]).astype(jnp.int32)

    def backward(k, total):
        other = to_other_core(total.astype(BF))
        return with_other_core(slope_kernel, total, other, live[k], (pre_act[k],), (BF,))[0]

    terms_a = [width_grad(err1, feats[0], True), width_grad(err1, feats[1], True)]
    give_a = y_give(scalars, terms_a)
    got_a = exchange(give_a, "y", 1)
    gpre1 = backward(1, mm(pass_on(dec_w, 2, 1, give_a)[0], err1, 0, 0))
    terms_b = [width_grad(err0, feats[0], False), width_grad(jnp.concatenate(in1), gpre1, True)]
    give_b = y_give(scalars, terms_b)
    got_b = exchange(give_b, "y", 1)
    near_a, keep_a = y_near(scalars, terms_a, got_a, (give_b,))
    last_a = exchange(near_a, "y", 0)
    back_w = pass_on(dec_w, 0, 2, near_a)
    gpre0 = backward(0, mm(back_w[1], err1, 0, 0) + mm(back_w[0], err0, 0, 0))
    terms_c = [width_grad(jnp.concatenate(in0), gpre0, False)]
    give_c = y_give(scalars, terms_c)
    got_c = exchange(give_c, "y", 1)

    bias_sum = jnp.stack([jnp.sum(g[:HALF].astype(F32), axis=1) for g in (gpre0, gpre1)])
    bias_sum = bias_sum.astype(BF).astype(F32).reshape(2, 4, 64)
    got = exchange(jnp.stack([at(bias_sum, y ^ m_second, 1), at(bias_sum, y ^ 2, 1)]), "y", 1)
    near = at(bias_sum, y ^ m_first, 1) + got[1]
    last = exchange(near, "y", 0)
    bias_out = at(bias_sum, y, 1) + got[0] + last

    near_b, keep_b = y_near(scalars, terms_b, got_b, (give_c, got))
    last_b = exchange(near_b, "y", 0)
    done_a = y_quarters(scalars, [(keep_a, last_a)], (near_b,))
    near_c, keep_c = y_near(scalars, terms_c, got_c, (done_a[0], last))
    last_c = exchange(near_c, "y", 0)
    done_b = y_quarters(scalars, [(keep_b, last_b)], (near_c,) + done_a[1:])
    done_c = y_quarters(scalars, [(keep_c, last_c)], done_b[1:])
    dec_out = write_out(place, (done_a, done_b), ((1, 0), (0, 0), (0, 1))).transpose(0, 2, 1)
    enc_out = write_out(place, (done_b, done_c), ((1, 0), (0, 1)))
    return (enc_out, bias_out[:, None, :], dec_out)


def solution(mesh):
    return jax.shard_map(
        per_device,
        mesh=mesh,
        in_specs=(
            P("tok", None, "layer"),
            P("tok", None, "layer"),
            P("tok", None),
            P("tok", None),
            P(None, None, "layer"),
            P(None, "layer"),
            P(None, "layer", None),
        ),
        out_specs=(P(None, "tok", "layer"), P(None, "layer", "tok"), P(None, "layer", "tok")),
        check_vma=False,
    )
```

```python
import functools
import math

import jax
import jax.numpy as jnp
from jax import lax
from jax.experimental import pallas as pl
from jax.experimental.pallas import tpu as pltpu
from jax.sharding import PartitionSpec as P

AXES = ("tok", "layer")
BF = jnp.bfloat16
F32 = jnp.float32
ROWS = 512
COLS = 144
HALF = 256
WIDE = 8 * COLS
SMALL = 8 * 1024 * 1024
NO_COST = pl.CostEstimate(flops=0, bytes_accessed=0, transcendentals=0)


def device_index(x, y, z, c):
    return ((x % 2) * 4 + y) * 16 + (x // 2) * 8 + z * 2 + c


def pairs_of(partner):
    out = []
    for x in range(4):
        for y in range(4):
            for z in range(4):
                for c in range(2):
                    out.append((device_index(x, y, z, c), device_index(*partner(x, y, z, c))))
    return out


def mask(step, c):
    return 1 if (step + c) % 2 == 0 else 3


def exchange(value, axis, step):
    def partner(x, y, z, c):
        m = mask(step, c)
        return {"x": (x ^ m, y, z, c), "y": (x, y ^ m, z, c), "z": (x, y, z ^ m, c)}[axis]

    return lax.ppermute(value, AXES, pairs_of(partner))


def exchange_far(value, axis):
    def partner(x, y, z, c):
        return {"x": (x ^ 2, y, z, c), "z": (x, y, z ^ 2, c)}[axis]

    return lax.ppermute(value, AXES, pairs_of(partner))


def to_other_core(value):
    return lax.ppermute(value, AXES, pairs_of(lambda x, y, z, c: (x, y, z, 1 - c)))


def to_mate(value, flip):
    return lax.ppermute(value, AXES, pairs_of(lambda x, y, z, c: (x ^ 1, y, z, c ^ flip)))


def activation_slope(pre_act):
    sigma = jax.nn.sigmoid(pre_act)
    return sigma + pre_act * sigma * (1.0 - sigma)


def mm(a, b, ca, cb):
    return lax.dot_general(a, b, (((ca,), (cb,)), ((), ())), preferred_element_type=F32)


def at(array, index, dim=0):
    starts = [jnp.int32(0)] * array.ndim
    starts[dim] = index
    sizes = list(array.shape)
    sizes[dim] = 1
    piece = lax.dynamic_slice(array, starts, sizes, allow_negative_indices=False)
    return piece.reshape(array.shape[:dim] + array.shape[dim + 1 :])


def slot_of(apart, core):
    on_core0 = apart ^ (apart >> 1)
    on_core1 = (on_core0 & 1) * 2 + (on_core0 >> 1)
    return jnp.where(core == 0, on_core0, on_core1)


def order_spec(array):
    tile = (min(16, array.shape[-2]), min(128, array.shape[-1]))
    return pl.BlockSpec((1,) * (array.ndim - 2) + tile, lambda *args: (0,) * array.ndim)


def order_kernel(turn, where_ref, w_ref, dep_ref, own_ref, give_ref):
    block = w_ref[0].T if turn else w_ref[0]
    core = where_ref[2]
    for zz in range(4):
        even = block[2 * zz * COLS : (2 * zz + 1) * COLS]
        odd = block[(2 * zz + 1) * COLS : (2 * zz + 2) * COLS]
        apart = zz ^ where_ref[3]
        own_ref[0, 0, slot_of(apart, core)] = jnp.where(core == 0, even, odd)
        give_ref[0, 0, slot_of(apart, 1 - core)] = jnp.where(core == 0, odd, even)


def ordered_weights(weights, where, dep, turn):
    count = weights.shape[0]
    if turn:
        in_spec = pl.BlockSpec((1, HALF, WIDE), lambda i, h, s: (i, s[0], h))
    else:
        in_spec = pl.BlockSpec((1, WIDE, HALF), lambda i, h, s: (i, h, s[0]))
    out_spec = pl.BlockSpec((1, 1, 4, COLS, HALF), lambda i, h, s: (i, (h + s[1]) % 2, 0, 0, 0))
    shape = jax.ShapeDtypeStruct((count, 2, 4, COLS, HALF), BF)
    return pl.pallas_call(
        functools.partial(order_kernel, turn),
        grid_spec=pltpu.PrefetchScalarGridSpec(
            num_scalar_prefetch=1,
            grid=(count, 2),
            in_specs=[in_spec, order_spec(dep)],
            out_specs=[out_spec, out_spec],
        ),
        out_shape=[shape, shape],
        compiler_params=pltpu.CompilerParams(vmem_limit_bytes=SMALL),
        cost_estimate=NO_COST,
    )(where, weights, dep)


def join_kernel(own_ref, got_ref, dep_ref, out_ref):
    first = pl.program_id(0) == 0
    for hi in range(2):
        for slot in range(4):
            chunk = jnp.where(first, slot * 2 + hi, hi * 4 + slot)
            out_ref[0, chunk, :, :HALF] = own_ref[0, hi, slot]
            out_ref[0, chunk, :, HALF:] = got_ref[0, hi, slot]


def joined_weights(own, got, dep):
    count = own.shape[0]
    in_spec = pl.BlockSpec((1, 2, 4, COLS, HALF), lambda i: (i, 0, 0, 0, 0))
    out = pl.pallas_call(
        join_kernel,
        grid=(count,),
        in_specs=[in_spec, in_spec, order_spec(dep)],
        out_specs=pl.BlockSpec((1, 8, COLS, 2 * HALF), lambda i: (i, 0, 0, 0)),
        out_shape=jax.ShapeDtypeStruct((count, 8, COLS, 2 * HALF), BF),
        compiler_params=pltpu.CompilerParams(vmem_limit_bytes=12 * 1024 * 1024),
        cost_estimate=NO_COST,
    )(own, got, dep)
    return out.reshape(count, WIDE, 2 * HALF)


def pass_on(value, first, count, *deps):
    def kernel(value_ref, *refs):
        refs[-1][...] = value_ref[...]

    block = (1,) + value.shape[1:]
    return pl.pallas_call(
        kernel,
        grid=(count,),
        in_specs=[pl.BlockSpec(block, lambda i: (first + i,) + (0,) * (value.ndim - 1))]
        + [order_spec(dep) for dep in deps],
        out_specs=pl.BlockSpec(block, lambda i: (i,) + (0,) * (value.ndim - 1)),
        out_shape=jax.ShapeDtypeStruct((count,) + value.shape[1:], value.dtype),
        compiler_params=pltpu.CompilerParams(vmem_limit_bytes=SMALL),
        cost_estimate=NO_COST,
    )(value, *deps)


def pack_x(core, own, first, second, far, deps):
    def kernel(core_ref, own_ref, first_ref, second_ref, far_ref, *rest):
        out_ref = rest[-1]
        swap = core_ref[0] != 0
        out_ref[0, :, :ROWS] = own_ref[...]
        out_ref[1, :, :ROWS] = far_ref[...]
        out_ref[0, :, ROWS:] = jnp.where(swap, second_ref[...], first_ref[...])
        out_ref[1, :, ROWS:] = jnp.where(swap, first_ref[...], second_ref[...])

    return pl.pallas_call(
        kernel,
        grid=(1,),
        in_specs=[pl.BlockSpec(memory_space=pltpu.SMEM)]
        + [pl.BlockSpec(memory_space=pltpu.VMEM)] * 4
        + [order_spec(dep) for dep in deps],
        out_specs=pl.BlockSpec(memory_space=pltpu.VMEM),
        out_shape=jax.ShapeDtypeStruct((2, COLS, 2 * ROWS), BF),
        compiler_params=pltpu.CompilerParams(vmem_limit_bytes=SMALL),
        cost_estimate=NO_COST,
    )(core, own, first, second, far, *deps)


def pack_z(pieces, deps):
    def kernel(*refs):
        for k in range(4):
            refs[-1][k] = refs[k][...]

    return pl.pallas_call(
        kernel,
        grid=(1,),
        in_specs=[pl.BlockSpec(memory_space=pltpu.VMEM)] * 4 + [order_spec(dep) for dep in deps],
        out_specs=pl.BlockSpec(memory_space=pltpu.VMEM),
        out_shape=jax.ShapeDtypeStruct((4, COLS, ROWS), BF),
        compiler_params=pltpu.CompilerParams(vmem_limit_bytes=SMALL),
        cost_estimate=NO_COST,
    )(*pieces, *deps)


def sum_kernel(core_ref, own_ref, oth_ref, got_own_ref, got_oth_ref, two_ref, got_two_ref, *outs):
    own = own_ref[...] + got_own_ref[...].astype(F32)
    oth = oth_ref[...] + got_oth_ref[...].astype(F32)
    two = two_ref[...] + got_two_ref[...].astype(F32)
    swap = core_ref[0] != 0
    keep1_ref, first1_ref, second1_ref, far1_ref, keep2_ref, first2_ref, second2_ref, far2_ref = outs
    keep1_ref[...] = own[0]
    first1_ref[...] = jnp.where(swap, oth[1], oth[0]).astype(BF)
    second1_ref[...] = jnp.where(swap, oth[0], oth[1]).astype(BF)
    far1_ref[...] = own[1].astype(BF)
    keep2_ref[...] = two[0]
    first2_ref[...] = two[1].astype(BF)
    second2_ref[...] = two[2].astype(BF)
    far2_ref[...] = two[3].astype(BF)


def heavy_sum(core, one, got1, two, got2):
    def spec(lead, shift):
        return pl.BlockSpec((lead, COLS, 128), lambda j, c: (0, 0, j + shift))

    kept = jax.ShapeDtypeStruct((COLS, ROWS), F32)
    give = jax.ShapeDtypeStruct((COLS, ROWS), BF)
    out = pl.pallas_call(
        sum_kernel,
        grid_spec=pltpu.PrefetchScalarGridSpec(
            num_scalar_prefetch=1,
            grid=(4,),
            in_specs=[spec(2, 0), spec(2, 4), spec(2, 0), spec(2, 4), spec(4, 0), spec(4, 0)],
            out_specs=[pl.BlockSpec((COLS, 128), lambda j, c: (0, j))] * 8,
        ),
        out_shape=[kept, give, give, give] * 2,
        compiler_params=pltpu.CompilerParams(vmem_limit_bytes=SMALL),
        cost_estimate=NO_COST,
    )(core, one, one, got1, got1, two, got2)
    return out[:4], out[4:]


def error_kernel(ids_ref, counts_ref, *refs):
    block = pl.program_id(0)
    scale = 1.0 / math.sqrt(4096)
    for k in range(2):
        recon = refs[4 * k][...]
        for got in refs[4 * k + 1 : 4 * k + 4]:
            recon = recon + got[...].astype(F32)
        live = jnp.where(block < counts_ref[k], 1.0, 0.0).astype(F32)
        refs[10 + k][...] = ((recon - refs[8 + k][0].astype(F32)) * live * scale).astype(BF)


def errors(ids, counts, one, two, targets):
    part = pl.BlockSpec((COLS, 128), lambda j, ids, counts: (0, j))
    out = jax.ShapeDtypeStruct((COLS, ROWS), BF)
    return pl.pallas_call(
        error_kernel,
        grid_spec=pltpu.PrefetchScalarGridSpec(
            num_scalar_prefetch=2,
            grid=(4,),
            in_specs=[part] * 8
            + [
                pl.BlockSpec((1, COLS, 128), lambda j, ids, counts: (ids[j], 0, 0)),
                pl.BlockSpec((1, COLS, 128), lambda j, ids, counts: (ids[4 + j], 0, 0)),
            ],
            out_specs=[part] * 2,
        ),
        out_shape=[out, out],
        compiler_params=pltpu.CompilerParams(vmem_limit_bytes=SMALL),
        cost_estimate=NO_COST,
    )(ids, counts, *one, *two, targets, targets)


def silu_kernel(part_ref, got_ref, live_ref, pre_ref, feat_ref):
    pre = part_ref[...] + got_ref[...].astype(F32)
    pre_ref[...] = pre
    feat_ref[...] = (jax.nn.silu(pre) * live_ref[...]).astype(BF)


def slope_kernel(part_ref, got_ref, live_ref, pre_ref, out_ref):
    grad = part_ref[...] + got_ref[...].astype(F32)
    out_ref[...] = (grad * live_ref[...] * activation_slope(pre_ref[...])).astype(BF)


def with_other_core(kernel, part, got, live, extra, outs):
    tile = 128
    count = 2 * HALF // tile
    own = pl.BlockSpec((tile, 2 * ROWS), lambda i: (i, 0))
    swapped = pl.BlockSpec((tile, 2 * ROWS), lambda i: ((i + count // 2) % count, 0))
    return pl.pallas_call(
        kernel,
        grid=(count,),
        in_specs=[own, swapped, pl.BlockSpec((1, 2 * ROWS), lambda i: (0, 0))] + [own] * len(extra),
        out_specs=[own] * len(outs),
        out_shape=[jax.ShapeDtypeStruct((2 * HALF, 2 * ROWS), kind) for kind in outs],
        compiler_params=pltpu.CompilerParams(vmem_limit_bytes=SMALL),
        cost_estimate=NO_COST,
    )(part, got, live, *extra)


def term_views(terms):
    return [term.reshape((2, 4, COLS, 2 * HALF) if hi_first else (4, 2, COLS, 2 * HALF)) for term, hi_first in terms]


def term_specs(terms, place):
    def one(hi_first):
        def index(*args):
            hi, slot = place(*args)
            return (hi, slot, 0, 0) if hi_first else (slot, hi, 0, 0)

        return pl.BlockSpec((1, 1, COLS, 2 * HALF), index)

    return [one(hi_first) for _, hi_first in terms]


def y_give(scalars, terms, deps=()):
    count = len(terms)

    def kernel(s_ref, *refs):
        for k in range(count):
            refs[-1][0, k, 0] = refs[k][0, 0]

    return pl.pallas_call(
        kernel,
        grid_spec=pltpu.PrefetchScalarGridSpec(
            num_scalar_prefetch=1,
            grid=(2, 2),
            in_specs=term_specs(terms, lambda i, hi, s: (hi, s[2 + i]))
            + [order_spec(dep) for dep in deps],
            out_specs=pl.BlockSpec((1, count, 1, COLS, 2 * HALF), lambda i, hi, s: (i, 0, hi, 0, 0)),
        ),
        out_shape=jax.ShapeDtypeStruct((2, count, 2, COLS, 2 * HALF), BF),
        compiler_params=pltpu.CompilerParams(vmem_limit_bytes=SMALL),
        cost_estimate=NO_COST,
    )(scalars, *term_views(terms), *deps)


def y_near(scalars, terms, got, deps=()):
    count = len(terms)

    def kernel(s_ref, *refs):
        for k in range(count):
            first = refs[k][0, 0].astype(F32) + refs[2 * count][1, k, 0].astype(F32)
            refs[-2][k, 0] = first.astype(BF)
            keep = refs[count + k][0, 0].astype(F32) + refs[2 * count][0, k, 0].astype(F32)
            refs[-1][k, 0] = keep.astype(BF)

    out = pl.BlockSpec((count, 1, COLS, 2 * HALF), lambda hi, s: (0, hi, 0, 0))
    shape = (count, 2, COLS, 2 * HALF)
    return pl.pallas_call(
        kernel,
        grid_spec=pltpu.PrefetchScalarGridSpec(
            num_scalar_prefetch=1,
            grid=(2,),
            in_specs=term_specs(terms, lambda hi, s: (hi, s[1]))
            + term_specs(terms, lambda hi, s: (hi, s[0]))
            + [pl.BlockSpec((2, count, 1, COLS, 2 * HALF), lambda hi, s: (0, 0, hi, 0, 0))]
            + [order_spec(dep) for dep in deps],
            out_specs=[out, out],
        ),
        out_shape=[jax.ShapeDtypeStruct(shape, BF)] * 2,
        compiler_params=pltpu.CompilerParams(vmem_limit_bytes=SMALL),
        cost_estimate=NO_COST,
    )(scalars, *term_views(terms), *term_views(terms), got, *deps)


def y_quarters(scalars, groups, deps=()):
    sizes = [keep.shape[0] for keep, _ in groups]
    count = sum(sizes)

    def kernel(s_ref, *refs):
        same_ref, core_ref, mate_ref, both_ref = refs[-4:]
        totals = []
        for n, size in enumerate(sizes):
            for k in range(size):
                totals.append(refs[2 * n][k, 0].astype(F32) + refs[2 * n + 1][k, 0].astype(F32))

        @pl.when(pl.program_id(0) == 0)
        def _():
            for k, total in enumerate(totals):
                same_ref[k] = total[:, :HALF]
                core_ref[k] = total[:, HALF:].astype(BF)

        @pl.when(pl.program_id(0) == 1)
        def _():
            for k, total in enumerate(totals):
                mate_ref[k] = total[:, :HALF].astype(BF)
                both_ref[k] = total[:, HALF:].astype(BF)

    def hi_of(i, s):
        return (i + s[4]) % 2

    in_specs, operands = [], []
    for size, group in zip(sizes, groups):
        in_specs += [pl.BlockSpec((size, 1, COLS, 2 * HALF), lambda i, s: (0, hi_of(i, s), 0, 0))] * 2
        operands += group
    out = pl.BlockSpec((count, COLS, HALF), lambda i, s: (0, 0, 0))
    sent = jax.ShapeDtypeStruct((count, COLS, HALF), BF)
    same, core, mate, both = pl.pallas_call(
        kernel,
        grid_spec=pltpu.PrefetchScalarGridSpec(
            num_scalar_prefetch=1,
            grid=(2,),
            in_specs=in_specs + [order_spec(dep) for dep in deps],
            out_specs=[out] * 4,
        ),
        out_shape=[jax.ShapeDtypeStruct((count, COLS, HALF), F32), sent, sent, sent],
        compiler_params=pltpu.CompilerParams(vmem_limit_bytes=SMALL),
        cost_estimate=NO_COST,
    )(scalars, *operands, *deps)
    return same, to_other_core(core), to_mate(mate, 0), to_mate(both, 1)


def write_out(place, groups, picks):
    def kernel(place_ref, *refs):
        core, x_lo = place_ref[0], place_ref[1]
        for n, (group, k) in enumerate(picks):
            same, from_core, from_mate, from_both = [ref[k].astype(F32) for ref in refs[4 * group : 4 * group + 4]]

            def side(own, mate):
                return jnp.where(
                    x_lo == 0, jnp.concatenate([own, mate], axis=1), jnp.concatenate([mate, own], axis=1)
                )

            refs[-1][n, pl.ds(pl.multiple_of(core * COLS, 8), COLS), :] = side(same, from_mate)
            refs[-1][n, pl.ds(pl.multiple_of((1 - core) * COLS, 8), COLS), :] = side(from_core, from_both)

    flat = [array for group in groups for array in group]
    return pl.pallas_call(
        kernel,
        in_specs=[pl.BlockSpec(memory_space=pltpu.SMEM)] + [pl.BlockSpec(memory_space=pltpu.VMEM)] * len(flat),
        out_specs=pl.BlockSpec(memory_space=pltpu.VMEM),
        out_shape=jax.ShapeDtypeStruct((len(picks), 2 * COLS, 2 * HALF), F32),
        compiler_params=pltpu.CompilerParams(vmem_limit_bytes=SMALL),
        cost_estimate=pl.CostEstimate(flops=0, bytes_accessed=28 * len(picks) * COLS * HALF, transcendentals=0),
    )(place, *flat)


def per_device(cache_in, cache_out, read_list, live_blocks, encoder, enc_bias, decoder):
    t = lax.axis_index("tok")
    l = lax.axis_index("layer")
    x_lo, y = t // 4, t % 4
    x_hi, z, core = l // 8, (l // 2) % 4, l % 2
    is_core0 = core == 0
    block_ids = read_list[0]

    def picked(cache):
        rows = cache.at[block_ids].get(mode="promise_in_bounds")
        return rows.reshape(2, ROWS, COLS).transpose(0, 2, 1)

    core_ref = core.reshape(1)

    def gather_both(one, two, steps=None):
        got2 = exchange(two, "z", 0), exchange(two, "z", 1), exchange_far(two, "z")
        got1 = exchange(one, "x", 0), exchange(one, "x", 1), exchange_far(one, "x")
        arrived = got2[0]
        block2 = pack_z((two,) + got2, got1)
        block1 = pack_x(core_ref, one, *got1, got2)
        got1, got2 = exchange(block1, "z", 0), exchange(block2, "x", 0)
        if steps is not None:
            steps.extend([arrived, block1, got2])
        more1 = [exchange(block1, "z", 1), exchange(got1, "z", 1)]
        more2 = [exchange(block2, "x", 1), exchange(got2, "x", 1)]
        near = jnp.where(is_core0, got2, more2[0])
        away = jnp.where(is_core0, more2[0], got2)

        def rows(*parts):
            return tuple(p.reshape(WIDE // 4, 2 * ROWS) for p in parts)

        return (
            rows(block1, got1, *more1),
            (
                jnp.concatenate([block2, near], axis=2).reshape(WIDE // 2, 2 * ROWS),
                jnp.concatenate([more2[1], away], axis=2).reshape(WIDE // 2, 2 * ROWS),
            ),
        )

    own_in = picked(cache_in)
    steps = []
    in0, in1 = gather_both(own_in[0], own_in[1], steps)
    where = jnp.stack([x_lo, x_hi, core, z]).astype(jnp.int32)
    enc_own, enc_give = ordered_weights(encoder, where, steps[0], False)
    dec_own, dec_give = ordered_weights(decoder, where, steps[1], True)
    enc_w = joined_weights(enc_own, to_other_core(enc_give), steps[2])
    dec_w = joined_weights(dec_own, to_other_core(dec_give), steps[2])
    live_other = to_mate(live_blocks, 0)
    row_blocks = jnp.arange(ROWS, dtype=jnp.int32) // 128
    own_live = (row_blocks[None, :] < live_blocks[0][:, None]).astype(F32)
    other_live = (row_blocks[None, :] < live_other[0][:, None]).astype(F32)
    live = jnp.concatenate([own_live, other_live], axis=1)[:, None, :]
    bias_half = lax.dynamic_slice(
        enc_bias, (jnp.int32(0), x_lo * HALF), (2, HALF), allow_negative_indices=False
    )
    bias_mine = jnp.concatenate([bias_half, jnp.zeros_like(bias_half)], axis=1)[:, :, None]

    inputs = (in0, in1)
    mid = WIDE // 2

    def over_width(mat, parts):
        size = WIDE // len(parts)
        total = mm(mat[:size], parts[0], 0, 0)
        for i in range(1, len(parts)):
            total = total + mm(mat[i * size : (i + 1) * size], parts[i], 0, 0)
        return total

    def encode(k):
        total = over_width(enc_w[k], inputs[k]) + bias_mine[k]
        other = to_other_core(total.astype(BF))
        return with_other_core(silu_kernel, total, other, live[k], (), (F32, BF))

    pre_act, feats = zip(*[encode(k) for k in range(2)])

    low = mid // 2
    dec_hi = [dec_w[k].reshape(2, mid, 2 * HALF) for k in (1, 2)]

    def slot_term(k):
        return mm(dec_w[0][k * low : (k + 1) * low], feats[0], 1, 0)

    def quarter(hi, first):
        total = mm(at(dec_hi[0], hi), feats[0][:, first : first + ROWS], 1, 0)
        return total + mm(at(dec_hi[1], hi), feats[1][:, first : first + ROWS], 1, 0)

    got = [
        exchange(slot_term(3).astype(BF), "z", 1),
        exchange(quarter(1, 0).astype(BF), "x", 1),
        exchange(slot_term(2).astype(BF), "z", 1),
        exchange(quarter(1 - core, ROWS).astype(BF), "x", 1),
    ]
    give1 = (slot_term(1) + got[0].astype(F32)).astype(BF)
    give2 = (quarter(core, ROWS) + got[1].astype(F32)).astype(BF)
    block1 = (slot_term(0) + got[2].astype(F32)).reshape(2, COLS, 2 * ROWS)
    block2 = (quarter(0, 0) + got[3].astype(F32)).reshape(4, COLS, ROWS)
    got1, got2 = exchange(give1, "z", 0), exchange(give2, "x", 0)
    one, two = heavy_sum(
        core_ref, block1, got1.reshape(2, COLS, 2 * ROWS), block2, got2.reshape(4, COLS, ROWS)
    )
    got2 = exchange(two[1], "z", 0), exchange(two[2], "z", 1), exchange_far(two[3], "z")
    got1 = exchange(one[1], "x", 0), exchange(one[2], "x", 1), exchange_far(one[3], "x")
    own_err = errors(
        block_ids, live_blocks[0], (one[0],) + got1, (two[0],) + got2, cache_out.transpose(0, 2, 1)
    )

    err0, err1 = gather_both(*own_err)

    err0, err1 = jnp.concatenate(err0), jnp.concatenate(err1)

    def width_grad(whole, other, hi_first):
        return mm(whole, other, 1, 1).astype(BF), hi_first

    m_first = jnp.where(is_core0, 1, 3)
    m_second = jnp.where(is_core0, 3, 1)
    scalars = jnp.stack([slot_of(z ^ y ^ m, core) for m in (0, m_first, m_second, 2)] + [x_lo ^ x_hi])
    scalars = scalars.astype(jnp.int32)
    place = jnp.stack([core, x_lo]).astype(jnp.int32)

    def backward(k, total):
        other = to_other_core(total.astype(BF))
        return with_other_core(slope_kernel, total, other, live[k], (pre_act[k],), (BF,))[0]

    terms_a = [width_grad(err1, feats[0], True), width_grad(err1, feats[1], True)]
    give_a = y_give(scalars, terms_a)
    got_a = exchange(give_a, "y", 1)
    gpre1 = backward(1, mm(pass_on(dec_w, 2, 1, give_a)[0], err1, 0, 0))
    terms_b = [width_grad(err0, feats[0], False), width_grad(jnp.concatenate(in1), gpre1, True)]
    give_b = y_give(scalars, terms_b)
    got_b = exchange(give_b, "y", 1)
    near_a, keep_a = y_near(scalars, terms_a, got_a, (give_b,))
    last_a = exchange(near_a, "y", 0)
    back_w = pass_on(dec_w, 0, 2, give_b)
    gpre0 = backward(0, mm(back_w[1], err1, 0, 0) + mm(back_w[0], err0, 0, 0))
    terms_c = [width_grad(jnp.concatenate(in0), gpre0, False)]
    give_c = y_give(scalars, terms_c)
    got_c = exchange(give_c, "y", 1)

    bias_sum = jnp.stack([jnp.sum(g[:HALF].astype(F32), axis=1) for g in (gpre0, gpre1)])
    bias_sum = bias_sum.astype(BF).astype(F32).reshape(2, 4, 64)
    give = jnp.stack([at(bias_sum, y ^ m_second, 1), at(bias_sum, y ^ 2, 1)])
    got = exchange(pass_on(give, 0, 2, give_c), "y", 1)
    near = at(bias_sum, y ^ m_first, 1) + got[1]
    bias_out = at(bias_sum, y, 1) + got[0] + exchange(near, "y", 0)

    near_b, keep_b = y_near(scalars, terms_b, got_b, (give_c,))
    last_b = exchange(near_b, "y", 0)
    done_a = y_quarters(scalars, [(keep_a, last_a)], (near_b,))
    near_c, keep_c = y_near(scalars, terms_c, got_c, (done_a[0],))
    last_c = exchange(near_c, "y", 0)
    done_b = y_quarters(scalars, [(keep_b, last_b)], (near_c,))
    done_c = y_quarters(scalars, [(keep_c, last_c)], (done_b[0],))
    dec_out = write_out(place, (done_a, done_b), ((1, 0), (0, 0), (0, 1))).transpose(0, 2, 1)
    enc_out = write_out(place, (done_b, done_c), ((1, 0), (0, 1)))
    return (enc_out, bias_out[:, None, :], dec_out)


def solution(mesh):
    return jax.shard_map(
        per_device,
        mesh=mesh,
        in_specs=(
            P("tok", None, "layer"),
            P("tok", None, "layer"),
            P("tok", None),
            P("tok", None),
            P(None, None, "layer"),
            P(None, "layer"),
            P(None, "layer", None),
        ),
        out_specs=(P(None, "tok", "layer"), P(None, "layer", "tok"), P(None, "layer", "tok")),
        check_vma=False,
    )
```

```python
import functools
import math

import jax
import jax.numpy as jnp
from jax import lax
from jax.experimental import pallas as pl
from jax.experimental.pallas import tpu as pltpu
from jax.sharding import PartitionSpec as P

AXES = ("tok", "layer")
BF = jnp.bfloat16
F32 = jnp.float32
ROWS = 512
COLS = 144
HALF = 256
WIDE = 8 * COLS
SMALL = 8 * 1024 * 1024
NO_COST = pl.CostEstimate(flops=0, bytes_accessed=0, transcendentals=0)


def device_index(x, y, z, c):
    return ((x % 2) * 4 + y) * 16 + (x // 2) * 8 + z * 2 + c


def pairs_of(partner):
    out = []
    for x in range(4):
        for y in range(4):
            for z in range(4):
                for c in range(2):
                    out.append((device_index(x, y, z, c), device_index(*partner(x, y, z, c))))
    return out


def mask(step, c):
    return 1 if (step + c) % 2 == 0 else 3


def exchange(value, axis, step):
    def partner(x, y, z, c):
        m = mask(step, c)
        return {"x": (x ^ m, y, z, c), "y": (x, y ^ m, z, c), "z": (x, y, z ^ m, c)}[axis]

    return lax.ppermute(value, AXES, pairs_of(partner))


def exchange_far(value, axis):
    def partner(x, y, z, c):
        return {"x": (x ^ 2, y, z, c), "z": (x, y, z ^ 2, c)}[axis]

    return lax.ppermute(value, AXES, pairs_of(partner))


def to_other_core(value):
    return lax.ppermute(value, AXES, pairs_of(lambda x, y, z, c: (x, y, z, 1 - c)))


def to_mate(value, flip):
    return lax.ppermute(value, AXES, pairs_of(lambda x, y, z, c: (x ^ 1, y, z, c ^ flip)))


def activation_slope(pre_act):
    sigma = jax.nn.sigmoid(pre_act)
    return sigma + pre_act * sigma * (1.0 - sigma)


def mm(a, b, ca, cb):
    return lax.dot_general(a, b, (((ca,), (cb,)), ((), ())), preferred_element_type=F32)


def at(array, index, dim=0):
    starts = [jnp.int32(0)] * array.ndim
    starts[dim] = index
    sizes = list(array.shape)
    sizes[dim] = 1
    piece = lax.dynamic_slice(array, starts, sizes, allow_negative_indices=False)
    return piece.reshape(array.shape[:dim] + array.shape[dim + 1 :])


def slot_of(apart, core):
    on_core0 = apart ^ (apart >> 1)
    on_core1 = (on_core0 & 1) * 2 + (on_core0 >> 1)
    return jnp.where(core == 0, on_core0, on_core1)


def order_spec(array):
    tile = (min(16, array.shape[-2]), min(128, array.shape[-1]))
    return pl.BlockSpec((1,) * (array.ndim - 2) + tile, lambda *args: (0,) * array.ndim)


def order_kernel(turn, where_ref, w_ref, dep_ref, own_ref, give_ref):
    block = w_ref[0].T if turn else w_ref[0]
    core = where_ref[2]
    for zz in range(4):
        even = block[2 * zz * COLS : (2 * zz + 1) * COLS]
        odd = block[(2 * zz + 1) * COLS : (2 * zz + 2) * COLS]
        apart = zz ^ where_ref[3]
        own_ref[0, 0, slot_of(apart, core)] = jnp.where(core == 0, even, odd)
        give_ref[0, 0, slot_of(apart, 1 - core)] = jnp.where(core == 0, odd, even)


def ordered_weights(weights, where, dep, turn):
    count = weights.shape[0]
    if turn:
        in_spec = pl.BlockSpec((1, HALF, WIDE), lambda i, h, s: (i, s[0], h))
    else:
        in_spec = pl.BlockSpec((1, WIDE, HALF), lambda i, h, s: (i, h, s[0]))
    out_spec = pl.BlockSpec((1, 1, 4, COLS, HALF), lambda i, h, s: (i, (h + s[1]) % 2, 0, 0, 0))
    shape = jax.ShapeDtypeStruct((count, 2, 4, COLS, HALF), BF)
    return pl.pallas_call(
        functools.partial(order_kernel, turn),
        grid_spec=pltpu.PrefetchScalarGridSpec(
            num_scalar_prefetch=1,
            grid=(count, 2),
            in_specs=[in_spec, order_spec(dep)],
            out_specs=[out_spec, out_spec],
        ),
        out_shape=[shape, shape],
        compiler_params=pltpu.CompilerParams(vmem_limit_bytes=SMALL),
        cost_estimate=NO_COST,
    )(where, weights, dep)


def join_kernel(own_ref, got_ref, dep_ref, out_ref):
    first = pl.program_id(0) == 0
    for hi in range(2):
        for slot in range(4):
            chunk = jnp.where(first, slot * 2 + hi, hi * 4 + slot)
            out_ref[0, chunk, :, :HALF] = own_ref[0, hi, slot]
            out_ref[0, chunk, :, HALF:] = got_ref[0, hi, slot]


def joined_weights(own, got, dep):
    count = own.shape[0]
    in_spec = pl.BlockSpec((1, 2, 4, COLS, HALF), lambda i: (i, 0, 0, 0, 0))
    out = pl.pallas_call(
        join_kernel,
        grid=(count,),
        in_specs=[in_spec, in_spec, order_spec(dep)],
        out_specs=pl.BlockSpec((1, 8, COLS, 2 * HALF), lambda i: (i, 0, 0, 0)),
        out_shape=jax.ShapeDtypeStruct((count, 8, COLS, 2 * HALF), BF),
        compiler_params=pltpu.CompilerParams(vmem_limit_bytes=12 * 1024 * 1024),
        cost_estimate=NO_COST,
    )(own, got, dep)
    return out.reshape(count, WIDE, 2 * HALF)


def pass_on(value, first, count, *deps):
    def kernel(value_ref, *refs):
        refs[-1][...] = value_ref[...]

    block = (1,) + value.shape[1:]
    return pl.pallas_call(
        kernel,
        grid=(count,),
        in_specs=[pl.BlockSpec(block, lambda i: (first + i,) + (0,) * (value.ndim - 1))]
        + [order_spec(dep) for dep in deps],
        out_specs=pl.BlockSpec(block, lambda i: (i,) + (0,) * (value.ndim - 1)),
        out_shape=jax.ShapeDtypeStruct((count,) + value.shape[1:], value.dtype),
        compiler_params=pltpu.CompilerParams(vmem_limit_bytes=SMALL),
        cost_estimate=NO_COST,
    )(value, *deps)


def pack_x(core, own, first, second, far, deps):
    def kernel(core_ref, own_ref, first_ref, second_ref, far_ref, *rest):
        out_ref = rest[-1]
        swap = core_ref[0] != 0
        out_ref[0, :, :ROWS] = own_ref[...]
        out_ref[1, :, :ROWS] = far_ref[...]
        out_ref[0, :, ROWS:] = jnp.where(swap, second_ref[...], first_ref[...])
        out_ref[1, :, ROWS:] = jnp.where(swap, first_ref[...], second_ref[...])

    return pl.pallas_call(
        kernel,
        grid=(1,),
        in_specs=[pl.BlockSpec(memory_space=pltpu.SMEM)]
        + [pl.BlockSpec(memory_space=pltpu.VMEM)] * 4
        + [order_spec(dep) for dep in deps],
        out_specs=pl.BlockSpec(memory_space=pltpu.VMEM),
        out_shape=jax.ShapeDtypeStruct((2, COLS, 2 * ROWS), BF),
        compiler_params=pltpu.CompilerParams(vmem_limit_bytes=SMALL),
        cost_estimate=NO_COST,
    )(core, own, first, second, far, *deps)


def pack_z(pieces, deps):
    def kernel(*refs):
        for k in range(4):
            refs[-1][k] = refs[k][...]

    return pl.pallas_call(
        kernel,
        grid=(1,),
        in_specs=[pl.BlockSpec(memory_space=pltpu.VMEM)] * 4 + [order_spec(dep) for dep in deps],
        out_specs=pl.BlockSpec(memory_space=pltpu.VMEM),
        out_shape=jax.ShapeDtypeStruct((4, COLS, ROWS), BF),
        compiler_params=pltpu.CompilerParams(vmem_limit_bytes=SMALL),
        cost_estimate=NO_COST,
    )(*pieces, *deps)


def sum_kernel(core_ref, own_ref, oth_ref, got_own_ref, got_oth_ref, two_ref, got_two_ref, *outs):
    own = own_ref[...] + got_own_ref[...].astype(F32)
    oth = oth_ref[...] + got_oth_ref[...].astype(F32)
    two = two_ref[...] + got_two_ref[...].astype(F32)
    swap = core_ref[0] != 0
    keep1_ref, first1_ref, second1_ref, far1_ref, keep2_ref, first2_ref, second2_ref, far2_ref = outs
    keep1_ref[...] = own[0]
    first1_ref[...] = jnp.where(swap, oth[1], oth[0]).astype(BF)
    second1_ref[...] = jnp.where(swap, oth[0], oth[1]).astype(BF)
    far1_ref[...] = own[1].astype(BF)
    keep2_ref[...] = two[0]
    first2_ref[...] = two[1].astype(BF)
    second2_ref[...] = two[2].astype(BF)
    far2_ref[...] = two[3].astype(BF)


def heavy_sum(core, one, got1, two, got2):
    def spec(lead, shift):
        return pl.BlockSpec((lead, COLS, 128), lambda j, c: (0, 0, j + shift))

    kept = jax.ShapeDtypeStruct((COLS, ROWS), F32)
    give = jax.ShapeDtypeStruct((COLS, ROWS), BF)
    out = pl.pallas_call(
        sum_kernel,
        grid_spec=pltpu.PrefetchScalarGridSpec(
            num_scalar_prefetch=1,
            grid=(4,),
            in_specs=[spec(2, 0), spec(2, 4), spec(2, 0), spec(2, 4), spec(4, 0), spec(4, 0)],
            out_specs=[pl.BlockSpec((COLS, 128), lambda j, c: (0, j))] * 8,
        ),
        out_shape=[kept, give, give, give] * 2,
        compiler_params=pltpu.CompilerParams(vmem_limit_bytes=SMALL),
        cost_estimate=NO_COST,
    )(core, one, one, got1, got1, two, got2)
    return out[:4], out[4:]


def error_kernel(ids_ref, counts_ref, *refs):
    block = pl.program_id(0)
    scale = 1.0 / math.sqrt(4096)
    for k in range(2):
        recon = refs[4 * k][...]
        for got in refs[4 * k + 1 : 4 * k + 4]:
            recon = recon + got[...].astype(F32)
        live = jnp.where(block < counts_ref[k], 1.0, 0.0).astype(F32)
        refs[10 + k][...] = ((recon - refs[8 + k][0].astype(F32)) * live * scale).astype(BF)


def errors(ids, counts, one, two, targets):
    part = pl.BlockSpec((COLS, 128), lambda j, ids, counts: (0, j))
    out = jax.ShapeDtypeStruct((COLS, ROWS), BF)
    return pl.pallas_call(
        error_kernel,
        grid_spec=pltpu.PrefetchScalarGridSpec(
            num_scalar_prefetch=2,
            grid=(4,),
            in_specs=[part] * 8
            + [
                pl.BlockSpec((1, COLS, 128), lambda j, ids, counts: (ids[j], 0, 0)),
                pl.BlockSpec((1, COLS, 128), lambda j, ids, counts: (ids[4 + j], 0, 0)),
            ],
            out_specs=[part] * 2,
        ),
        out_shape=[out, out],
        compiler_params=pltpu.CompilerParams(vmem_limit_bytes=SMALL),
        cost_estimate=NO_COST,
    )(ids, counts, *one, *two, targets, targets)


def silu_kernel(part_ref, got_ref, live_ref, slope_ref, feat_ref):
    pre = part_ref[...] + got_ref[...].astype(F32)
    live = live_ref[...]
    slope_ref[...] = (activation_slope(pre) * live).astype(BF)
    feat_ref[...] = (jax.nn.silu(pre) * live).astype(BF)


def slope_kernel(part_ref, got_ref, slope_ref, out_ref):
    grad = part_ref[...] + got_ref[...].astype(F32)
    out_ref[...] = (grad * slope_ref[...].astype(F32)).astype(BF)


def with_other_core(kernel, part, got, extra, outs):
    tile = 128
    count = 2 * HALF // tile
    own = pl.BlockSpec((tile, 2 * ROWS), lambda i: (i, 0))
    swapped = pl.BlockSpec((tile, 2 * ROWS), lambda i: ((i + count // 2) % count, 0))
    return pl.pallas_call(
        kernel,
        grid=(count,),
        in_specs=[own, swapped]
        + [own if array.shape[0] > 1 else pl.BlockSpec((1, 2 * ROWS), lambda i: (0, 0)) for array in extra],
        out_specs=[own] * len(outs),
        out_shape=[jax.ShapeDtypeStruct((2 * HALF, 2 * ROWS), kind) for kind in outs],
        compiler_params=pltpu.CompilerParams(vmem_limit_bytes=SMALL),
        cost_estimate=NO_COST,
    )(part, got, *extra)


def term_views(terms):
    return [term.reshape((2, 4, COLS, 2 * HALF) if hi_first else (4, 2, COLS, 2 * HALF)) for term, hi_first in terms]


def term_specs(terms, place):
    def one(hi_first):
        def index(*args):
            hi, slot = place(*args)
            return (hi, slot, 0, 0) if hi_first else (slot, hi, 0, 0)

        return pl.BlockSpec((1, 1, COLS, 2 * HALF), index)

    return [one(hi_first) for _, hi_first in terms]


def y_give(scalars, terms, deps=()):
    count = len(terms)

    def kernel(s_ref, *refs):
        for k in range(count):
            refs[-1][0, k, 0] = refs[k][0, 0]

    return pl.pallas_call(
        kernel,
        grid_spec=pltpu.PrefetchScalarGridSpec(
            num_scalar_prefetch=1,
            grid=(2, 2),
            in_specs=term_specs(terms, lambda i, hi, s: (hi, s[2 + i]))
            + [order_spec(dep) for dep in deps],
            out_specs=pl.BlockSpec((1, count, 1, COLS, 2 * HALF), lambda i, hi, s: (i, 0, hi, 0, 0)),
        ),
        out_shape=jax.ShapeDtypeStruct((2, count, 2, COLS, 2 * HALF), BF),
        compiler_params=pltpu.CompilerParams(vmem_limit_bytes=SMALL),
        cost_estimate=NO_COST,
    )(scalars, *term_views(terms), *deps)


def y_near(scalars, terms, got, deps=()):
    count = len(terms)

    def kernel(s_ref, *refs):
        for k in range(count):
            first = refs[k][0, 0].astype(F32) + refs[2 * count][1, k, 0].astype(F32)
            refs[-2][k, 0] = first.astype(BF)
            keep = refs[count + k][0, 0].astype(F32) + refs[2 * count][0, k, 0].astype(F32)
            refs[-1][k, 0] = keep.astype(BF)

    out = pl.BlockSpec((count, 1, COLS, 2 * HALF), lambda hi, s: (0, hi, 0, 0))
    shape = (count, 2, COLS, 2 * HALF)
    return pl.pallas_call(
        kernel,
        grid_spec=pltpu.PrefetchScalarGridSpec(
            num_scalar_prefetch=1,
            grid=(2,),
            in_specs=term_specs(terms, lambda hi, s: (hi, s[1]))
            + term_specs(terms, lambda hi, s: (hi, s[0]))
            + [pl.BlockSpec((2, count, 1, COLS, 2 * HALF), lambda hi, s: (0, 0, hi, 0, 0))]
            + [order_spec(dep) for dep in deps],
            out_specs=[out, out],
        ),
        out_shape=[jax.ShapeDtypeStruct(shape, BF)] * 2,
        compiler_params=pltpu.CompilerParams(vmem_limit_bytes=SMALL),
        cost_estimate=NO_COST,
    )(scalars, *term_views(terms), *term_views(terms), got, *deps)


def y_quarters(scalars, groups, deps=()):
    sizes = [keep.shape[0] for keep, _ in groups]
    count = sum(sizes)

    def kernel(s_ref, *refs):
        same_ref, core_ref, mate_ref, both_ref = refs[-4:]
        totals = []
        for n, size in enumerate(sizes):
            for k in range(size):
                totals.append(refs[2 * n][k, 0].astype(F32) + refs[2 * n + 1][k, 0].astype(F32))

        @pl.when(pl.program_id(0) == 0)
        def _():
            for k, total in enumerate(totals):
                same_ref[k] = total[:, :HALF]
                core_ref[k] = total[:, HALF:].astype(BF)

        @pl.when(pl.program_id(0) == 1)
        def _():
            for k, total in enumerate(totals):
                mate_ref[k] = total[:, :HALF].astype(BF)
                both_ref[k] = total[:, HALF:].astype(BF)

    def hi_of(i, s):
        return (i + s[4]) % 2

    in_specs, operands = [], []
    for size, group in zip(sizes, groups):
        in_specs += [pl.BlockSpec((size, 1, COLS, 2 * HALF), lambda i, s: (0, hi_of(i, s), 0, 0))] * 2
        operands += group
    out = pl.BlockSpec((count, COLS, HALF), lambda i, s: (0, 0, 0))
    sent = jax.ShapeDtypeStruct((count, COLS, HALF), BF)
    same, core, mate, both = pl.pallas_call(
        kernel,
        grid_spec=pltpu.PrefetchScalarGridSpec(
            num_scalar_prefetch=1,
            grid=(2,),
            in_specs=in_specs + [order_spec(dep) for dep in deps],
            out_specs=[out] * 4,
        ),
        out_shape=[jax.ShapeDtypeStruct((count, COLS, HALF), F32), sent, sent, sent],
        compiler_params=pltpu.CompilerParams(vmem_limit_bytes=SMALL),
        cost_estimate=NO_COST,
    )(scalars, *operands, *deps)
    return same, to_other_core(core), to_mate(mate, 0), to_mate(both, 1)


def write_out(place, groups, picks):
    def kernel(place_ref, *refs):
        core, x_lo = place_ref[0], place_ref[1]
        for n, (group, k) in enumerate(picks):
            same, from_core, from_mate, from_both = [ref[k].astype(F32) for ref in refs[4 * group : 4 * group + 4]]

            def side(own, mate):
                return jnp.where(
                    x_lo == 0, jnp.concatenate([own, mate], axis=1), jnp.concatenate([mate, own], axis=1)
                )

            refs[-1][n, pl.ds(pl.multiple_of(core * COLS, 8), COLS), :] = side(same, from_mate)
            refs[-1][n, pl.ds(pl.multiple_of((1 - core) * COLS, 8), COLS), :] = side(from_core, from_both)

    flat = [array for group in groups for array in group]
    return pl.pallas_call(
        kernel,
        in_specs=[pl.BlockSpec(memory_space=pltpu.SMEM)] + [pl.BlockSpec(memory_space=pltpu.VMEM)] * len(flat),
        out_specs=pl.BlockSpec(memory_space=pltpu.VMEM),
        out_shape=jax.ShapeDtypeStruct((len(picks), 2 * COLS, 2 * HALF), F32),
        compiler_params=pltpu.CompilerParams(vmem_limit_bytes=SMALL),
        cost_estimate=NO_COST,
    )(place, *flat)


def per_device(cache_in, cache_out, read_list, live_blocks, encoder, enc_bias, decoder):
    t = lax.axis_index("tok")
    l = lax.axis_index("layer")
    x_lo, y = t // 4, t % 4
    x_hi, z, core = l // 8, (l // 2) % 4, l % 2
    is_core0 = core == 0
    block_ids = read_list[0]

    def picked(cache):
        rows = cache.at[block_ids].get(mode="promise_in_bounds")
        return rows.reshape(2, ROWS, COLS).transpose(0, 2, 1)

    core_ref = core.reshape(1)

    def gather_both(one, two, steps=None):
        got2 = exchange(two, "z", 0), exchange(two, "z", 1), exchange_far(two, "z")
        got1 = exchange(one, "x", 0), exchange(one, "x", 1), exchange_far(one, "x")
        arrived = got2[0]
        block2 = pack_z((two,) + got2, got1)
        block1 = pack_x(core_ref, one, *got1, got2)
        got1, got2 = exchange(block1, "z", 0), exchange(block2, "x", 0)
        if steps is not None:
            steps.extend([arrived, block1, got2])
        more1 = [exchange(block1, "z", 1), exchange(got1, "z", 1)]
        more2 = [exchange(block2, "x", 1), exchange(got2, "x", 1)]
        near = jnp.where(is_core0, got2, more2[0])
        away = jnp.where(is_core0, more2[0], got2)

        def rows(*parts):
            return tuple(p.reshape(WIDE // 4, 2 * ROWS) for p in parts)

        return (
            rows(block1, got1, *more1),
            (
                jnp.concatenate([block2, near], axis=2).reshape(WIDE // 2, 2 * ROWS),
                jnp.concatenate([more2[1], away], axis=2).reshape(WIDE // 2, 2 * ROWS),
            ),
        )

    own_in = picked(cache_in)
    steps = []
    in0, in1 = gather_both(own_in[0], own_in[1], steps)
    where = jnp.stack([x_lo, x_hi, core, z]).astype(jnp.int32)
    enc_own, enc_give = ordered_weights(encoder, where, steps[0], False)
    dec_own, dec_give = ordered_weights(decoder, where, steps[1], True)
    enc_w = joined_weights(enc_own, to_other_core(enc_give), steps[2])
    dec_w = joined_weights(dec_own, to_other_core(dec_give), steps[2])
    live_other = to_mate(live_blocks, 0)
    row_blocks = jnp.arange(ROWS, dtype=jnp.int32) // 128
    own_live = (row_blocks[None, :] < live_blocks[0][:, None]).astype(F32)
    other_live = (row_blocks[None, :] < live_other[0][:, None]).astype(F32)
    live = jnp.concatenate([own_live, other_live], axis=1)[:, None, :]
    bias_half = lax.dynamic_slice(
        enc_bias, (jnp.int32(0), x_lo * HALF), (2, HALF), allow_negative_indices=False
    )
    bias_mine = jnp.concatenate([bias_half, jnp.zeros_like(bias_half)], axis=1)[:, :, None]

    inputs = (in0, in1)
    mid = WIDE // 2

    def over_width(mat, parts):
        size = WIDE // len(parts)
        total = mm(mat[:size], parts[0], 0, 0)
        for i in range(1, len(parts)):
            total = total + mm(mat[i * size : (i + 1) * size], parts[i], 0, 0)
        return total

    def encode(k):
        total = over_width(enc_w[k], inputs[k]) + bias_mine[k]
        other = to_other_core(total.astype(BF))
        return with_other_core(silu_kernel, total, other, (live[k],), (BF, BF))

    slopes, feats = zip(*[encode(k) for k in range(2)])

    low = mid // 2
    dec_hi = [dec_w[k].reshape(2, mid, 2 * HALF) for k in (1, 2)]

    def slot_term(k):
        return mm(dec_w[0][k * low : (k + 1) * low], feats[0], 1, 0)

    def quarter(hi, first):
        total = mm(at(dec_hi[0], hi), feats[0][:, first : first + ROWS], 1, 0)
        return total + mm(at(dec_hi[1], hi), feats[1][:, first : first + ROWS], 1, 0)

    got = [
        exchange(slot_term(3).astype(BF), "z", 1),
        exchange(quarter(1, 0).astype(BF), "x", 1),
        exchange(slot_term(2).astype(BF), "z", 1),
        exchange(quarter(1 - core, ROWS).astype(BF), "x", 1),
    ]
    give1 = (slot_term(1) + got[0].astype(F32)).astype(BF)
    give2 = (quarter(core, ROWS) + got[1].astype(F32)).astype(BF)
    block1 = (slot_term(0) + got[2].astype(F32)).reshape(2, COLS, 2 * ROWS)
    block2 = (quarter(0, 0) + got[3].astype(F32)).reshape(4, COLS, ROWS)
    got1, got2 = exchange(give1, "z", 0), exchange(give2, "x", 0)
    one, two = heavy_sum(
        core_ref, block1, got1.reshape(2, COLS, 2 * ROWS), block2, got2.reshape(4, COLS, ROWS)
    )
    got2 = exchange(two[1], "z", 0), exchange(two[2], "z", 1), exchange_far(two[3], "z")
    got1 = exchange(one[1], "x", 0), exchange(one[2], "x", 1), exchange_far(one[3], "x")
    own_err = errors(
        block_ids, live_blocks[0], (one[0],) + got1, (two[0],) + got2, cache_out.transpose(0, 2, 1)
    )

    err0, err1 = gather_both(*own_err)

    err0, err1 = jnp.concatenate(err0), jnp.concatenate(err1)

    def width_grad(whole, other, hi_first):
        return mm(whole, other, 1, 1).astype(BF), hi_first

    m_first = jnp.where(is_core0, 1, 3)
    m_second = jnp.where(is_core0, 3, 1)
    scalars = jnp.stack([slot_of(z ^ y ^ m, core) for m in (0, m_first, m_second, 2)] + [x_lo ^ x_hi])
    scalars = scalars.astype(jnp.int32)
    place = jnp.stack([core, x_lo]).astype(jnp.int32)

    def backward(k, total):
        other = to_other_core(total.astype(BF))
        return with_other_core(slope_kernel, total, other, (slopes[k],), (BF,))[0]

    terms_a = [width_grad(err1, feats[0], True), width_grad(err1, feats[1], True)]
    give_a = y_give(scalars, terms_a)
    got_a = exchange(give_a, "y", 1)
    gpre1 = backward(1, mm(pass_on(dec_w, 2, 1, give_a)[0], err1, 0, 0))
    terms_b = [width_grad(err0, feats[0], False), width_grad(jnp.concatenate(in1), gpre1, True)]
    give_b = y_give(scalars, terms_b)
    got_b = exchange(give_b, "y", 1)
    near_a, keep_a = y_near(scalars, terms_a, got_a, (give_b,))
    last_a = exchange(near_a, "y", 0)
    back_w = pass_on(dec_w, 0, 2, give_b)
    gpre0 = backward(0, mm(back_w[1], err1, 0, 0) + mm(back_w[0], err0, 0, 0))
    terms_c = [width_grad(jnp.concatenate(in0), gpre0, False)]
    give_c = y_give(scalars, terms_c)
    got_c = exchange(give_c, "y", 1)

    bias_sum = jnp.stack([jnp.sum(g[:HALF].astype(F32), axis=1) for g in (gpre0, gpre1)])
    bias_sum = bias_sum.astype(BF).astype(F32).reshape(2, 4, 64)
    give = jnp.stack([at(bias_sum, y ^ m_second, 1), at(bias_sum, y ^ 2, 1)])
    give = pass_on(give, 0, 2, give_c)
    got = exchange(give, "y", 1)
    near = at(bias_sum, y ^ m_first, 1) + got[1]
    bias_out = at(bias_sum, y, 1) + got[0] + exchange(near, "y", 0)

    near_b, keep_b = y_near(scalars, terms_b, got_b, (give_c, give))
    last_b = exchange(near_b, "y", 0)
    done_a = y_quarters(scalars, [(keep_a, last_a)], (near_b,))
    near_c, keep_c = y_near(scalars, terms_c, got_c, (done_a[0], got))
    last_c = exchange(near_c, "y", 0)
    done_b = y_quarters(scalars, [(keep_b, last_b)], (near_c,))
    done_c = y_quarters(scalars, [(keep_c, last_c)], (done_b[0],))
    dec_out = write_out(place, (done_a, done_b), ((1, 0), (0, 0), (0, 1))).transpose(0, 2, 1)
    enc_out = write_out(place, (done_b, done_c), ((1, 0), (0, 1)))
    return (enc_out, bias_out[:, None, :], dec_out)


def solution(mesh):
    return jax.shard_map(
        per_device,
        mesh=mesh,
        in_specs=(
            P("tok", None, "layer"),
            P("tok", None, "layer"),
            P("tok", None),
            P("tok", None),
            P(None, None, "layer"),
            P(None, "layer"),
            P(None, "layer", None),
        ),
        out_specs=(P(None, "tok", "layer"), P(None, "layer", "tok"), P(None, "layer", "tok")),
        check_vma=False,
    )
```

```python
import functools
import math

import jax
import jax.numpy as jnp
from jax import lax
from jax.experimental import pallas as pl
from jax.experimental.pallas import tpu as pltpu
from jax.sharding import PartitionSpec as P

AXES = ("tok", "layer")
BF = jnp.bfloat16
F32 = jnp.float32
ROWS = 512
COLS = 144
HALF = 256
WIDE = 8 * COLS
SMALL = 8 * 1024 * 1024
NO_COST = pl.CostEstimate(flops=0, bytes_accessed=0, transcendentals=0)


def device_index(x, y, z, c):
    return ((x % 2) * 4 + y) * 16 + (x // 2) * 8 + z * 2 + c


def pairs_of(partner):
    out = []
    for x in range(4):
        for y in range(4):
            for z in range(4):
                for c in range(2):
                    out.append((device_index(x, y, z, c), device_index(*partner(x, y, z, c))))
    return out


def mask(step, c):
    return 1 if (step + c) % 2 == 0 else 3


def exchange(value, axis, step):
    def partner(x, y, z, c):
        m = mask(step, c)
        return {"x": (x ^ m, y, z, c), "y": (x, y ^ m, z, c), "z": (x, y, z ^ m, c)}[axis]

    return lax.ppermute(value, AXES, pairs_of(partner))


def exchange_far(value, axis):
    def partner(x, y, z, c):
        return {"x": (x ^ 2, y, z, c), "z": (x, y, z ^ 2, c)}[axis]

    return lax.ppermute(value, AXES, pairs_of(partner))


def to_other_core(value):
    return lax.ppermute(value, AXES, pairs_of(lambda x, y, z, c: (x, y, z, 1 - c)))


def to_mate(value, flip):
    return lax.ppermute(value, AXES, pairs_of(lambda x, y, z, c: (x ^ 1, y, z, c ^ flip)))


def activation_slope(pre_act):
    sigma = jax.nn.sigmoid(pre_act)
    return sigma + pre_act * sigma * (1.0 - sigma)


def mm(a, b, ca, cb):
    return lax.dot_general(a, b, (((ca,), (cb,)), ((), ())), preferred_element_type=F32)


def at(array, index, dim=0):
    starts = [jnp.int32(0)] * array.ndim
    starts[dim] = index
    sizes = list(array.shape)
    sizes[dim] = 1
    piece = lax.dynamic_slice(array, starts, sizes, allow_negative_indices=False)
    return piece.reshape(array.shape[:dim] + array.shape[dim + 1 :])


def slot_of(apart, core):
    on_core0 = apart ^ (apart >> 1)
    on_core1 = (on_core0 & 1) * 2 + (on_core0 >> 1)
    return jnp.where(core == 0, on_core0, on_core1)


def order_spec(array):
    tile = (min(16, array.shape[-2]), min(128, array.shape[-1]))
    return pl.BlockSpec((1,) * (array.ndim - 2) + tile, lambda *args: (0,) * array.ndim)


def order_kernel(turn, where_ref, w_ref, dep_ref, own_ref, give_ref):
    block = w_ref[0].T if turn else w_ref[0]
    core = where_ref[2]
    for zz in range(4):
        even = block[2 * zz * COLS : (2 * zz + 1) * COLS]
        odd = block[(2 * zz + 1) * COLS : (2 * zz + 2) * COLS]
        apart = zz ^ where_ref[3]
        own_ref[0, 0, slot_of(apart, core)] = jnp.where(core == 0, even, odd)
        give_ref[0, 0, slot_of(apart, 1 - core)] = jnp.where(core == 0, odd, even)


def ordered_weights(weights, where, dep, turn):
    count = weights.shape[0]
    if turn:
        in_spec = pl.BlockSpec((1, HALF, WIDE), lambda i, h, s: (i, s[0], h))
    else:
        in_spec = pl.BlockSpec((1, WIDE, HALF), lambda i, h, s: (i, h, s[0]))
    out_spec = pl.BlockSpec((1, 1, 4, COLS, HALF), lambda i, h, s: (i, (h + s[1]) % 2, 0, 0, 0))
    shape = jax.ShapeDtypeStruct((count, 2, 4, COLS, HALF), BF)
    return pl.pallas_call(
        functools.partial(order_kernel, turn),
        grid_spec=pltpu.PrefetchScalarGridSpec(
            num_scalar_prefetch=1,
            grid=(count, 2),
            in_specs=[in_spec, order_spec(dep)],
            out_specs=[out_spec, out_spec],
        ),
        out_shape=[shape, shape],
        compiler_params=pltpu.CompilerParams(vmem_limit_bytes=SMALL),
        cost_estimate=NO_COST,
    )(where, weights, dep)


def join_kernel(own_ref, got_ref, dep_ref, out_ref):
    first = pl.program_id(0) == 0
    for hi in range(2):
        for slot in range(4):
            chunk = jnp.where(first, slot * 2 + hi, hi * 4 + slot)
            out_ref[0, chunk, :, :HALF] = own_ref[0, hi, slot]
            out_ref[0, chunk, :, HALF:] = got_ref[0, hi, slot]


def joined_weights(own, got, dep):
    count = own.shape[0]
    in_spec = pl.BlockSpec((1, 2, 4, COLS, HALF), lambda i: (i, 0, 0, 0, 0))
    out = pl.pallas_call(
        join_kernel,
        grid=(count,),
        in_specs=[in_spec, in_spec, order_spec(dep)],
        out_specs=pl.BlockSpec((1, 8, COLS, 2 * HALF), lambda i: (i, 0, 0, 0)),
        out_shape=jax.ShapeDtypeStruct((count, 8, COLS, 2 * HALF), BF),
        compiler_params=pltpu.CompilerParams(vmem_limit_bytes=12 * 1024 * 1024),
        cost_estimate=NO_COST,
    )(own, got, dep)
    return out.reshape(count, WIDE, 2 * HALF)


def pass_on(value, first, count, *deps):
    def kernel(value_ref, *refs):
        refs[-1][...] = value_ref[...]

    block = (1,) + value.shape[1:]
    return pl.pallas_call(
        kernel,
        grid=(count,),
        in_specs=[pl.BlockSpec(block, lambda i: (first + i,) + (0,) * (value.ndim - 1))]
        + [order_spec(dep) for dep in deps],
        out_specs=pl.BlockSpec(block, lambda i: (i,) + (0,) * (value.ndim - 1)),
        out_shape=jax.ShapeDtypeStruct((count,) + value.shape[1:], value.dtype),
        compiler_params=pltpu.CompilerParams(vmem_limit_bytes=SMALL),
        cost_estimate=NO_COST,
    )(value, *deps)


def pack_x(core, own, first, second, far, deps):
    def kernel(core_ref, own_ref, first_ref, second_ref, far_ref, *rest):
        out_ref = rest[-1]
        swap = core_ref[0] != 0
        out_ref[0, :, :ROWS] = own_ref[...]
        out_ref[1, :, :ROWS] = far_ref[...]
        out_ref[0, :, ROWS:] = jnp.where(swap, second_ref[...], first_ref[...])
        out_ref[1, :, ROWS:] = jnp.where(swap, first_ref[...], second_ref[...])

    return pl.pallas_call(
        kernel,
        grid=(1,),
        in_specs=[pl.BlockSpec(memory_space=pltpu.SMEM)]
        + [pl.BlockSpec(memory_space=pltpu.VMEM)] * 4
        + [order_spec(dep) for dep in deps],
        out_specs=pl.BlockSpec(memory_space=pltpu.VMEM),
        out_shape=jax.ShapeDtypeStruct((2, COLS, 2 * ROWS), BF),
        compiler_params=pltpu.CompilerParams(vmem_limit_bytes=SMALL),
        cost_estimate=NO_COST,
    )(core, own, first, second, far, *deps)


def pack_z(pieces, deps):
    def kernel(*refs):
        for k in range(4):
            refs[-1][k] = refs[k][...]

    return pl.pallas_call(
        kernel,
        grid=(1,),
        in_specs=[pl.BlockSpec(memory_space=pltpu.VMEM)] * 4 + [order_spec(dep) for dep in deps],
        out_specs=pl.BlockSpec(memory_space=pltpu.VMEM),
        out_shape=jax.ShapeDtypeStruct((4, COLS, ROWS), BF),
        compiler_params=pltpu.CompilerParams(vmem_limit_bytes=SMALL),
        cost_estimate=NO_COST,
    )(*pieces, *deps)


def sum_kernel(core_ref, own_ref, oth_ref, got_own_ref, got_oth_ref, two_ref, got_two_ref, *outs):
    own = own_ref[...] + got_own_ref[...].astype(F32)
    oth = oth_ref[...] + got_oth_ref[...].astype(F32)
    two = two_ref[...] + got_two_ref[...].astype(F32)
    swap = core_ref[0] != 0
    keep1_ref, first1_ref, second1_ref, far1_ref, keep2_ref, first2_ref, second2_ref, far2_ref = outs
    keep1_ref[...] = own[0]
    first1_ref[...] = jnp.where(swap, oth[1], oth[0]).astype(BF)
    second1_ref[...] = jnp.where(swap, oth[0], oth[1]).astype(BF)
    far1_ref[...] = own[1].astype(BF)
    keep2_ref[...] = two[0]
    first2_ref[...] = two[1].astype(BF)
    second2_ref[...] = two[2].astype(BF)
    far2_ref[...] = two[3].astype(BF)


def heavy_sum(core, one, got1, two, got2):
    def spec(lead, shift):
        return pl.BlockSpec((lead, COLS, 128), lambda j, c: (0, 0, j + shift))

    kept = jax.ShapeDtypeStruct((COLS, ROWS), F32)
    give = jax.ShapeDtypeStruct((COLS, ROWS), BF)
    out = pl.pallas_call(
        sum_kernel,
        grid_spec=pltpu.PrefetchScalarGridSpec(
            num_scalar_prefetch=1,
            grid=(4,),
            in_specs=[spec(2, 0), spec(2, 4), spec(2, 0), spec(2, 4), spec(4, 0), spec(4, 0)],
            out_specs=[pl.BlockSpec((COLS, 128), lambda j, c: (0, j))] * 8,
        ),
        out_shape=[kept, give, give, give] * 2,
        compiler_params=pltpu.CompilerParams(vmem_limit_bytes=SMALL),
        cost_estimate=NO_COST,
    )(core, one, one, got1, got1, two, got2)
    return out[:4], out[4:]


def error_kernel(ids_ref, counts_ref, *refs):
    block = pl.program_id(0)
    scale = 1.0 / math.sqrt(4096)
    for k in range(2):
        recon = refs[4 * k][...]
        for got in refs[4 * k + 1 : 4 * k + 4]:
            recon = recon + got[...].astype(F32)
        live = jnp.where(block < counts_ref[k], 1.0, 0.0).astype(F32)
        refs[10 + k][...] = ((recon - refs[8 + k][0].astype(F32)) * live * scale).astype(BF)


def errors(ids, counts, one, two, targets):
    part = pl.BlockSpec((COLS, 128), lambda j, ids, counts: (0, j))
    out = jax.ShapeDtypeStruct((COLS, ROWS), BF)
    return pl.pallas_call(
        error_kernel,
        grid_spec=pltpu.PrefetchScalarGridSpec(
            num_scalar_prefetch=2,
            grid=(4,),
            in_specs=[part] * 8
            + [
                pl.BlockSpec((1, COLS, 128), lambda j, ids, counts: (ids[j], 0, 0)),
                pl.BlockSpec((1, COLS, 128), lambda j, ids, counts: (ids[4 + j], 0, 0)),
            ],
            out_specs=[part] * 2,
        ),
        out_shape=[out, out],
        compiler_params=pltpu.CompilerParams(vmem_limit_bytes=SMALL),
        cost_estimate=NO_COST,
    )(ids, counts, *one, *two, targets, targets)


def silu_kernel(part_ref, got_ref, live_ref, slope_ref, feat_ref):
    pre = part_ref[...] + got_ref[...].astype(F32)
    live = live_ref[...]
    slope_ref[...] = (activation_slope(pre) * live).astype(BF)
    feat_ref[...] = (jax.nn.silu(pre) * live).astype(BF)


def slope_kernel(part_ref, got_ref, slope_ref, out_ref, sum_ref):
    grad = part_ref[...] + got_ref[...].astype(F32)
    grad = (grad * slope_ref[...].astype(F32)).astype(BF)
    out_ref[...] = grad
    sum_ref[...] = mm(jnp.ones((8, 2 * ROWS), BF), grad, 1, 1)


def with_other_core(kernel, part, got, extra, outs, with_sum=0):
    tile = 128
    count = 2 * HALF // tile
    own = pl.BlockSpec((tile, 2 * ROWS), lambda i: (i, 0))
    swapped = pl.BlockSpec((tile, 2 * ROWS), lambda i: ((i + count // 2) % count, 0))
    return pl.pallas_call(
        kernel,
        grid=(count,),
        in_specs=[own, swapped]
        + [own if array.shape[0] > 1 else pl.BlockSpec((1, 2 * ROWS), lambda i: (0, 0)) for array in extra],
        out_specs=[own] * len(outs) + [pl.BlockSpec((8, tile), lambda i: (0, i))] * with_sum,
        out_shape=[jax.ShapeDtypeStruct((2 * HALF, 2 * ROWS), kind) for kind in outs]
        + [jax.ShapeDtypeStruct((8, 2 * HALF), F32)] * with_sum,
        compiler_params=pltpu.CompilerParams(vmem_limit_bytes=SMALL),
        cost_estimate=NO_COST,
    )(part, got, *extra)


def term_views(terms):
    return [term.reshape((2, 4, COLS, 2 * HALF) if hi_first else (4, 2, COLS, 2 * HALF)) for term, hi_first in terms]


def term_specs(terms, place):
    def one(hi_first):
        def index(*args):
            hi, slot = place(*args)
            return (hi, slot, 0, 0) if hi_first else (slot, hi, 0, 0)

        return pl.BlockSpec((1, 1, COLS, 2 * HALF), index)

    return [one(hi_first) for _, hi_first in terms]


MORE = 16


def more_rows(sums):
    row = jnp.concatenate([ref[:, :HALF] for ref in sums], axis=1)
    return jnp.concatenate([row, row], axis=0)


def y_give(scalars, terms, deps=(), sums=()):
    count = len(terms)
    rows = COLS + (MORE if sums else 0)

    def kernel(s_ref, *refs):
        for k in range(count):
            refs[-1][0, k, 0, :COLS] = refs[k][0, 0]
        if sums:
            refs[-1][0, 0, 0, COLS:] = more_rows(refs[count : count + 2]).astype(BF)

    return pl.pallas_call(
        kernel,
        grid_spec=pltpu.PrefetchScalarGridSpec(
            num_scalar_prefetch=1,
            grid=(2, 2),
            in_specs=term_specs(terms, lambda i, hi, s: (hi, s[2 + i]))
            + [pl.BlockSpec((8, 2 * HALF), lambda i, hi, s: (0, 0))] * len(sums)
            + [order_spec(dep) for dep in deps],
            out_specs=pl.BlockSpec((1, count, 1, rows, 2 * HALF), lambda i, hi, s: (i, 0, hi, 0, 0)),
        ),
        out_shape=jax.ShapeDtypeStruct((2, count, 2, rows, 2 * HALF), BF),
        compiler_params=pltpu.CompilerParams(vmem_limit_bytes=SMALL),
        cost_estimate=NO_COST,
    )(scalars, *term_views(terms), *sums, *deps)


def y_near(scalars, terms, got, deps=(), sums=()):
    count = len(terms)
    rows = got.shape[3]

    def kernel(s_ref, *refs):
        got_ref = refs[2 * count]
        near_ref, keep_ref = refs[-2:]
        for k in range(count):
            first = refs[k][0, 0].astype(F32) + got_ref[1, k, 0, :COLS].astype(F32)
            near_ref[k, 0, :COLS] = first.astype(BF)
            keep = refs[count + k][0, 0].astype(F32) + got_ref[0, k, 0, :COLS].astype(F32)
            keep_ref[k, 0, :COLS] = keep.astype(BF)
        if sums:
            more = more_rows(refs[2 * count + 1 : 2 * count + 3])
            near_ref[0, 0, COLS:] = (more + got_ref[1, 0, 0, COLS:].astype(F32)).astype(BF)
            keep_ref[0, 0, COLS:] = (more + got_ref[0, 0, 0, COLS:].astype(F32)).astype(BF)

    out = pl.BlockSpec((count, 1, rows, 2 * HALF), lambda hi, s: (0, hi, 0, 0))
    shape = (count, 2, rows, 2 * HALF)
    return pl.pallas_call(
        kernel,
        grid_spec=pltpu.PrefetchScalarGridSpec(
            num_scalar_prefetch=1,
            grid=(2,),
            in_specs=term_specs(terms, lambda hi, s: (hi, s[1]))
            + term_specs(terms, lambda hi, s: (hi, s[0]))
            + [pl.BlockSpec((2, count, 1, rows, 2 * HALF), lambda hi, s: (0, 0, hi, 0, 0))]
            + [pl.BlockSpec((8, 2 * HALF), lambda hi, s: (0, 0))] * len(sums)
            + [order_spec(dep) for dep in deps],
            out_specs=[out, out],
        ),
        out_shape=[jax.ShapeDtypeStruct(shape, BF)] * 2,
        compiler_params=pltpu.CompilerParams(vmem_limit_bytes=SMALL),
        cost_estimate=NO_COST,
    )(scalars, *term_views(terms), *term_views(terms), got, *sums, *deps)


def y_quarters(scalars, keep, last, deps=()):
    count, _, rows, _ = keep.shape

    def kernel(s_ref, keep_ref, last_ref, *refs):
        outs = refs[len(deps) :]
        totals = [keep_ref[k, 0].astype(F32) + last_ref[k, 0].astype(F32) for k in range(count)]

        @pl.when(pl.program_id(0) == 0)
        def _():
            for k, total in enumerate(totals):
                outs[0][k] = total[:COLS, :HALF]
                outs[1][k] = total[:COLS, HALF:].astype(BF)
            if rows > COLS:
                outs[4][...] = totals[0][COLS:]

        @pl.when(pl.program_id(0) == 1)
        def _():
            for k, total in enumerate(totals):
                outs[2][k] = total[:COLS, :HALF].astype(BF)
                outs[3][k] = total[:COLS, HALF:].astype(BF)

    part = pl.BlockSpec((count, 1, rows, 2 * HALF), lambda i, s: (0, (i + s[4]) % 2, 0, 0))
    out = pl.BlockSpec((count, COLS, HALF), lambda i, s: (0, 0, 0))
    sent = jax.ShapeDtypeStruct((count, COLS, HALF), BF)
    more = rows - COLS
    same, core, mate, both, *sums = pl.pallas_call(
        kernel,
        grid_spec=pltpu.PrefetchScalarGridSpec(
            num_scalar_prefetch=1,
            grid=(2,),
            in_specs=[part, part] + [order_spec(dep) for dep in deps],
            out_specs=[out] * 4 + [pl.BlockSpec((MORE, 2 * HALF), lambda i, s: (0, 0))] * (more // MORE),
        ),
        out_shape=[jax.ShapeDtypeStruct((count, COLS, HALF), F32), sent, sent, sent]
        + [jax.ShapeDtypeStruct((MORE, 2 * HALF), F32)] * (more // MORE),
        compiler_params=pltpu.CompilerParams(vmem_limit_bytes=SMALL),
        cost_estimate=NO_COST,
    )(scalars, keep, last, *deps)
    return (same, to_other_core(core), to_mate(mate, 0), to_mate(both, 1)), sums


def write_out(place, groups, picks):
    def kernel(place_ref, *refs):
        core, x_lo = place_ref[0], place_ref[1]
        for n, (group, k) in enumerate(picks):
            same, from_core, from_mate, from_both = [ref[k].astype(F32) for ref in refs[4 * group : 4 * group + 4]]

            def side(own, mate):
                return jnp.where(
                    x_lo == 0, jnp.concatenate([own, mate], axis=1), jnp.concatenate([mate, own], axis=1)
                )

            refs[-1][n, pl.ds(pl.multiple_of(core * COLS, 8), COLS), :] = side(same, from_mate)
            refs[-1][n, pl.ds(pl.multiple_of((1 - core) * COLS, 8), COLS), :] = side(from_core, from_both)

    flat = [array for group in groups for array in group]
    return pl.pallas_call(
        kernel,
        in_specs=[pl.BlockSpec(memory_space=pltpu.SMEM)] + [pl.BlockSpec(memory_space=pltpu.VMEM)] * len(flat),
        out_specs=pl.BlockSpec(memory_space=pltpu.VMEM),
        out_shape=jax.ShapeDtypeStruct((len(picks), 2 * COLS, 2 * HALF), F32),
        compiler_params=pltpu.CompilerParams(vmem_limit_bytes=SMALL),
        cost_estimate=NO_COST,
    )(place, *flat)


def per_device(cache_in, cache_out, read_list, live_blocks, encoder, enc_bias, decoder):
    t = lax.axis_index("tok")
    l = lax.axis_index("layer")
    x_lo, y = t // 4, t % 4
    x_hi, z, core = l // 8, (l // 2) % 4, l % 2
    is_core0 = core == 0
    block_ids = read_list[0]

    def picked(cache):
        rows = cache.at[block_ids].get(mode="promise_in_bounds")
        return rows.reshape(2, ROWS, COLS).transpose(0, 2, 1)

    core_ref = core.reshape(1)

    def gather_both(one, two, steps=None):
        far1, far2 = exchange_far(one, "x"), exchange_far(two, "z")
        got2 = exchange(two, "z", 0), exchange(two, "z", 1), far2
        got1 = exchange(one, "x", 0), exchange(one, "x", 1), far1
        arrived = got2[0]
        block2 = pack_z((two,) + got2, got1)
        block1 = pack_x(core_ref, one, *got1, got2)
        got1, got2 = exchange(block1, "z", 0), exchange(block2, "x", 0)
        if steps is not None:
            steps.extend([arrived, block1, got2])
        more1 = [exchange(block1, "z", 1), exchange(got1, "z", 1)]
        more2 = [exchange(block2, "x", 1), exchange(got2, "x", 1)]
        near = jnp.where(is_core0, got2, more2[0])
        away = jnp.where(is_core0, more2[0], got2)

        def rows(*parts):
            return tuple(p.reshape(WIDE // 4, 2 * ROWS) for p in parts)

        return (
            rows(block1, got1, *more1),
            (
                jnp.concatenate([block2, near], axis=2).reshape(WIDE // 2, 2 * ROWS),
                jnp.concatenate([more2[1], away], axis=2).reshape(WIDE // 2, 2 * ROWS),
            ),
        )

    own_in = picked(cache_in)
    steps = []
    in0, in1 = gather_both(own_in[0], own_in[1], steps)
    where = jnp.stack([x_lo, x_hi, core, z]).astype(jnp.int32)
    enc_own, enc_give = ordered_weights(encoder, where, steps[0], False)
    dec_own, dec_give = ordered_weights(decoder, where, steps[1], True)
    enc_w = joined_weights(enc_own, to_other_core(enc_give), steps[2])
    dec_w = joined_weights(dec_own, to_other_core(dec_give), steps[2])
    live_other = to_mate(live_blocks, 0)
    row_blocks = jnp.arange(ROWS, dtype=jnp.int32) // 128
    own_live = (row_blocks[None, :] < live_blocks[0][:, None]).astype(F32)
    other_live = (row_blocks[None, :] < live_other[0][:, None]).astype(F32)
    live = jnp.concatenate([own_live, other_live], axis=1)[:, None, :]
    bias_half = lax.dynamic_slice(
        enc_bias, (jnp.int32(0), x_lo * HALF), (2, HALF), allow_negative_indices=False
    )
    bias_mine = jnp.concatenate([bias_half, jnp.zeros_like(bias_half)], axis=1)[:, :, None]

    inputs = (in0, in1)
    mid = WIDE // 2

    def over_width(mat, parts):
        size = WIDE // len(parts)
        total = mm(mat[:size], parts[0], 0, 0)
        for i in range(1, len(parts)):
            total = total + mm(mat[i * size : (i + 1) * size], parts[i], 0, 0)
        return total

    def encode(k):
        total = over_width(enc_w[k], inputs[k]) + bias_mine[k]
        other = to_other_core(total.astype(BF))
        return with_other_core(silu_kernel, total, other, (live[k],), (BF, BF))

    slopes, feats = zip(*[encode(k) for k in range(2)])

    low = mid // 2
    dec_hi = [dec_w[k].reshape(2, mid, 2 * HALF) for k in (1, 2)]

    def slot_term(k):
        return mm(dec_w[0][k * low : (k + 1) * low], feats[0], 1, 0)

    def quarter(hi, first):
        total = mm(at(dec_hi[0], hi), feats[0][:, first : first + ROWS], 1, 0)
        return total + mm(at(dec_hi[1], hi), feats[1][:, first : first + ROWS], 1, 0)

    got = [
        exchange(slot_term(3).astype(BF), "z", 1),
        exchange(quarter(1, 0).astype(BF), "x", 1),
        exchange(slot_term(2).astype(BF), "z", 1),
        exchange(quarter(1 - core, ROWS).astype(BF), "x", 1),
    ]
    give1 = (slot_term(1) + got[0].astype(F32)).astype(BF)
    give2 = (quarter(core, ROWS) + got[1].astype(F32)).astype(BF)
    block1 = (slot_term(0) + got[2].astype(F32)).reshape(2, COLS, 2 * ROWS)
    block2 = (quarter(0, 0) + got[3].astype(F32)).reshape(4, COLS, ROWS)
    got1, got2 = exchange(give1, "z", 0), exchange(give2, "x", 0)
    one, two = heavy_sum(
        core_ref, block1, got1.reshape(2, COLS, 2 * ROWS), block2, got2.reshape(4, COLS, ROWS)
    )
    far1, far2 = exchange_far(one[3], "x"), exchange_far(two[3], "z")
    got2 = exchange(two[1], "z", 0), exchange(two[2], "z", 1), far2
    got1 = exchange(one[1], "x", 0), exchange(one[2], "x", 1), far1
    own_err = errors(
        block_ids, live_blocks[0], (one[0],) + got1, (two[0],) + got2, cache_out.transpose(0, 2, 1)
    )

    err0, err1 = gather_both(*own_err)

    err0, err1 = jnp.concatenate(err0), jnp.concatenate(err1)

    def width_grad(whole, other, hi_first):
        return mm(whole, other, 1, 1).astype(BF), hi_first

    m_first = jnp.where(is_core0, 1, 3)
    m_second = jnp.where(is_core0, 3, 1)
    scalars = jnp.stack([slot_of(z ^ y ^ m, core) for m in (0, m_first, m_second, 2)] + [x_lo ^ x_hi])
    scalars = scalars.astype(jnp.int32)
    place = jnp.stack([core, x_lo]).astype(jnp.int32)

    def backward(k, total):
        other = to_other_core(total.astype(BF))
        return with_other_core(slope_kernel, total, other, (slopes[k],), (BF,), 1)

    terms_a = [width_grad(err1, feats[0], True), width_grad(err1, feats[1], True)]
    give_a = y_give(scalars, terms_a)
    got_a = exchange(give_a, "y", 1)
    gpre1, sum1 = backward(1, mm(pass_on(dec_w, 2, 1, give_a)[0], err1, 0, 0))
    terms_b = [width_grad(err0, feats[0], False), width_grad(jnp.concatenate(in1), gpre1, True)]
    give_b = y_give(scalars, terms_b)
    got_b = exchange(give_b, "y", 1)
    near_a, keep_a = y_near(scalars, terms_a, got_a, (give_b,))
    last_a = exchange(near_a, "y", 0)
    back_w = pass_on(dec_w, 0, 2, give_b)
    gpre0, sum0 = backward(0, mm(back_w[1], err1, 0, 0) + mm(back_w[0], err0, 0, 0))
    terms_c = [width_grad(jnp.concatenate(in0), gpre0, False)]
    give_c = y_give(scalars, terms_c, (), (sum0, sum1))
    got_c = exchange(give_c, "y", 1)

    near_b, keep_b = y_near(scalars, terms_b, got_b, (give_c,))
    last_b = exchange(near_b, "y", 0)
    done_a, _ = y_quarters(scalars, keep_a, last_a, (near_b,))
    near_c, keep_c = y_near(scalars, terms_c, got_c, (done_a[0],), (sum0, sum1))
    last_c = exchange(near_c, "y", 0)
    done_b, _ = y_quarters(scalars, keep_b, last_b, (near_c,))
    done_c, sums = y_quarters(scalars, keep_c, last_c, (done_b[0],))
    bias_out = at(sums[0][0].reshape(2, 4, 64), y, 1)
    dec_out = write_out(place, (done_a, done_b), ((1, 0), (0, 0), (0, 1))).transpose(0, 2, 1)
    enc_out = write_out(place, (done_b, done_c), ((1, 0), (0, 1)))
    return (enc_out, bias_out[:, None, :], dec_out)


def solution(mesh):
    return jax.shard_map(
        per_device,
        mesh=mesh,
        in_specs=(
            P("tok", None, "layer"),
            P("tok", None, "layer"),
            P("tok", None),
            P("tok", None),
            P(None, None, "layer"),
            P(None, "layer"),
            P(None, "layer", None),
        ),
        out_specs=(P(None, "tok", "layer"), P(None, "layer", "tok"), P(None, "layer", "tok")),
        check_vma=False,
    )
```

```python
import functools
import math

import jax
import jax.numpy as jnp
from jax import lax
from jax.experimental import pallas as pl
from jax.experimental.pallas import tpu as pltpu
from jax.sharding import PartitionSpec as P

AXES = ("tok", "layer")
BF = jnp.bfloat16
F32 = jnp.float32
ROWS = 512
COLS = 144
HALF = 256
WIDE = 8 * COLS
SMALL = 8 * 1024 * 1024
NO_COST = pl.CostEstimate(flops=0, bytes_accessed=0, transcendentals=0)


def device_index(x, y, z, c):
    return ((x % 2) * 4 + y) * 16 + (x // 2) * 8 + z * 2 + c


def pairs_of(partner):
    out = []
    for x in range(4):
        for y in range(4):
            for z in range(4):
                for c in range(2):
                    out.append((device_index(x, y, z, c), device_index(*partner(x, y, z, c))))
    return out


def mask(step, c):
    return 1 if (step + c) % 2 == 0 else 3


def exchange(value, axis, step):
    def partner(x, y, z, c):
        m = mask(step, c)
        return {"x": (x ^ m, y, z, c), "y": (x, y ^ m, z, c), "z": (x, y, z ^ m, c)}[axis]

    return lax.ppermute(value, AXES, pairs_of(partner))


def exchange_far(value, axis):
    def partner(x, y, z, c):
        return {"x": (x ^ 2, y, z, c), "z": (x, y, z ^ 2, c)}[axis]

    return lax.ppermute(value, AXES, pairs_of(partner))


def to_other_core(value):
    return lax.ppermute(value, AXES, pairs_of(lambda x, y, z, c: (x, y, z, 1 - c)))


def to_mate(value, flip):
    return lax.ppermute(value, AXES, pairs_of(lambda x, y, z, c: (x ^ 1, y, z, c ^ flip)))


def activation_slope(pre_act):
    sigma = jax.nn.sigmoid(pre_act)
    return sigma + pre_act * sigma * (1.0 - sigma)


def mm(a, b, ca, cb):
    return lax.dot_general(a, b, (((ca,), (cb,)), ((), ())), preferred_element_type=F32)


def at(array, index, dim=0):
    starts = [jnp.int32(0)] * array.ndim
    starts[dim] = index
    sizes = list(array.shape)
    sizes[dim] = 1
    piece = lax.dynamic_slice(array, starts, sizes, allow_negative_indices=False)
    return piece.reshape(array.shape[:dim] + array.shape[dim + 1 :])


def slot_of(apart, core):
    on_core0 = apart ^ (apart >> 1)
    on_core1 = (on_core0 & 1) * 2 + (on_core0 >> 1)
    return jnp.where(core == 0, on_core0, on_core1)


def order_spec(array):
    tile = (min(16, array.shape[-2]), min(128, array.shape[-1]))
    return pl.BlockSpec((1,) * (array.ndim - 2) + tile, lambda *args: (0,) * array.ndim)


def order_kernel(turn, where_ref, w_ref, dep_ref, own_ref, give_ref):
    block = w_ref[0].T if turn else w_ref[0]
    core = where_ref[2]
    for zz in range(4):
        even = block[2 * zz * COLS : (2 * zz + 1) * COLS]
        odd = block[(2 * zz + 1) * COLS : (2 * zz + 2) * COLS]
        apart = zz ^ where_ref[3]
        own_ref[0, 0, slot_of(apart, core)] = jnp.where(core == 0, even, odd)
        give_ref[0, 0, slot_of(apart, 1 - core)] = jnp.where(core == 0, odd, even)


def ordered_weights(weights, where, dep, turn):
    count = weights.shape[0]
    if turn:
        in_spec = pl.BlockSpec((1, HALF, WIDE), lambda i, h, s: (i, s[0], h))
    else:
        in_spec = pl.BlockSpec((1, WIDE, HALF), lambda i, h, s: (i, h, s[0]))
    out_spec = pl.BlockSpec((1, 1, 4, COLS, HALF), lambda i, h, s: (i, (h + s[1]) % 2, 0, 0, 0))
    shape = jax.ShapeDtypeStruct((count, 2, 4, COLS, HALF), BF)
    return pl.pallas_call(
        functools.partial(order_kernel, turn),
        grid_spec=pltpu.PrefetchScalarGridSpec(
            num_scalar_prefetch=1,
            grid=(count, 2),
            in_specs=[in_spec, order_spec(dep)],
            out_specs=[out_spec, out_spec],
        ),
        out_shape=[shape, shape],
        compiler_params=pltpu.CompilerParams(vmem_limit_bytes=SMALL),
        cost_estimate=NO_COST,
    )(where, weights, dep)


def join_kernel(own_ref, got_ref, dep_ref, out_ref):
    first = pl.program_id(0) == 0
    for hi in range(2):
        for slot in range(4):
            chunk = jnp.where(first, slot * 2 + hi, hi * 4 + slot)
            out_ref[0, chunk, :, :HALF] = own_ref[0, hi, slot]
            out_ref[0, chunk, :, HALF:] = got_ref[0, hi, slot]


def joined_weights(own, got, dep):
    count = own.shape[0]
    in_spec = pl.BlockSpec((1, 2, 4, COLS, HALF), lambda i: (i, 0, 0, 0, 0))
    out = pl.pallas_call(
        join_kernel,
        grid=(count,),
        in_specs=[in_spec, in_spec, order_spec(dep)],
        out_specs=pl.BlockSpec((1, 8, COLS, 2 * HALF), lambda i: (i, 0, 0, 0)),
        out_shape=jax.ShapeDtypeStruct((count, 8, COLS, 2 * HALF), BF),
        compiler_params=pltpu.CompilerParams(vmem_limit_bytes=12 * 1024 * 1024),
        cost_estimate=NO_COST,
    )(own, got, dep)
    return out.reshape(count, WIDE, 2 * HALF)


def pass_on(value, first, count, *deps):
    def kernel(value_ref, *refs):
        refs[-1][...] = value_ref[...]

    block = (1,) + value.shape[1:]
    return pl.pallas_call(
        kernel,
        grid=(count,),
        in_specs=[pl.BlockSpec(block, lambda i: (first + i,) + (0,) * (value.ndim - 1))]
        + [order_spec(dep) for dep in deps],
        out_specs=pl.BlockSpec(block, lambda i: (i,) + (0,) * (value.ndim - 1)),
        out_shape=jax.ShapeDtypeStruct((count,) + value.shape[1:], value.dtype),
        compiler_params=pltpu.CompilerParams(vmem_limit_bytes=SMALL),
        cost_estimate=NO_COST,
    )(value, *deps)


def pack_x(core, own, first, second, far, deps):
    def kernel(core_ref, own_ref, first_ref, second_ref, far_ref, *rest):
        out_ref = rest[-1]
        swap = core_ref[0] != 0
        out_ref[0, :, :ROWS] = own_ref[...]
        out_ref[1, :, :ROWS] = far_ref[...]
        out_ref[0, :, ROWS:] = jnp.where(swap, second_ref[...], first_ref[...])
        out_ref[1, :, ROWS:] = jnp.where(swap, first_ref[...], second_ref[...])

    return pl.pallas_call(
        kernel,
        grid=(1,),
        in_specs=[pl.BlockSpec(memory_space=pltpu.SMEM)]
        + [pl.BlockSpec(memory_space=pltpu.VMEM)] * 4
        + [order_spec(dep) for dep in deps],
        out_specs=pl.BlockSpec(memory_space=pltpu.VMEM),
        out_shape=jax.ShapeDtypeStruct((2, COLS, 2 * ROWS), BF),
        compiler_params=pltpu.CompilerParams(vmem_limit_bytes=SMALL),
        cost_estimate=NO_COST,
    )(core, own, first, second, far, *deps)


def pack_z(pieces, deps):
    def kernel(*refs):
        for k in range(4):
            refs[-1][k] = refs[k][...]

    return pl.pallas_call(
        kernel,
        grid=(1,),
        in_specs=[pl.BlockSpec(memory_space=pltpu.VMEM)] * 4 + [order_spec(dep) for dep in deps],
        out_specs=pl.BlockSpec(memory_space=pltpu.VMEM),
        out_shape=jax.ShapeDtypeStruct((4, COLS, ROWS), BF),
        compiler_params=pltpu.CompilerParams(vmem_limit_bytes=SMALL),
        cost_estimate=NO_COST,
    )(*pieces, *deps)


def sum_kernel(core_ref, own_ref, oth_ref, got_own_ref, got_oth_ref, two_ref, got_two_ref, *outs):
    own = own_ref[...] + got_own_ref[...].astype(F32)
    oth = oth_ref[...] + got_oth_ref[...].astype(F32)
    two = two_ref[...] + got_two_ref[...].astype(F32)
    swap = core_ref[0] != 0
    keep1_ref, first1_ref, second1_ref, far1_ref, keep2_ref, first2_ref, second2_ref, far2_ref = outs
    keep1_ref[...] = own[0]
    first1_ref[...] = jnp.where(swap, oth[1], oth[0]).astype(BF)
    second1_ref[...] = jnp.where(swap, oth[0], oth[1]).astype(BF)
    far1_ref[...] = own[1].astype(BF)
    keep2_ref[...] = two[0]
    first2_ref[...] = two[1].astype(BF)
    second2_ref[...] = two[2].astype(BF)
    far2_ref[...] = two[3].astype(BF)


def heavy_sum(core, one, got1, two, got2):
    def spec(lead, shift):
        return pl.BlockSpec((lead, COLS, 128), lambda j, c: (0, 0, j + shift))

    kept = jax.ShapeDtypeStruct((COLS, ROWS), F32)
    give = jax.ShapeDtypeStruct((COLS, ROWS), BF)
    out = pl.pallas_call(
        sum_kernel,
        grid_spec=pltpu.PrefetchScalarGridSpec(
            num_scalar_prefetch=1,
            grid=(4,),
            in_specs=[spec(2, 0), spec(2, 4), spec(2, 0), spec(2, 4), spec(4, 0), spec(4, 0)],
            out_specs=[pl.BlockSpec((COLS, 128), lambda j, c: (0, j))] * 8,
        ),
        out_shape=[kept, give, give, give] * 2,
        compiler_params=pltpu.CompilerParams(vmem_limit_bytes=SMALL),
        cost_estimate=NO_COST,
    )(core, one, one, got1, got1, two, got2)
    return out[:4], out[4:]


def error_kernel(ids_ref, counts_ref, *refs):
    block = pl.program_id(0)
    scale = 1.0 / math.sqrt(4096)
    for k in range(2):
        recon = refs[4 * k][...]
        for got in refs[4 * k + 1 : 4 * k + 4]:
            recon = recon + got[...].astype(F32)
        live = jnp.where(block < counts_ref[k], 1.0, 0.0).astype(F32)
        refs[10 + k][...] = ((recon - refs[8 + k][0].astype(F32)) * live * scale).astype(BF)


def errors(ids, counts, one, two, targets):
    part = pl.BlockSpec((COLS, 128), lambda j, ids, counts: (0, j))
    out = jax.ShapeDtypeStruct((COLS, ROWS), BF)
    return pl.pallas_call(
        error_kernel,
        grid_spec=pltpu.PrefetchScalarGridSpec(
            num_scalar_prefetch=2,
            grid=(4,),
            in_specs=[part] * 8
            + [
                pl.BlockSpec((1, COLS, 128), lambda j, ids, counts: (ids[j], 0, 0)),
                pl.BlockSpec((1, COLS, 128), lambda j, ids, counts: (ids[4 + j], 0, 0)),
            ],
            out_specs=[part] * 2,
        ),
        out_shape=[out, out],
        compiler_params=pltpu.CompilerParams(vmem_limit_bytes=SMALL),
        cost_estimate=NO_COST,
    )(ids, counts, *one, *two, targets, targets)


def silu_kernel(part_ref, got_ref, live_ref, slope_ref, feat_ref):
    pre = part_ref[...] + got_ref[...].astype(F32)
    live = live_ref[...]
    slope_ref[...] = (activation_slope(pre) * live).astype(BF)
    feat_ref[...] = (jax.nn.silu(pre) * live).astype(BF)


def slope_kernel(part_ref, got_ref, slope_ref, *refs):
    out_ref, sum_ref = refs[-2:]
    grad = part_ref[...] + got_ref[...].astype(F32)
    grad = (grad * slope_ref[...].astype(F32)).astype(BF)
    out_ref[...] = grad
    sum_ref[...] = mm(jnp.ones((8, 2 * ROWS), BF), grad, 1, 1)


def with_other_core(kernel, part, got, extra, outs, with_sum=0, deps=()):
    tile = 128
    count = 2 * HALF // tile
    own = pl.BlockSpec((tile, 2 * ROWS), lambda i: (i, 0))
    swapped = pl.BlockSpec((tile, 2 * ROWS), lambda i: ((i + count // 2) % count, 0))
    return pl.pallas_call(
        kernel,
        grid=(count,),
        in_specs=[own, swapped]
        + [own if array.shape[0] > 1 else pl.BlockSpec((1, 2 * ROWS), lambda i: (0, 0)) for array in extra]
        + [order_spec(dep) for dep in deps],
        out_specs=[own] * len(outs) + [pl.BlockSpec((8, tile), lambda i: (0, i))] * with_sum,
        out_shape=[jax.ShapeDtypeStruct((2 * HALF, 2 * ROWS), kind) for kind in outs]
        + [jax.ShapeDtypeStruct((8, 2 * HALF), F32)] * with_sum,
        compiler_params=pltpu.CompilerParams(vmem_limit_bytes=SMALL),
        cost_estimate=NO_COST,
    )(part, got, *extra, *deps)


def term_views(terms):
    return [term.reshape((2, 4, COLS, 2 * HALF) if hi_first else (4, 2, COLS, 2 * HALF)) for term, hi_first in terms]


def term_specs(terms, place):
    def one(hi_first):
        def index(*args):
            hi, slot = place(*args)
            return (hi, slot, 0, 0) if hi_first else (slot, hi, 0, 0)

        return pl.BlockSpec((1, 1, COLS, 2 * HALF), index)

    return [one(hi_first) for _, hi_first in terms]


MORE = 16


def more_rows(sums):
    row = jnp.concatenate([ref[:, :HALF] for ref in sums], axis=1)
    return jnp.concatenate([row, row], axis=0)


def y_give(scalars, terms, deps=(), sums=()):
    count = len(terms)
    rows = COLS + (MORE if sums else 0)

    def kernel(s_ref, *refs):
        for k in range(count):
            refs[-1][0, k, 0, :COLS] = refs[k][0, 0]
        if sums:
            refs[-1][0, 0, 0, COLS:] = more_rows(refs[count : count + 2]).astype(BF)

    return pl.pallas_call(
        kernel,
        grid_spec=pltpu.PrefetchScalarGridSpec(
            num_scalar_prefetch=1,
            grid=(2, 2),
            in_specs=term_specs(terms, lambda i, hi, s: (hi, s[2 + i]))
            + [pl.BlockSpec((8, 2 * HALF), lambda i, hi, s: (0, 0))] * len(sums)
            + [order_spec(dep) for dep in deps],
            out_specs=pl.BlockSpec((1, count, 1, rows, 2 * HALF), lambda i, hi, s: (i, 0, hi, 0, 0)),
        ),
        out_shape=jax.ShapeDtypeStruct((2, count, 2, rows, 2 * HALF), BF),
        compiler_params=pltpu.CompilerParams(vmem_limit_bytes=SMALL),
        cost_estimate=NO_COST,
    )(scalars, *term_views(terms), *sums, *deps)


def y_near(scalars, terms, got, deps=(), sums=()):
    count = len(terms)
    rows = got.shape[3]

    def kernel(s_ref, *refs):
        got_ref = refs[2 * count]
        near_ref, keep_ref = refs[-2:]
        for k in range(count):
            first = refs[k][0, 0].astype(F32) + got_ref[1, k, 0, :COLS].astype(F32)
            near_ref[k, 0, :COLS] = first.astype(BF)
            keep = refs[count + k][0, 0].astype(F32) + got_ref[0, k, 0, :COLS].astype(F32)
            keep_ref[k, 0, :COLS] = keep.astype(BF)
        if sums:
            more = more_rows(refs[2 * count + 1 : 2 * count + 3])
            near_ref[0, 0, COLS:] = (more + got_ref[1, 0, 0, COLS:].astype(F32)).astype(BF)
            keep_ref[0, 0, COLS:] = (more + got_ref[0, 0, 0, COLS:].astype(F32)).astype(BF)

    out = pl.BlockSpec((count, 1, rows, 2 * HALF), lambda hi, s: (0, hi, 0, 0))
    shape = (count, 2, rows, 2 * HALF)
    return pl.pallas_call(
        kernel,
        grid_spec=pltpu.PrefetchScalarGridSpec(
            num_scalar_prefetch=1,
            grid=(2,),
            in_specs=term_specs(terms, lambda hi, s: (hi, s[1]))
            + term_specs(terms, lambda hi, s: (hi, s[0]))
            + [pl.BlockSpec((2, count, 1, rows, 2 * HALF), lambda hi, s: (0, 0, hi, 0, 0))]
            + [pl.BlockSpec((8, 2 * HALF), lambda hi, s: (0, 0))] * len(sums)
            + [order_spec(dep) for dep in deps],
            out_specs=[out, out],
        ),
        out_shape=[jax.ShapeDtypeStruct(shape, BF)] * 2,
        compiler_params=pltpu.CompilerParams(vmem_limit_bytes=SMALL),
        cost_estimate=NO_COST,
    )(scalars, *term_views(terms), *term_views(terms), got, *sums, *deps)


def y_quarters(scalars, keep, last, deps=()):
    count, _, rows, _ = keep.shape

    def kernel(s_ref, keep_ref, last_ref, *refs):
        outs = refs[len(deps) :]
        totals = [keep_ref[k, 0].astype(F32) + last_ref[k, 0].astype(F32) for k in range(count)]

        @pl.when(pl.program_id(0) == 0)
        def _():
            for k, total in enumerate(totals):
                outs[0][k] = total[:COLS, :HALF]
                outs[1][k] = total[:COLS, HALF:].astype(BF)
            if rows > COLS:
                outs[4][...] = totals[0][COLS:]

        @pl.when(pl.program_id(0) == 1)
        def _():
            for k, total in enumerate(totals):
                outs[2][k] = total[:COLS, :HALF].astype(BF)
                outs[3][k] = total[:COLS, HALF:].astype(BF)

    part = pl.BlockSpec((count, 1, rows, 2 * HALF), lambda i, s: (0, (i + s[4]) % 2, 0, 0))
    out = pl.BlockSpec((count, COLS, HALF), lambda i, s: (0, 0, 0))
    sent = jax.ShapeDtypeStruct((count, COLS, HALF), BF)
    more = rows - COLS
    same, core, mate, both, *sums = pl.pallas_call(
        kernel,
        grid_spec=pltpu.PrefetchScalarGridSpec(
            num_scalar_prefetch=1,
            grid=(2,),
            in_specs=[part, part] + [order_spec(dep) for dep in deps],
            out_specs=[out] * 4 + [pl.BlockSpec((MORE, 2 * HALF), lambda i, s: (0, 0))] * (more // MORE),
        ),
        out_shape=[jax.ShapeDtypeStruct((count, COLS, HALF), F32), sent, sent, sent]
        + [jax.ShapeDtypeStruct((MORE, 2 * HALF), F32)] * (more // MORE),
        compiler_params=pltpu.CompilerParams(vmem_limit_bytes=SMALL),
        cost_estimate=NO_COST,
    )(scalars, keep, last, *deps)
    return (same, to_other_core(core), to_mate(mate, 0), to_mate(both, 1)), sums


def write_out(place, groups, picks):
    def kernel(place_ref, *refs):
        core, x_lo = place_ref[0], place_ref[1]
        for n, (group, k) in enumerate(picks):
            same, from_core, from_mate, from_both = [ref[k].astype(F32) for ref in refs[4 * group : 4 * group + 4]]

            def side(own, mate):
                return jnp.where(
                    x_lo == 0, jnp.concatenate([own, mate], axis=1), jnp.concatenate([mate, own], axis=1)
                )

            refs[-1][n, pl.ds(pl.multiple_of(core * COLS, 8), COLS), :] = side(same, from_mate)
            refs[-1][n, pl.ds(pl.multiple_of((1 - core) * COLS, 8), COLS), :] = side(from_core, from_both)

    flat = [array for group in groups for array in group]
    return pl.pallas_call(
        kernel,
        in_specs=[pl.BlockSpec(memory_space=pltpu.SMEM)] + [pl.BlockSpec(memory_space=pltpu.VMEM)] * len(flat),
        out_specs=pl.BlockSpec(memory_space=pltpu.VMEM),
        out_shape=jax.ShapeDtypeStruct((len(picks), 2 * COLS, 2 * HALF), F32),
        compiler_params=pltpu.CompilerParams(vmem_limit_bytes=SMALL),
        cost_estimate=NO_COST,
    )(place, *flat)


def per_device(cache_in, cache_out, read_list, live_blocks, encoder, enc_bias, decoder):
    t = lax.axis_index("tok")
    l = lax.axis_index("layer")
    x_lo, y = t // 4, t % 4
    x_hi, z, core = l // 8, (l // 2) % 4, l % 2
    is_core0 = core == 0
    block_ids = read_list[0]

    def picked(cache):
        rows = cache.at[block_ids].get(mode="promise_in_bounds")
        return rows.reshape(2, ROWS, COLS).transpose(0, 2, 1)

    core_ref = core.reshape(1)

    def gather_both(one, two, steps=None):
        far1, far2 = exchange_far(one, "x"), exchange_far(two, "z")
        got2 = exchange(two, "z", 0), exchange(two, "z", 1), far2
        got1 = exchange(one, "x", 0), exchange(one, "x", 1), far1
        arrived = got2[0]
        block2 = pack_z((two,) + got2, got1)
        block1 = pack_x(core_ref, one, *got1, got2)
        got1, got2 = exchange(block1, "z", 0), exchange(block2, "x", 0)
        if steps is not None:
            steps.extend([arrived, block1, got2])
        more1 = [exchange(block1, "z", 1), exchange(got1, "z", 1)]
        more2 = [exchange(block2, "x", 1), exchange(got2, "x", 1)]
        near = jnp.where(is_core0, got2, more2[0])
        away = jnp.where(is_core0, more2[0], got2)

        def rows(*parts):
            return tuple(p.reshape(WIDE // 4, 2 * ROWS) for p in parts)

        return (
            rows(block1, got1, *more1),
            (
                jnp.concatenate([block2, near], axis=2).reshape(WIDE // 2, 2 * ROWS),
                jnp.concatenate([more2[1], away], axis=2).reshape(WIDE // 2, 2 * ROWS),
            ),
        )

    own_in = picked(cache_in)
    steps = []
    in0, in1 = gather_both(own_in[0], own_in[1], steps)
    where = jnp.stack([x_lo, x_hi, core, z]).astype(jnp.int32)
    enc_own, enc_give = ordered_weights(encoder, where, steps[0], False)
    dec_own, dec_give = ordered_weights(decoder, where, steps[1], True)
    enc_w = joined_weights(enc_own, to_other_core(enc_give), steps[2])
    dec_w = joined_weights(dec_own, to_other_core(dec_give), steps[2])
    live_other = to_mate(live_blocks, 0)
    row_blocks = jnp.arange(ROWS, dtype=jnp.int32) // 128
    own_live = (row_blocks[None, :] < live_blocks[0][:, None]).astype(F32)
    other_live = (row_blocks[None, :] < live_other[0][:, None]).astype(F32)
    live = jnp.concatenate([own_live, other_live], axis=1)[:, None, :]
    bias_half = lax.dynamic_slice(
        enc_bias, (jnp.int32(0), x_lo * HALF), (2, HALF), allow_negative_indices=False
    )
    bias_mine = jnp.concatenate([bias_half, jnp.zeros_like(bias_half)], axis=1)[:, :, None]

    inputs = (in0, in1)
    mid = WIDE // 2

    def over_width(mat, parts):
        size = WIDE // len(parts)
        total = mm(mat[:size], parts[0], 0, 0)
        for i in range(1, len(parts)):
            total = total + mm(mat[i * size : (i + 1) * size], parts[i], 0, 0)
        return total

    def encode(k):
        total = over_width(enc_w[k], inputs[k]) + bias_mine[k]
        other = to_other_core(total.astype(BF))
        return with_other_core(silu_kernel, total, other, (live[k],), (BF, BF))

    slopes, feats = zip(*[encode(k) for k in range(2)])

    low = mid // 2
    dec_hi = [dec_w[k].reshape(2, mid, 2 * HALF) for k in (1, 2)]

    def slot_term(k):
        return mm(dec_w[0][k * low : (k + 1) * low], feats[0], 1, 0)

    def quarter(hi, first):
        total = mm(at(dec_hi[0], hi), feats[0][:, first : first + ROWS], 1, 0)
        return total + mm(at(dec_hi[1], hi), feats[1][:, first : first + ROWS], 1, 0)

    got = [
        exchange(slot_term(3).astype(BF), "z", 1),
        exchange(quarter(1, 0).astype(BF), "x", 1),
        exchange(slot_term(2).astype(BF), "z", 1),
        exchange(quarter(1 - core, ROWS).astype(BF), "x", 1),
    ]
    give1 = (slot_term(1) + got[0].astype(F32)).astype(BF)
    give2 = (quarter(core, ROWS) + got[1].astype(F32)).astype(BF)
    block1 = (slot_term(0) + got[2].astype(F32)).reshape(2, COLS, 2 * ROWS)
    block2 = (quarter(0, 0) + got[3].astype(F32)).reshape(4, COLS, ROWS)
    got1, got2 = exchange(give1, "z", 0), exchange(give2, "x", 0)
    one, two = heavy_sum(
        core_ref, block1, got1.reshape(2, COLS, 2 * ROWS), block2, got2.reshape(4, COLS, ROWS)
    )
    far1, far2 = exchange_far(one[3], "x"), exchange_far(two[3], "z")
    got2 = exchange(two[1], "z", 0), exchange(two[2], "z", 1), far2
    got1 = exchange(one[1], "x", 0), exchange(one[2], "x", 1), far1
    own_err = errors(
        block_ids, live_blocks[0], (one[0],) + got1, (two[0],) + got2, cache_out.transpose(0, 2, 1)
    )

    err0, err1 = gather_both(*own_err)

    err0, err1 = jnp.concatenate(err0), jnp.concatenate(err1)

    def width_grad(whole, other, hi_first):
        return mm(whole, other, 1, 1).astype(BF), hi_first

    m_first = jnp.where(is_core0, 1, 3)
    m_second = jnp.where(is_core0, 3, 1)
    scalars = jnp.stack([slot_of(z ^ y ^ m, core) for m in (0, m_first, m_second, 2)] + [x_lo ^ x_hi])
    scalars = scalars.astype(jnp.int32)
    place = jnp.stack([core, x_lo]).astype(jnp.int32)

    def backward(k, total, deps=()):
        other = to_other_core(total.astype(BF))
        return with_other_core(slope_kernel, total, other, (slopes[k],), (BF,), 1, deps)

    terms_a = [width_grad(err1, feats[0], True), width_grad(err1, feats[1], True)]
    give_a = y_give(scalars, terms_a)
    got_a = exchange(give_a, "y", 1)
    gpre1, sum1 = backward(1, mm(pass_on(dec_w, 2, 1, give_a)[0], err1, 0, 0))
    terms_b = [width_grad(err0, feats[0], False), width_grad(jnp.concatenate(in1), gpre1, True)]
    give_b = y_give(scalars, terms_b)
    got_b = exchange(give_b, "y", 1)
    near_a, keep_a = y_near(scalars, terms_a, got_a, (give_b,))
    last_a = exchange(near_a, "y", 0)
    back_w = pass_on(dec_w, 0, 2, give_b)
    gpre0, sum0 = backward(0, mm(back_w[1], err1, 0, 0) + mm(back_w[0], err0, 0, 0), (near_a,))
    terms_c = [width_grad(jnp.concatenate(in0), gpre0, False)]
    give_c = y_give(scalars, terms_c, (), (sum0, sum1))
    got_c = exchange(give_c, "y", 1)

    near_b, keep_b = y_near(scalars, terms_b, got_b, (give_c,))
    last_b = exchange(near_b, "y", 0)
    done_a, _ = y_quarters(scalars, keep_a, last_a, (near_b,))
    near_c, keep_c = y_near(scalars, terms_c, got_c, (done_a[0],), (sum0, sum1))
    last_c = exchange(near_c, "y", 0)
    done_b, _ = y_quarters(scalars, keep_b, last_b, (near_c,) + done_a[1:])
    done_c, sums = y_quarters(scalars, keep_c, last_c, (done_b[0],))
    bias_out = at(sums[0][0].reshape(2, 4, 64), y, 1)
    dec_out = write_out(place, (done_a, done_b), ((1, 0), (0, 0), (0, 1))).transpose(0, 2, 1)
    enc_out = write_out(place, (done_b, done_c), ((1, 0), (0, 1)))
    return (enc_out, bias_out[:, None, :], dec_out)


def solution(mesh):
    return jax.shard_map(
        per_device,
        mesh=mesh,
        in_specs=(
            P("tok", None, "layer"),
            P("tok", None, "layer"),
            P("tok", None),
            P("tok", None),
            P(None, None, "layer"),
            P(None, "layer"),
            P(None, "layer", None),
        ),
        out_specs=(P(None, "tok", "layer"), P(None, "layer", "tok"), P(None, "layer", "tok")),
        check_vma=False,
    )
```

```python
import functools
import math

import jax
import jax.numpy as jnp
from jax import lax
from jax.experimental import pallas as pl
from jax.experimental.pallas import tpu as pltpu
from jax.sharding import PartitionSpec as P

AXES = ("tok", "layer")
BF = jnp.bfloat16
F32 = jnp.float32
ROWS = 512
COLS = 144
HALF = 256
WIDE = 8 * COLS
SMALL = 8 * 1024 * 1024
NO_COST = pl.CostEstimate(flops=0, bytes_accessed=0, transcendentals=0)


def device_index(x, y, z, c):
    return ((x % 2) * 4 + y) * 16 + (x // 2) * 8 + z * 2 + c


def pairs_of(partner):
    out = []
    for x in range(4):
        for y in range(4):
            for z in range(4):
                for c in range(2):
                    out.append((device_index(x, y, z, c), device_index(*partner(x, y, z, c))))
    return out


def mask(step, c):
    return 1 if (step + c) % 2 == 0 else 3


def exchange(value, axis, step):
    def partner(x, y, z, c):
        m = mask(step, c)
        return {"x": (x ^ m, y, z, c), "y": (x, y ^ m, z, c), "z": (x, y, z ^ m, c)}[axis]

    return lax.ppermute(value, AXES, pairs_of(partner))


def exchange_far(value, axis):
    def partner(x, y, z, c):
        return {"x": (x ^ 2, y, z, c), "z": (x, y, z ^ 2, c)}[axis]

    return lax.ppermute(value, AXES, pairs_of(partner))


def to_other_core(value):
    return lax.ppermute(value, AXES, pairs_of(lambda x, y, z, c: (x, y, z, 1 - c)))


def to_mate(value, flip):
    return lax.ppermute(value, AXES, pairs_of(lambda x, y, z, c: (x ^ 1, y, z, c ^ flip)))


def activation_slope(pre_act):
    sigma = jax.nn.sigmoid(pre_act)
    return sigma + pre_act * sigma * (1.0 - sigma)


def mm(a, b, ca, cb):
    return lax.dot_general(a, b, (((ca,), (cb,)), ((), ())), preferred_element_type=F32)


def at(array, index, dim=0):
    starts = [jnp.int32(0)] * array.ndim
    starts[dim] = index
    sizes = list(array.shape)
    sizes[dim] = 1
    piece = lax.dynamic_slice(array, starts, sizes, allow_negative_indices=False)
    return piece.reshape(array.shape[:dim] + array.shape[dim + 1 :])


def slot_of(apart, core):
    on_core0 = apart ^ (apart >> 1)
    on_core1 = (on_core0 & 1) * 2 + (on_core0 >> 1)
    return jnp.where(core == 0, on_core0, on_core1)


def order_spec(array):
    tile = (min(16, array.shape[-2]), min(128, array.shape[-1]))
    return pl.BlockSpec((1,) * (array.ndim - 2) + tile, lambda *args: (0,) * array.ndim)


def order_kernel(turn, where_ref, w_ref, dep_ref, own_ref, give_ref):
    block = w_ref[0].T if turn else w_ref[0]
    core = where_ref[2]
    for zz in range(4):
        even = block[2 * zz * COLS : (2 * zz + 1) * COLS]
        odd = block[(2 * zz + 1) * COLS : (2 * zz + 2) * COLS]
        apart = zz ^ where_ref[3]
        own_ref[0, 0, slot_of(apart, core)] = jnp.where(core == 0, even, odd)
        give_ref[0, 0, slot_of(apart, 1 - core)] = jnp.where(core == 0, odd, even)


def ordered_weights(weights, where, dep, turn):
    count = weights.shape[0]
    if turn:
        in_spec = pl.BlockSpec((1, HALF, WIDE), lambda i, h, s: (i, s[0], h))
    else:
        in_spec = pl.BlockSpec((1, WIDE, HALF), lambda i, h, s: (i, h, s[0]))
    out_spec = pl.BlockSpec((1, 1, 4, COLS, HALF), lambda i, h, s: (i, (h + s[1]) % 2, 0, 0, 0))
    shape = jax.ShapeDtypeStruct((count, 2, 4, COLS, HALF), BF)
    return pl.pallas_call(
        functools.partial(order_kernel, turn),
        grid_spec=pltpu.PrefetchScalarGridSpec(
            num_scalar_prefetch=1,
            grid=(count, 2),
            in_specs=[in_spec, order_spec(dep)],
            out_specs=[out_spec, out_spec],
        ),
        out_shape=[shape, shape],
        compiler_params=pltpu.CompilerParams(vmem_limit_bytes=SMALL),
        cost_estimate=NO_COST,
    )(where, weights, dep)


def join_kernel(own_ref, got_ref, dep_ref, out_ref):
    first = pl.program_id(0) == 0
    for hi in range(2):
        for slot in range(4):
            chunk = jnp.where(first, slot * 2 + hi, hi * 4 + slot)
            out_ref[0, chunk, :, :HALF] = own_ref[0, hi, slot]
            out_ref[0, chunk, :, HALF:] = got_ref[0, hi, slot]


def joined_weights(own, got, dep):
    count = own.shape[0]
    in_spec = pl.BlockSpec((1, 2, 4, COLS, HALF), lambda i: (i, 0, 0, 0, 0))
    out = pl.pallas_call(
        join_kernel,
        grid=(count,),
        in_specs=[in_spec, in_spec, order_spec(dep)],
        out_specs=pl.BlockSpec((1, 8, COLS, 2 * HALF), lambda i: (i, 0, 0, 0)),
        out_shape=jax.ShapeDtypeStruct((count, 8, COLS, 2 * HALF), BF),
        compiler_params=pltpu.CompilerParams(vmem_limit_bytes=12 * 1024 * 1024),
        cost_estimate=NO_COST,
    )(own, got, dep)
    return out.reshape(count, WIDE, 2 * HALF)


def pass_on(value, first, count, *deps):
    def kernel(value_ref, *refs):
        refs[-1][...] = value_ref[...]

    block = (1,) + value.shape[1:]
    return pl.pallas_call(
        kernel,
        grid=(count,),
        in_specs=[pl.BlockSpec(block, lambda i: (first + i,) + (0,) * (value.ndim - 1))]
        + [order_spec(dep) for dep in deps],
        out_specs=pl.BlockSpec(block, lambda i: (i,) + (0,) * (value.ndim - 1)),
        out_shape=jax.ShapeDtypeStruct((count,) + value.shape[1:], value.dtype),
        compiler_params=pltpu.CompilerParams(vmem_limit_bytes=SMALL),
        cost_estimate=NO_COST,
    )(value, *deps)


def pack_x(core, own, first, second, far, deps):
    def kernel(core_ref, own_ref, first_ref, second_ref, far_ref, *rest):
        out_ref = rest[-1]
        swap = core_ref[0] != 0
        out_ref[0, :, :ROWS] = own_ref[...]
        out_ref[1, :, :ROWS] = far_ref[...]
        out_ref[0, :, ROWS:] = jnp.where(swap, second_ref[...], first_ref[...])
        out_ref[1, :, ROWS:] = jnp.where(swap, first_ref[...], second_ref[...])

    return pl.pallas_call(
        kernel,
        grid=(1,),
        in_specs=[pl.BlockSpec(memory_space=pltpu.SMEM)]
        + [pl.BlockSpec(memory_space=pltpu.VMEM)] * 4
        + [order_spec(dep) for dep in deps],
        out_specs=pl.BlockSpec(memory_space=pltpu.VMEM),
        out_shape=jax.ShapeDtypeStruct((2, COLS, 2 * ROWS), BF),
        compiler_params=pltpu.CompilerParams(vmem_limit_bytes=SMALL),
        cost_estimate=NO_COST,
    )(core, own, first, second, far, *deps)


def pack_z(pieces, deps):
    def kernel(*refs):
        for k in range(4):
            refs[-1][k] = refs[k][...]

    return pl.pallas_call(
        kernel,
        grid=(1,),
        in_specs=[pl.BlockSpec(memory_space=pltpu.VMEM)] * 4 + [order_spec(dep) for dep in deps],
        out_specs=pl.BlockSpec(memory_space=pltpu.VMEM),
        out_shape=jax.ShapeDtypeStruct((4, COLS, ROWS), BF),
        compiler_params=pltpu.CompilerParams(vmem_limit_bytes=SMALL),
        cost_estimate=NO_COST,
    )(*pieces, *deps)


def sum_kernel(core_ref, own_ref, oth_ref, got_own_ref, got_oth_ref, two_ref, got_two_ref, *outs):
    own = own_ref[...] + got_own_ref[...].astype(F32)
    oth = oth_ref[...] + got_oth_ref[...].astype(F32)
    two = two_ref[...] + got_two_ref[...].astype(F32)
    swap = core_ref[0] != 0
    keep1_ref, first1_ref, second1_ref, far1_ref, keep2_ref, first2_ref, second2_ref, far2_ref = outs
    keep1_ref[...] = own[0]
    first1_ref[...] = jnp.where(swap, oth[1], oth[0]).astype(BF)
    second1_ref[...] = jnp.where(swap, oth[0], oth[1]).astype(BF)
    far1_ref[...] = own[1].astype(BF)
    keep2_ref[...] = two[0]
    first2_ref[...] = two[1].astype(BF)
    second2_ref[...] = two[2].astype(BF)
    far2_ref[...] = two[3].astype(BF)


def heavy_sum(core, one, got1, two, got2):
    def spec(lead, shift):
        return pl.BlockSpec((lead, COLS, 128), lambda j, c: (0, 0, j + shift))

    kept = jax.ShapeDtypeStruct((COLS, ROWS), F32)
    give = jax.ShapeDtypeStruct((COLS, ROWS), BF)
    out = pl.pallas_call(
        sum_kernel,
        grid_spec=pltpu.PrefetchScalarGridSpec(
            num_scalar_prefetch=1,
            grid=(4,),
            in_specs=[spec(2, 0), spec(2, 4), spec(2, 0), spec(2, 4), spec(4, 0), spec(4, 0)],
            out_specs=[pl.BlockSpec((COLS, 128), lambda j, c: (0, j))] * 8,
        ),
        out_shape=[kept, give, give, give] * 2,
        compiler_params=pltpu.CompilerParams(vmem_limit_bytes=SMALL),
        cost_estimate=NO_COST,
    )(core, one, one, got1, got1, two, got2)
    return out[:4], out[4:]


def error_kernel(ids_ref, counts_ref, *refs):
    block = pl.program_id(0)
    scale = 1.0 / math.sqrt(4096)
    for k in range(2):
        recon = refs[4 * k][...]
        for got in refs[4 * k + 1 : 4 * k + 4]:
            recon = recon + got[...].astype(F32)
        live = jnp.where(block < counts_ref[k], 1.0, 0.0).astype(F32)
        refs[10 + k][...] = ((recon - refs[8 + k][0].astype(F32)) * live * scale).astype(BF)


def errors(ids, counts, one, two, targets):
    part = pl.BlockSpec((COLS, 128), lambda j, ids, counts: (0, j))
    out = jax.ShapeDtypeStruct((COLS, ROWS), BF)
    return pl.pallas_call(
        error_kernel,
        grid_spec=pltpu.PrefetchScalarGridSpec(
            num_scalar_prefetch=2,
            grid=(4,),
            in_specs=[part] * 8
            + [
                pl.BlockSpec((1, COLS, 128), lambda j, ids, counts: (ids[j], 0, 0)),
                pl.BlockSpec((1, COLS, 128), lambda j, ids, counts: (ids[4 + j], 0, 0)),
            ],
            out_specs=[part] * 2,
        ),
        out_shape=[out, out],
        compiler_params=pltpu.CompilerParams(vmem_limit_bytes=SMALL),
        cost_estimate=NO_COST,
    )(ids, counts, *one, *two, targets, targets)


def silu_kernel(part_ref, got_ref, live_ref, slope_ref, feat_ref):
    pre = part_ref[...] + got_ref[...].astype(F32)
    live = live_ref[...]
    slope_ref[...] = (activation_slope(pre) * live).astype(BF)
    feat_ref[...] = (jax.nn.silu(pre) * live).astype(BF)


def slope_kernel(part_ref, got_ref, slope_ref, *refs):
    out_ref, sum_ref = refs[-2:]
    grad = part_ref[...] + got_ref[...].astype(F32)
    grad = (grad * slope_ref[...].astype(F32)).astype(BF)
    out_ref[...] = grad
    sum_ref[...] = mm(jnp.ones((8, 2 * ROWS), BF), grad, 1, 1)


def with_other_core(kernel, part, got, extra, outs, with_sum=0, deps=()):
    tile = 128
    count = 2 * HALF // tile
    own = pl.BlockSpec((tile, 2 * ROWS), lambda i: (i, 0))
    swapped = pl.BlockSpec((tile, 2 * ROWS), lambda i: ((i + count // 2) % count, 0))
    return pl.pallas_call(
        kernel,
        grid=(count,),
        in_specs=[own, swapped]
        + [own if array.shape[0] > 1 else pl.BlockSpec((1, 2 * ROWS), lambda i: (0, 0)) for array in extra]
        + [order_spec(dep) for dep in deps],
        out_specs=[own] * len(outs) + [pl.BlockSpec((8, tile), lambda i: (0, i))] * with_sum,
        out_shape=[jax.ShapeDtypeStruct((2 * HALF, 2 * ROWS), kind) for kind in outs]
        + [jax.ShapeDtypeStruct((8, 2 * HALF), F32)] * with_sum,
        compiler_params=pltpu.CompilerParams(vmem_limit_bytes=SMALL),
        cost_estimate=NO_COST,
    )(part, got, *extra, *deps)


def term_views(terms):
    return [term.reshape((2, 4, COLS, 2 * HALF) if hi_first else (4, 2, COLS, 2 * HALF)) for term, hi_first in terms]


def term_specs(terms, place):
    def one(hi_first):
        def index(*args):
            hi, slot = place(*args)
            return (hi, slot, 0, 0) if hi_first else (slot, hi, 0, 0)

        return pl.BlockSpec((1, 1, COLS, 2 * HALF), index)

    return [one(hi_first) for _, hi_first in terms]


MORE = 16


def more_rows(sums):
    row = jnp.concatenate([ref[:, :HALF] for ref in sums], axis=1)
    return jnp.concatenate([row, row], axis=0)


def y_give(scalars, terms, deps=(), sums=()):
    count = len(terms)
    rows = COLS + (MORE if sums else 0)

    def kernel(s_ref, *refs):
        for k in range(count):
            refs[-1][0, k, 0, :COLS] = refs[k][0, 0]
        if sums:
            refs[-1][0, 0, 0, COLS:] = more_rows(refs[count : count + 2]).astype(BF)

    return pl.pallas_call(
        kernel,
        grid_spec=pltpu.PrefetchScalarGridSpec(
            num_scalar_prefetch=1,
            grid=(2, 2),
            in_specs=term_specs(terms, lambda i, hi, s: (hi, s[2 + i]))
            + [pl.BlockSpec((8, 2 * HALF), lambda i, hi, s: (0, 0))] * len(sums)
            + [order_spec(dep) for dep in deps],
            out_specs=pl.BlockSpec((1, count, 1, rows, 2 * HALF), lambda i, hi, s: (i, 0, hi, 0, 0)),
        ),
        out_shape=jax.ShapeDtypeStruct((2, count, 2, rows, 2 * HALF), BF),
        compiler_params=pltpu.CompilerParams(vmem_limit_bytes=SMALL),
        cost_estimate=NO_COST,
    )(scalars, *term_views(terms), *sums, *deps)


def y_near(scalars, terms, got, deps=(), sums=()):
    count = len(terms)
    rows = got.shape[3]

    def kernel(s_ref, *refs):
        got_ref = refs[2 * count]
        near_ref, keep_ref = refs[-2:]
        for k in range(count):
            first = refs[k][0, 0].astype(F32) + got_ref[1, k, 0, :COLS].astype(F32)
            near_ref[k, 0, :COLS] = first.astype(BF)
            keep = refs[count + k][0, 0].astype(F32) + got_ref[0, k, 0, :COLS].astype(F32)
            keep_ref[k, 0, :COLS] = keep.astype(BF)
        if sums:
            more = more_rows(refs[2 * count + 1 : 2 * count + 3])
            near_ref[0, 0, COLS:] = (more + got_ref[1, 0, 0, COLS:].astype(F32)).astype(BF)
            keep_ref[0, 0, COLS:] = (more + got_ref[0, 0, 0, COLS:].astype(F32)).astype(BF)

    out = pl.BlockSpec((count, 1, rows, 2 * HALF), lambda hi, s: (0, hi, 0, 0))
    shape = (count, 2, rows, 2 * HALF)
    return pl.pallas_call(
        kernel,
        grid_spec=pltpu.PrefetchScalarGridSpec(
            num_scalar_prefetch=1,
            grid=(2,),
            in_specs=term_specs(terms, lambda hi, s: (hi, s[1]))
            + term_specs(terms, lambda hi, s: (hi, s[0]))
            + [pl.BlockSpec((2, count, 1, rows, 2 * HALF), lambda hi, s: (0, 0, hi, 0, 0))]
            + [pl.BlockSpec((8, 2 * HALF), lambda hi, s: (0, 0))] * len(sums)
            + [order_spec(dep) for dep in deps],
            out_specs=[out, out],
        ),
        out_shape=[jax.ShapeDtypeStruct(shape, BF)] * 2,
        compiler_params=pltpu.CompilerParams(vmem_limit_bytes=SMALL),
        cost_estimate=NO_COST,
    )(scalars, *term_views(terms), *term_views(terms), got, *sums, *deps)


def y_quarters(scalars, keep, last, deps=()):
    count, _, rows, _ = keep.shape

    def kernel(s_ref, keep_ref, last_ref, *refs):
        outs = refs[len(deps) :]
        totals = [keep_ref[k, 0].astype(F32) + last_ref[k, 0].astype(F32) for k in range(count)]

        @pl.when(pl.program_id(0) == 0)
        def _():
            for k, total in enumerate(totals):
                outs[0][k] = total[:COLS, :HALF]
                outs[1][k] = total[:COLS, HALF:].astype(BF)
            if rows > COLS:
                outs[4][...] = totals[0][COLS:]

        @pl.when(pl.program_id(0) == 1)
        def _():
            for k, total in enumerate(totals):
                outs[2][k] = total[:COLS, :HALF].astype(BF)
                outs[3][k] = total[:COLS, HALF:].astype(BF)

    part = pl.BlockSpec((count, 1, rows, 2 * HALF), lambda i, s: (0, (i + s[4]) % 2, 0, 0))
    out = pl.BlockSpec((count, COLS, HALF), lambda i, s: (0, 0, 0))
    sent = jax.ShapeDtypeStruct((count, COLS, HALF), BF)
    more = rows - COLS
    same, core, mate, both, *sums = pl.pallas_call(
        kernel,
        grid_spec=pltpu.PrefetchScalarGridSpec(
            num_scalar_prefetch=1,
            grid=(2,),
            in_specs=[part, part] + [order_spec(dep) for dep in deps],
            out_specs=[out] * 4 + [pl.BlockSpec((MORE, 2 * HALF), lambda i, s: (0, 0))] * (more // MORE),
        ),
        out_shape=[jax.ShapeDtypeStruct((count, COLS, HALF), F32), sent, sent, sent]
        + [jax.ShapeDtypeStruct((MORE, 2 * HALF), F32)] * (more // MORE),
        compiler_params=pltpu.CompilerParams(vmem_limit_bytes=SMALL),
        cost_estimate=NO_COST,
    )(scalars, keep, last, *deps)
    return (same, to_other_core(core), to_mate(mate, 0), to_mate(both, 1)), sums


def write_out(place, groups, picks, deps=()):
    def kernel(place_ref, *refs):
        core, x_lo = place_ref[0], place_ref[1]
        for n, (group, k) in enumerate(picks):
            same, from_core, from_mate, from_both = [ref[k].astype(F32) for ref in refs[4 * group : 4 * group + 4]]

            def side(own, mate):
                return jnp.where(
                    x_lo == 0, jnp.concatenate([own, mate], axis=1), jnp.concatenate([mate, own], axis=1)
                )

            refs[-1][n, pl.ds(pl.multiple_of(core * COLS, 8), COLS), :] = side(same, from_mate)
            refs[-1][n, pl.ds(pl.multiple_of((1 - core) * COLS, 8), COLS), :] = side(from_core, from_both)

    flat = [array for group in groups for array in group]
    return pl.pallas_call(
        kernel,
        in_specs=[pl.BlockSpec(memory_space=pltpu.SMEM)] + [pl.BlockSpec(memory_space=pltpu.VMEM)] * len(flat + list(deps)),
        out_specs=pl.BlockSpec(memory_space=pltpu.VMEM),
        out_shape=jax.ShapeDtypeStruct((len(picks), 2 * COLS, 2 * HALF), F32),
        compiler_params=pltpu.CompilerParams(vmem_limit_bytes=SMALL),
        cost_estimate=NO_COST,
    )(place, *flat, *deps)


def per_device(cache_in, cache_out, read_list, live_blocks, encoder, enc_bias, decoder):
    t = lax.axis_index("tok")
    l = lax.axis_index("layer")
    x_lo, y = t // 4, t % 4
    x_hi, z, core = l // 8, (l // 2) % 4, l % 2
    is_core0 = core == 0
    block_ids = read_list[0]

    def picked(cache):
        rows = cache.at[block_ids].get(mode="promise_in_bounds")
        return rows.reshape(2, ROWS, COLS).transpose(0, 2, 1)

    core_ref = core.reshape(1)

    def gather_both(one, two, steps=None):
        far1, far2 = exchange_far(one, "x"), exchange_far(two, "z")
        got2 = exchange(two, "z", 0), exchange(two, "z", 1), far2
        got1 = exchange(one, "x", 0), exchange(one, "x", 1), far1
        arrived = got2[0]
        block2 = pack_z((two,) + got2, got1)
        block1 = pack_x(core_ref, one, *got1, got2)
        got1, got2 = exchange(block1, "z", 0), exchange(block2, "x", 0)
        if steps is not None:
            steps.extend([arrived, block1, got2])
        more1 = [exchange(block1, "z", 1), exchange(got1, "z", 1)]
        more2 = [exchange(block2, "x", 1), exchange(got2, "x", 1)]
        near = jnp.where(is_core0, got2, more2[0])
        away = jnp.where(is_core0, more2[0], got2)

        def rows(*parts):
            return tuple(p.reshape(WIDE // 4, 2 * ROWS) for p in parts)

        return (
            rows(block1, got1, *more1),
            (
                jnp.concatenate([block2, near], axis=2).reshape(WIDE // 2, 2 * ROWS),
                jnp.concatenate([more2[1], away], axis=2).reshape(WIDE // 2, 2 * ROWS),
            ),
        )

    own_in = picked(cache_in)
    steps = []
    in0, in1 = gather_both(own_in[0], own_in[1], steps)
    where = jnp.stack([x_lo, x_hi, core, z]).astype(jnp.int32)
    enc_own, enc_give = ordered_weights(encoder, where, steps[0], False)
    dec_own, dec_give = ordered_weights(decoder, where, steps[1], True)
    enc_w = joined_weights(enc_own, to_other_core(enc_give), steps[2])
    dec_w = joined_weights(dec_own, to_other_core(dec_give), steps[2])
    live_other = to_mate(live_blocks, 0)
    row_blocks = jnp.arange(ROWS, dtype=jnp.int32) // 128
    own_live = (row_blocks[None, :] < live_blocks[0][:, None]).astype(F32)
    other_live = (row_blocks[None, :] < live_other[0][:, None]).astype(F32)
    live = jnp.concatenate([own_live, other_live], axis=1)[:, None, :]
    bias_half = lax.dynamic_slice(
        enc_bias, (jnp.int32(0), x_lo * HALF), (2, HALF), allow_negative_indices=False
    )
    bias_mine = jnp.concatenate([bias_half, jnp.zeros_like(bias_half)], axis=1)[:, :, None]

    inputs = (in0, in1)
    mid = WIDE // 2

    def over_width(mat, parts):
        size = WIDE // len(parts)
        total = mm(mat[:size], parts[0], 0, 0)
        for i in range(1, len(parts)):
            total = total + mm(mat[i * size : (i + 1) * size], parts[i], 0, 0)
        return total

    def encode(k):
        total = over_width(enc_w[k], inputs[k]) + bias_mine[k]
        other = to_other_core(total.astype(BF))
        return with_other_core(silu_kernel, total, other, (live[k],), (BF, BF))

    slopes, feats = zip(*[encode(k) for k in range(2)])

    low = mid // 2
    dec_hi = [dec_w[k].reshape(2, mid, 2 * HALF) for k in (1, 2)]

    def slot_term(k):
        return mm(dec_w[0][k * low : (k + 1) * low], feats[0], 1, 0)

    def quarter(hi, first):
        total = mm(at(dec_hi[0], hi), feats[0][:, first : first + ROWS], 1, 0)
        return total + mm(at(dec_hi[1], hi), feats[1][:, first : first + ROWS], 1, 0)

    got = [
        exchange(slot_term(3).astype(BF), "z", 1),
        exchange(quarter(1, 0).astype(BF), "x", 1),
        exchange(slot_term(2).astype(BF), "z", 1),
        exchange(quarter(1 - core, ROWS).astype(BF), "x", 1),
    ]
    give1 = (slot_term(1) + got[0].astype(F32)).astype(BF)
    give2 = (quarter(core, ROWS) + got[1].astype(F32)).astype(BF)
    block1 = (slot_term(0) + got[2].astype(F32)).reshape(2, COLS, 2 * ROWS)
    block2 = (quarter(0, 0) + got[3].astype(F32)).reshape(4, COLS, ROWS)
    got1, got2 = exchange(give1, "z", 0), exchange(give2, "x", 0)
    one, two = heavy_sum(
        core_ref, block1, got1.reshape(2, COLS, 2 * ROWS), block2, got2.reshape(4, COLS, ROWS)
    )
    far1, far2 = exchange_far(one[3], "x"), exchange_far(two[3], "z")
    got2 = exchange(two[1], "z", 0), exchange(two[2], "z", 1), far2
    got1 = exchange(one[1], "x", 0), exchange(one[2], "x", 1), far1
    own_err = errors(
        block_ids, live_blocks[0], (one[0],) + got1, (two[0],) + got2, cache_out.transpose(0, 2, 1)
    )

    err0, err1 = gather_both(*own_err)

    err0, err1 = jnp.concatenate(err0), jnp.concatenate(err1)

    def width_grad(whole, other, hi_first):
        return mm(whole, other, 1, 1).astype(BF), hi_first

    m_first = jnp.where(is_core0, 1, 3)
    m_second = jnp.where(is_core0, 3, 1)
    scalars = jnp.stack([slot_of(z ^ y ^ m, core) for m in (0, m_first, m_second, 2)] + [x_lo ^ x_hi])
    scalars = scalars.astype(jnp.int32)
    place = jnp.stack([core, x_lo]).astype(jnp.int32)

    def backward(k, total, deps=()):
        other = to_other_core(total.astype(BF))
        return with_other_core(slope_kernel, total, other, (slopes[k],), (BF,), 1, deps)

    terms_a = [width_grad(err1, feats[0], True), width_grad(err1, feats[1], True)]
    give_a = y_give(scalars, terms_a)
    got_a = exchange(give_a, "y", 1)
    gpre1, sum1 = backward(1, mm(pass_on(dec_w, 2, 1, give_a)[0], err1, 0, 0))
    terms_b = [width_grad(err0, feats[0], False), width_grad(jnp.concatenate(in1), gpre1, True)]
    give_b = y_give(scalars, terms_b)
    got_b = exchange(give_b, "y", 1)
    near_a, keep_a = y_near(scalars, terms_a, got_a, (give_b,))
    last_a = exchange(near_a, "y", 0)
    back_w = pass_on(dec_w, 0, 2, give_b)
    gpre0, sum0 = backward(0, mm(back_w[1], err1, 0, 0) + mm(back_w[0], err0, 0, 0), (near_a,))
    terms_c = [width_grad(jnp.concatenate(in0), gpre0, False)]
    give_c = y_give(scalars, terms_c, (), (sum0, sum1))
    got_c = exchange(give_c, "y", 1)

    near_b, keep_b = y_near(scalars, terms_b, got_b, (give_c,))
    last_b = exchange(near_b, "y", 0)
    done_a, _ = y_quarters(scalars, keep_a, last_a, (near_b,))
    near_c, keep_c = y_near(scalars, terms_c, got_c, done_a, (sum0, sum1))
    last_c = exchange(near_c, "y", 0)
    done_b, _ = y_quarters(scalars, keep_b, last_b, (near_c,))
    done_c, sums = y_quarters(scalars, keep_c, last_c, done_b)
    bias_out = at(sums[0][0].reshape(2, 4, 64), y, 1)
    dec_out = write_out(place, (done_a, done_b), ((1, 0), (0, 0), (0, 1)), done_c[:1]).transpose(0, 2, 1)
    enc_out = write_out(place, (done_b, done_c), ((1, 0), (0, 1)))
    return (enc_out, bias_out[:, None, :], dec_out)


def solution(mesh):
    return jax.shard_map(
        per_device,
        mesh=mesh,
        in_specs=(
            P("tok", None, "layer"),
            P("tok", None, "layer"),
            P("tok", None),
            P("tok", None),
            P(None, None, "layer"),
            P(None, "layer"),
            P(None, "layer", None),
        ),
        out_specs=(P(None, "tok", "layer"), P(None, "layer", "tok"), P(None, "layer", "tok")),
        check_vma=False,
    )
```

```python
import functools
import math

import jax
import jax.numpy as jnp
from jax import lax
from jax.experimental import pallas as pl
from jax.experimental.pallas import tpu as pltpu
from jax.sharding import PartitionSpec as P

AXES = ("tok", "layer")
BF = jnp.bfloat16
F32 = jnp.float32
ROWS = 512
COLS = 144
HALF = 256
WIDE = 8 * COLS
SMALL = 8 * 1024 * 1024
NO_COST = pl.CostEstimate(flops=0, bytes_accessed=0, transcendentals=0)


def device_index(x, y, z, c):
    return ((x % 2) * 4 + y) * 16 + (x // 2) * 8 + z * 2 + c


def pairs_of(partner):
    out = []
    for x in range(4):
        for y in range(4):
            for z in range(4):
                for c in range(2):
                    out.append((device_index(x, y, z, c), device_index(*partner(x, y, z, c))))
    return out


def mask(step, c):
    return 1 if (step + c) % 2 == 0 else 3


def exchange(value, axis, step):
    def partner(x, y, z, c):
        m = mask(step, c)
        return {"x": (x ^ m, y, z, c), "y": (x, y ^ m, z, c), "z": (x, y, z ^ m, c)}[axis]

    return lax.ppermute(value, AXES, pairs_of(partner))


def exchange_far(value, axis):
    def partner(x, y, z, c):
        return {"x": (x ^ 2, y, z, c), "z": (x, y, z ^ 2, c)}[axis]

    return lax.ppermute(value, AXES, pairs_of(partner))


def to_other_core(value):
    return lax.ppermute(value, AXES, pairs_of(lambda x, y, z, c: (x, y, z, 1 - c)))


def to_mate(value, flip):
    return lax.ppermute(value, AXES, pairs_of(lambda x, y, z, c: (x ^ 1, y, z, c ^ flip)))


def activation_slope(pre_act):
    sigma = jax.nn.sigmoid(pre_act)
    return sigma + pre_act * sigma * (1.0 - sigma)


def mm(a, b, ca, cb):
    return lax.dot_general(a, b, (((ca,), (cb,)), ((), ())), preferred_element_type=F32)


def at(array, index, dim=0):
    starts = [jnp.int32(0)] * array.ndim
    starts[dim] = index
    sizes = list(array.shape)
    sizes[dim] = 1
    piece = lax.dynamic_slice(array, starts, sizes, allow_negative_indices=False)
    return piece.reshape(array.shape[:dim] + array.shape[dim + 1 :])


def slot_of(apart, core):
    on_core0 = apart ^ (apart >> 1)
    on_core1 = (on_core0 & 1) * 2 + (on_core0 >> 1)
    return jnp.where(core == 0, on_core0, on_core1)


def order_spec(array):
    tile = (min(16, array.shape[-2]), min(128, array.shape[-1]))
    return pl.BlockSpec((1,) * (array.ndim - 2) + tile, lambda *args: (0,) * array.ndim)


def order_kernel(turn, where_ref, w_ref, dep_ref, own_ref, give_ref):
    block = w_ref[0].T if turn else w_ref[0]
    core = where_ref[2]
    for zz in range(4):
        even = block[2 * zz * COLS : (2 * zz + 1) * COLS]
        odd = block[(2 * zz + 1) * COLS : (2 * zz + 2) * COLS]
        apart = zz ^ where_ref[3]
        own_ref[0, 0, slot_of(apart, core)] = jnp.where(core == 0, even, odd)
        give_ref[0, 0, slot_of(apart, 1 - core)] = jnp.where(core == 0, odd, even)


def ordered_weights(weights, where, dep, turn):
    count = weights.shape[0]
    if turn:
        in_spec = pl.BlockSpec((1, HALF, WIDE), lambda i, h, s: (i, s[0], h))
    else:
        in_spec = pl.BlockSpec((1, WIDE, HALF), lambda i, h, s: (i, h, s[0]))
    out_spec = pl.BlockSpec((1, 1, 4, COLS, HALF), lambda i, h, s: (i, (h + s[1]) % 2, 0, 0, 0))
    shape = jax.ShapeDtypeStruct((count, 2, 4, COLS, HALF), BF)
    return pl.pallas_call(
        functools.partial(order_kernel, turn),
        grid_spec=pltpu.PrefetchScalarGridSpec(
            num_scalar_prefetch=1,
            grid=(count, 2),
            in_specs=[in_spec, order_spec(dep)],
            out_specs=[out_spec, out_spec],
        ),
        out_shape=[shape, shape],
        compiler_params=pltpu.CompilerParams(vmem_limit_bytes=SMALL),
        cost_estimate=NO_COST,
    )(where, weights, dep)


def join_kernel(own_ref, got_ref, dep_ref, out_ref):
    first = pl.program_id(0) == 0
    for hi in range(2):
        for slot in range(4):
            chunk = jnp.where(first, slot * 2 + hi, hi * 4 + slot)
            out_ref[0, chunk, :, :HALF] = own_ref[0, hi, slot]
            out_ref[0, chunk, :, HALF:] = got_ref[0, hi, slot]


def joined_weights(own, got, dep):
    count = own.shape[0]
    in_spec = pl.BlockSpec((1, 2, 4, COLS, HALF), lambda i: (i, 0, 0, 0, 0))
    out = pl.pallas_call(
        join_kernel,
        grid=(count,),
        in_specs=[in_spec, in_spec, order_spec(dep)],
        out_specs=pl.BlockSpec((1, 8, COLS, 2 * HALF), lambda i: (i, 0, 0, 0)),
        out_shape=jax.ShapeDtypeStruct((count, 8, COLS, 2 * HALF), BF),
        compiler_params=pltpu.CompilerParams(vmem_limit_bytes=12 * 1024 * 1024),
        cost_estimate=NO_COST,
    )(own, got, dep)
    return out.reshape(count, WIDE, 2 * HALF)


def pass_on(value, first, count, *deps):
    def kernel(value_ref, *refs):
        refs[-1][...] = value_ref[...]

    block = (1,) + value.shape[1:]
    return pl.pallas_call(
        kernel,
        grid=(count,),
        in_specs=[pl.BlockSpec(block, lambda i: (first + i,) + (0,) * (value.ndim - 1))]
        + [order_spec(dep) for dep in deps],
        out_specs=pl.BlockSpec(block, lambda i: (i,) + (0,) * (value.ndim - 1)),
        out_shape=jax.ShapeDtypeStruct((count,) + value.shape[1:], value.dtype),
        compiler_params=pltpu.CompilerParams(vmem_limit_bytes=SMALL),
        cost_estimate=NO_COST,
    )(value, *deps)


def pack_x(core, own, first, second, far, deps):
    def kernel(core_ref, own_ref, first_ref, second_ref, far_ref, *rest):
        out_ref = rest[-1]
        swap = core_ref[0] != 0
        out_ref[0, :, :ROWS] = own_ref[...]
        out_ref[1, :, :ROWS] = far_ref[...]
        out_ref[0, :, ROWS:] = jnp.where(swap, second_ref[...], first_ref[...])
        out_ref[1, :, ROWS:] = jnp.where(swap, first_ref[...], second_ref[...])

    return pl.pallas_call(
        kernel,
        grid=(1,),
        in_specs=[pl.BlockSpec(memory_space=pltpu.SMEM)]
        + [pl.BlockSpec(memory_space=pltpu.VMEM)] * 4
        + [order_spec(dep) for dep in deps],
        out_specs=pl.BlockSpec(memory_space=pltpu.VMEM),
        out_shape=jax.ShapeDtypeStruct((2, COLS, 2 * ROWS), BF),
        compiler_params=pltpu.CompilerParams(vmem_limit_bytes=SMALL),
        cost_estimate=NO_COST,
    )(core, own, first, second, far, *deps)


def pack_z(pieces, deps):
    def kernel(*refs):
        for k in range(4):
            refs[-1][k] = refs[k][...]

    return pl.pallas_call(
        kernel,
        grid=(1,),
        in_specs=[pl.BlockSpec(memory_space=pltpu.VMEM)] * 4 + [order_spec(dep) for dep in deps],
        out_specs=pl.BlockSpec(memory_space=pltpu.VMEM),
        out_shape=jax.ShapeDtypeStruct((4, COLS, ROWS), BF),
        compiler_params=pltpu.CompilerParams(vmem_limit_bytes=SMALL),
        cost_estimate=NO_COST,
    )(*pieces, *deps)


def sum_kernel(core_ref, own_ref, oth_ref, got_own_ref, got_oth_ref, two_ref, got_two_ref, *outs):
    own = own_ref[...] + got_own_ref[...].astype(F32)
    oth = oth_ref[...] + got_oth_ref[...].astype(F32)
    two = two_ref[...] + got_two_ref[...].astype(F32)
    swap = core_ref[0] != 0
    keep1_ref, first1_ref, second1_ref, far1_ref, keep2_ref, first2_ref, second2_ref, far2_ref = outs
    keep1_ref[...] = own[0]
    first1_ref[...] = jnp.where(swap, oth[1], oth[0]).astype(BF)
    second1_ref[...] = jnp.where(swap, oth[0], oth[1]).astype(BF)
    far1_ref[...] = own[1].astype(BF)
    keep2_ref[...] = two[0]
    first2_ref[...] = two[1].astype(BF)
    second2_ref[...] = two[2].astype(BF)
    far2_ref[...] = two[3].astype(BF)


def heavy_sum(core, one, got1, two, got2):
    def spec(lead, shift):
        return pl.BlockSpec((lead, COLS, 128), lambda j, c: (0, 0, j + shift))

    kept = jax.ShapeDtypeStruct((COLS, ROWS), F32)
    give = jax.ShapeDtypeStruct((COLS, ROWS), BF)
    out = pl.pallas_call(
        sum_kernel,
        grid_spec=pltpu.PrefetchScalarGridSpec(
            num_scalar_prefetch=1,
            grid=(4,),
            in_specs=[spec(2, 0), spec(2, 4), spec(2, 0), spec(2, 4), spec(4, 0), spec(4, 0)],
            out_specs=[pl.BlockSpec((COLS, 128), lambda j, c: (0, j))] * 8,
        ),
        out_shape=[kept, give, give, give] * 2,
        compiler_params=pltpu.CompilerParams(vmem_limit_bytes=SMALL),
        cost_estimate=NO_COST,
    )(core, one, one, got1, got1, two, got2)
    return out[:4], out[4:]


def error_kernel(ids_ref, counts_ref, *refs):
    block = pl.program_id(0)
    scale = 1.0 / math.sqrt(4096)
    for k in range(2):
        recon = refs[4 * k][...]
        for got in refs[4 * k + 1 : 4 * k + 4]:
            recon = recon + got[...].astype(F32)
        live = jnp.where(block < counts_ref[k], 1.0, 0.0).astype(F32)
        refs[10 + k][...] = ((recon - refs[8 + k][0].astype(F32)) * live * scale).astype(BF)


def errors(ids, counts, one, two, targets):
    part = pl.BlockSpec((COLS, 128), lambda j, ids, counts: (0, j))
    out = jax.ShapeDtypeStruct((COLS, ROWS), BF)
    return pl.pallas_call(
        error_kernel,
        grid_spec=pltpu.PrefetchScalarGridSpec(
            num_scalar_prefetch=2,
            grid=(4,),
            in_specs=[part] * 8
            + [
                pl.BlockSpec((1, COLS, 128), lambda j, ids, counts: (ids[j], 0, 0)),
                pl.BlockSpec((1, COLS, 128), lambda j, ids, counts: (ids[4 + j], 0, 0)),
            ],
            out_specs=[part] * 2,
        ),
        out_shape=[out, out],
        compiler_params=pltpu.CompilerParams(vmem_limit_bytes=SMALL),
        cost_estimate=NO_COST,
    )(ids, counts, *one, *two, targets, targets)


def silu_kernel(part_ref, got_ref, live_ref, feat_ref):
    pre = part_ref[...] + got_ref[...].astype(F32)
    feat_ref[...] = (jax.nn.silu(pre) * live_ref[...]).astype(BF)


def silu_slope_kernel(part_ref, got_ref, live_ref, *refs):
    pre = part_ref[...] + got_ref[...].astype(F32)
    refs[-1][...] = (activation_slope(pre) * live_ref[...]).astype(BF)


def slope_kernel(part_ref, got_ref, slope_ref, *refs):
    out_ref, sum_ref = refs[-2:]
    grad = part_ref[...] + got_ref[...].astype(F32)
    grad = (grad * slope_ref[...].astype(F32)).astype(BF)
    out_ref[...] = grad
    sum_ref[...] = mm(jnp.ones((8, 2 * ROWS), BF), grad, 1, 1)


def with_other_core(kernel, part, got, extra, outs, with_sum=0, deps=()):
    tile = 128
    count = 2 * HALF // tile
    own = pl.BlockSpec((tile, 2 * ROWS), lambda i: (i, 0))
    swapped = pl.BlockSpec((tile, 2 * ROWS), lambda i: ((i + count // 2) % count, 0))
    return pl.pallas_call(
        kernel,
        grid=(count,),
        in_specs=[own, swapped]
        + [own if array.shape[0] > 1 else pl.BlockSpec((1, 2 * ROWS), lambda i: (0, 0)) for array in extra]
        + [order_spec(dep) for dep in deps],
        out_specs=[own] * len(outs) + [pl.BlockSpec((8, tile), lambda i: (0, i))] * with_sum,
        out_shape=[jax.ShapeDtypeStruct((2 * HALF, 2 * ROWS), kind) for kind in outs]
        + [jax.ShapeDtypeStruct((8, 2 * HALF), F32)] * with_sum,
        compiler_params=pltpu.CompilerParams(vmem_limit_bytes=SMALL),
        cost_estimate=NO_COST,
    )(part, got, *extra, *deps)


def term_views(terms):
    return [term.reshape((2, 4, COLS, 2 * HALF) if hi_first else (4, 2, COLS, 2 * HALF)) for term, hi_first in terms]


def term_specs(terms, place):
    def one(hi_first):
        def index(*args):
            hi, slot = place(*args)
            return (hi, slot, 0, 0) if hi_first else (slot, hi, 0, 0)

        return pl.BlockSpec((1, 1, COLS, 2 * HALF), index)

    return [one(hi_first) for _, hi_first in terms]


MORE = 16


def more_rows(sums):
    row = jnp.concatenate([ref[:, :HALF] for ref in sums], axis=1)
    return jnp.concatenate([row, row], axis=0)


def y_give(scalars, terms, deps=(), sums=()):
    count = len(terms)
    rows = COLS + (MORE if sums else 0)

    def kernel(s_ref, *refs):
        for k in range(count):
            refs[-1][0, k, 0, :COLS] = refs[k][0, 0]
        if sums:
            refs[-1][0, 0, 0, COLS:] = more_rows(refs[count : count + 2]).astype(BF)

    return pl.pallas_call(
        kernel,
        grid_spec=pltpu.PrefetchScalarGridSpec(
            num_scalar_prefetch=1,
            grid=(2, 2),
            in_specs=term_specs(terms, lambda i, hi, s: (hi, s[2 + i]))
            + [pl.BlockSpec((8, 2 * HALF), lambda i, hi, s: (0, 0))] * len(sums)
            + [order_spec(dep) for dep in deps],
            out_specs=pl.BlockSpec((1, count, 1, rows, 2 * HALF), lambda i, hi, s: (i, 0, hi, 0, 0)),
        ),
        out_shape=jax.ShapeDtypeStruct((2, count, 2, rows, 2 * HALF), BF),
        compiler_params=pltpu.CompilerParams(vmem_limit_bytes=SMALL),
        cost_estimate=NO_COST,
    )(scalars, *term_views(terms), *sums, *deps)


def y_near(scalars, terms, got, deps=(), sums=()):
    count = len(terms)
    rows = got.shape[3]

    def kernel(s_ref, *refs):
        got_ref = refs[2 * count]
        near_ref, keep_ref = refs[-2:]
        for k in range(count):
            first = refs[k][0, 0].astype(F32) + got_ref[1, k, 0, :COLS].astype(F32)
            near_ref[k, 0, :COLS] = first.astype(BF)
            keep = refs[count + k][0, 0].astype(F32) + got_ref[0, k, 0, :COLS].astype(F32)
            keep_ref[k, 0, :COLS] = keep.astype(BF)
        if sums:
            more = more_rows(refs[2 * count + 1 : 2 * count + 3])
            near_ref[0, 0, COLS:] = (more + got_ref[1, 0, 0, COLS:].astype(F32)).astype(BF)
            keep_ref[0, 0, COLS:] = (more + got_ref[0, 0, 0, COLS:].astype(F32)).astype(BF)

    out = pl.BlockSpec((count, 1, rows, 2 * HALF), lambda hi, s: (0, hi, 0, 0))
    shape = (count, 2, rows, 2 * HALF)
    return pl.pallas_call(
        kernel,
        grid_spec=pltpu.PrefetchScalarGridSpec(
            num_scalar_prefetch=1,
            grid=(2,),
            in_specs=term_specs(terms, lambda hi, s: (hi, s[1]))
            + term_specs(terms, lambda hi, s: (hi, s[0]))
            + [pl.BlockSpec((2, count, 1, rows, 2 * HALF), lambda hi, s: (0, 0, hi, 0, 0))]
            + [pl.BlockSpec((8, 2 * HALF), lambda hi, s: (0, 0))] * len(sums)
            + [order_spec(dep) for dep in deps],
            out_specs=[out, out],
        ),
        out_shape=[jax.ShapeDtypeStruct(shape, BF)] * 2,
        compiler_params=pltpu.CompilerParams(vmem_limit_bytes=SMALL),
        cost_estimate=NO_COST,
    )(scalars, *term_views(terms), *term_views(terms), got, *sums, *deps)


def y_quarters(scalars, keep, last, deps=()):
    count, _, rows, _ = keep.shape

    def kernel(s_ref, keep_ref, last_ref, *refs):
        outs = refs[len(deps) :]
        totals = [keep_ref[k, 0].astype(F32) + last_ref[k, 0].astype(F32) for k in range(count)]

        @pl.when(pl.program_id(0) == 0)
        def _():
            for k, total in enumerate(totals):
                outs[0][k] = total[:COLS, :HALF]
                outs[1][k] = total[:COLS, HALF:].astype(BF)
            if rows > COLS:
                outs[4][...] = totals[0][COLS:]

        @pl.when(pl.program_id(0) == 1)
        def _():
            for k, total in enumerate(totals):
                outs[2][k] = total[:COLS, :HALF].astype(BF)
                outs[3][k] = total[:COLS, HALF:].astype(BF)

    part = pl.BlockSpec((count, 1, rows, 2 * HALF), lambda i, s: (0, (i + s[4]) % 2, 0, 0))
    out = pl.BlockSpec((count, COLS, HALF), lambda i, s: (0, 0, 0))
    sent = jax.ShapeDtypeStruct((count, COLS, HALF), BF)
    more = rows - COLS
    same, core, mate, both, *sums = pl.pallas_call(
        kernel,
        grid_spec=pltpu.PrefetchScalarGridSpec(
            num_scalar_prefetch=1,
            grid=(2,),
            in_specs=[part, part] + [order_spec(dep) for dep in deps],
            out_specs=[out] * 4 + [pl.BlockSpec((MORE, 2 * HALF), lambda i, s: (0, 0))] * (more // MORE),
        ),
        out_shape=[jax.ShapeDtypeStruct((count, COLS, HALF), F32), sent, sent, sent]
        + [jax.ShapeDtypeStruct((MORE, 2 * HALF), F32)] * (more // MORE),
        compiler_params=pltpu.CompilerParams(vmem_limit_bytes=SMALL),
        cost_estimate=NO_COST,
    )(scalars, keep, last, *deps)
    return (same, to_other_core(core), to_mate(mate, 0), to_mate(both, 1)), sums


def write_out(place, groups, picks, deps=()):
    def kernel(place_ref, *refs):
        core, x_lo = place_ref[0], place_ref[1]
        for n, (group, k) in enumerate(picks):
            same, from_core, from_mate, from_both = [ref[k].astype(F32) for ref in refs[4 * group : 4 * group + 4]]

            def side(own, mate):
                return jnp.where(
                    x_lo == 0, jnp.concatenate([own, mate], axis=1), jnp.concatenate([mate, own], axis=1)
                )

            refs[-1][n, pl.ds(pl.multiple_of(core * COLS, 8), COLS), :] = side(same, from_mate)
            refs[-1][n, pl.ds(pl.multiple_of((1 - core) * COLS, 8), COLS), :] = side(from_core, from_both)

    flat = [array for group in groups for array in group]
    return pl.pallas_call(
        kernel,
        in_specs=[pl.BlockSpec(memory_space=pltpu.SMEM)] + [pl.BlockSpec(memory_space=pltpu.VMEM)] * len(flat + list(deps)),
        out_specs=pl.BlockSpec(memory_space=pltpu.VMEM),
        out_shape=jax.ShapeDtypeStruct((len(picks), 2 * COLS, 2 * HALF), F32),
        compiler_params=pltpu.CompilerParams(vmem_limit_bytes=SMALL),
        cost_estimate=NO_COST,
    )(place, *flat, *deps)


def per_device(cache_in, cache_out, read_list, live_blocks, encoder, enc_bias, decoder):
    t = lax.axis_index("tok")
    l = lax.axis_index("layer")
    x_lo, y = t // 4, t % 4
    x_hi, z, core = l // 8, (l // 2) % 4, l % 2
    is_core0 = core == 0
    block_ids = read_list[0]

    def picked(cache):
        rows = cache.at[block_ids].get(mode="promise_in_bounds")
        return rows.reshape(2, ROWS, COLS).transpose(0, 2, 1)

    core_ref = core.reshape(1)

    def gather_both(one, two, steps=None):
        far1, far2 = exchange_far(one, "x"), exchange_far(two, "z")
        got2 = exchange(two, "z", 0), exchange(two, "z", 1), far2
        got1 = exchange(one, "x", 0), exchange(one, "x", 1), far1
        arrived = got2[0]
        block2 = pack_z((two,) + got2, got1)
        block1 = pack_x(core_ref, one, *got1, got2)
        got1, got2 = exchange(block1, "z", 0), exchange(block2, "x", 0)
        if steps is not None:
            steps.extend([arrived, block1, got2])
        more1 = [exchange(block1, "z", 1), exchange(got1, "z", 1)]
        more2 = [exchange(block2, "x", 1), exchange(got2, "x", 1)]
        near = jnp.where(is_core0, got2, more2[0])
        away = jnp.where(is_core0, more2[0], got2)

        def rows(*parts):
            return tuple(p.reshape(WIDE // 4, 2 * ROWS) for p in parts)

        return (
            rows(block1, got1, *more1),
            (
                jnp.concatenate([block2, near], axis=2).reshape(WIDE // 2, 2 * ROWS),
                jnp.concatenate([more2[1], away], axis=2).reshape(WIDE // 2, 2 * ROWS),
            ),
        )

    own_in = picked(cache_in)
    steps = []
    in0, in1 = gather_both(own_in[0], own_in[1], steps)
    where = jnp.stack([x_lo, x_hi, core, z]).astype(jnp.int32)
    enc_own, enc_give = ordered_weights(encoder, where, steps[0], False)
    dec_own, dec_give = ordered_weights(decoder, where, steps[1], True)
    enc_w = joined_weights(enc_own, to_other_core(enc_give), steps[2])
    dec_w = joined_weights(dec_own, to_other_core(dec_give), steps[2])
    live_other = to_mate(live_blocks, 0)
    row_blocks = jnp.arange(ROWS, dtype=jnp.int32) // 128
    own_live = (row_blocks[None, :] < live_blocks[0][:, None]).astype(F32)
    other_live = (row_blocks[None, :] < live_other[0][:, None]).astype(F32)
    live = jnp.concatenate([own_live, other_live], axis=1)[:, None, :]
    bias_half = lax.dynamic_slice(
        enc_bias, (jnp.int32(0), x_lo * HALF), (2, HALF), allow_negative_indices=False
    )
    bias_mine = jnp.concatenate([bias_half, jnp.zeros_like(bias_half)], axis=1)[:, :, None]

    inputs = (in0, in1)
    mid = WIDE // 2

    def over_width(mat, parts):
        size = WIDE // len(parts)
        total = mm(mat[:size], parts[0], 0, 0)
        for i in range(1, len(parts)):
            total = total + mm(mat[i * size : (i + 1) * size], parts[i], 0, 0)
        return total

    def encode(k):
        total = over_width(enc_w[k], inputs[k]) + bias_mine[k]
        other = to_other_core(total.astype(BF))
        return with_other_core(silu_kernel, total, other, (live[k],), (BF,))[0], total, other

    feats, totals, others = zip(*[encode(k) for k in range(2)])

    low = mid // 2
    dec_hi = [dec_w[k].reshape(2, mid, 2 * HALF) for k in (1, 2)]

    def slot_term(k):
        return mm(dec_w[0][k * low : (k + 1) * low], feats[0], 1, 0)

    def quarter(hi, first):
        total = mm(at(dec_hi[0], hi), feats[0][:, first : first + ROWS], 1, 0)
        return total + mm(at(dec_hi[1], hi), feats[1][:, first : first + ROWS], 1, 0)

    got = [
        exchange(slot_term(3).astype(BF), "z", 1),
        exchange(quarter(1, 0).astype(BF), "x", 1),
        exchange(slot_term(2).astype(BF), "z", 1),
        exchange(quarter(1 - core, ROWS).astype(BF), "x", 1),
    ]
    slopes = [
        with_other_core(silu_slope_kernel, totals[k], others[k], (live[k],), (BF,), 0, (got[0],))[0]
        for k in range(2)
    ]
    give1 = (slot_term(1) + got[0].astype(F32)).astype(BF)
    give2 = (quarter(core, ROWS) + got[1].astype(F32)).astype(BF)
    block1 = (slot_term(0) + got[2].astype(F32)).reshape(2, COLS, 2 * ROWS)
    block2 = (quarter(0, 0) + got[3].astype(F32)).reshape(4, COLS, ROWS)
    got1, got2 = exchange(give1, "z", 0), exchange(give2, "x", 0)
    one, two = heavy_sum(
        core_ref, block1, got1.reshape(2, COLS, 2 * ROWS), block2, got2.reshape(4, COLS, ROWS)
    )
    far1, far2 = exchange_far(one[3], "x"), exchange_far(two[3], "z")
    got2 = exchange(two[1], "z", 0), exchange(two[2], "z", 1), far2
    got1 = exchange(one[1], "x", 0), exchange(one[2], "x", 1), far1
    own_err = errors(
        block_ids, live_blocks[0], (one[0],) + got1, (two[0],) + got2, cache_out.transpose(0, 2, 1)
    )

    err0, err1 = gather_both(*own_err)

    err0, err1 = jnp.concatenate(err0), jnp.concatenate(err1)

    def width_grad(whole, other, hi_first):
        return mm(whole, other, 1, 1).astype(BF), hi_first

    m_first = jnp.where(is_core0, 1, 3)
    m_second = jnp.where(is_core0, 3, 1)
    scalars = jnp.stack([slot_of(z ^ y ^ m, core) for m in (0, m_first, m_second, 2)] + [x_lo ^ x_hi])
    scalars = scalars.astype(jnp.int32)
    place = jnp.stack([core, x_lo]).astype(jnp.int32)

    def backward(k, total, deps=()):
        other = to_other_core(total.astype(BF))
        return with_other_core(slope_kernel, total, other, (slopes[k],), (BF,), 1, deps)

    terms_a = [width_grad(err1, feats[0], True), width_grad(err1, feats[1], True)]
    give_a = y_give(scalars, terms_a)
    got_a = exchange(give_a, "y", 1)
    gpre1, sum1 = backward(1, mm(pass_on(dec_w, 2, 1, give_a)[0], err1, 0, 0))
    terms_b = [width_grad(err0, feats[0], False), width_grad(jnp.concatenate(in1), gpre1, True)]
    give_b = y_give(scalars, terms_b)
    got_b = exchange(give_b, "y", 1)
    near_a, keep_a = y_near(scalars, terms_a, got_a, (give_b,))
    last_a = exchange(near_a, "y", 0)
    back_w = pass_on(dec_w, 0, 2, give_b)
    gpre0, sum0 = backward(0, mm(back_w[1], err1, 0, 0) + mm(back_w[0], err0, 0, 0), (near_a,))
    terms_c = [width_grad(jnp.concatenate(in0), gpre0, False)]
    give_c = y_give(scalars, terms_c, (), (sum0, sum1))
    got_c = exchange(give_c, "y", 1)

    near_b, keep_b = y_near(scalars, terms_b, got_b, (give_c,))
    last_b = exchange(near_b, "y", 0)
    done_a, _ = y_quarters(scalars, keep_a, last_a, (near_b,))
    near_c, keep_c = y_near(scalars, terms_c, got_c, done_a, (sum0, sum1))
    last_c = exchange(near_c, "y", 0)
    done_b, _ = y_quarters(scalars, keep_b, last_b, (near_c,))
    done_c, sums = y_quarters(scalars, keep_c, last_c, done_b[:2])
    bias_out = at(sums[0][0].reshape(2, 4, 64), y, 1)
    dec_out = write_out(place, (done_a, done_b), ((1, 0), (0, 0), (0, 1)), done_c[:1]).transpose(0, 2, 1)
    enc_out = write_out(place, (done_b, done_c), ((1, 0), (0, 1)))
    return (enc_out, bias_out[:, None, :], dec_out)


def solution(mesh):
    return jax.shard_map(
        per_device,
        mesh=mesh,
        in_specs=(
            P("tok", None, "layer"),
            P("tok", None, "layer"),
            P("tok", None),
            P("tok", None),
            P(None, None, "layer"),
            P(None, "layer"),
            P(None, "layer", None),
        ),
        out_specs=(P(None, "tok", "layer"), P(None, "layer", "tok"), P(None, "layer", "tok")),
        check_vma=False,
    )
```

```python
import functools
import math

import jax
import jax.numpy as jnp
from jax import lax
from jax.experimental import pallas as pl
from jax.experimental.pallas import tpu as pltpu
from jax.sharding import PartitionSpec as P

AXES = ("tok", "layer")
BF = jnp.bfloat16
F32 = jnp.float32
ROWS = 512
COLS = 144
HALF = 256
WIDE = 8 * COLS
SMALL = 8 * 1024 * 1024
NO_COST = pl.CostEstimate(flops=0, bytes_accessed=0, transcendentals=0)


def device_index(x, y, z, c):
    return ((x % 2) * 4 + y) * 16 + (x // 2) * 8 + z * 2 + c


def pairs_of(partner):
    out = []
    for x in range(4):
        for y in range(4):
            for z in range(4):
                for c in range(2):
                    out.append((device_index(x, y, z, c), device_index(*partner(x, y, z, c))))
    return out


def mask(step, c):
    return 1 if (step + c) % 2 == 0 else 3


def exchange(value, axis, step):
    def partner(x, y, z, c):
        m = mask(step, c)
        return {"x": (x ^ m, y, z, c), "y": (x, y ^ m, z, c), "z": (x, y, z ^ m, c)}[axis]

    return lax.ppermute(value, AXES, pairs_of(partner))


def exchange_far(value, axis):
    def partner(x, y, z, c):
        return {"x": (x ^ 2, y, z, c), "z": (x, y, z ^ 2, c)}[axis]

    return lax.ppermute(value, AXES, pairs_of(partner))


def to_other_core(value):
    return lax.ppermute(value, AXES, pairs_of(lambda x, y, z, c: (x, y, z, 1 - c)))


def to_mate(value, flip):
    return lax.ppermute(value, AXES, pairs_of(lambda x, y, z, c: (x ^ 1, y, z, c ^ flip)))


def activation_slope(pre_act):
    sigma = jax.nn.sigmoid(pre_act)
    return sigma + pre_act * sigma * (1.0 - sigma)


def mm(a, b, ca, cb):
    return lax.dot_general(a, b, (((ca,), (cb,)), ((), ())), preferred_element_type=F32)


def at(array, index, dim=0):
    starts = [jnp.int32(0)] * array.ndim
    starts[dim] = index
    sizes = list(array.shape)
    sizes[dim] = 1
    piece = lax.dynamic_slice(array, starts, sizes, allow_negative_indices=False)
    return piece.reshape(array.shape[:dim] + array.shape[dim + 1 :])


def slot_of(apart, core):
    on_core0 = apart ^ (apart >> 1)
    on_core1 = (on_core0 & 1) * 2 + (on_core0 >> 1)
    return jnp.where(core == 0, on_core0, on_core1)


def order_spec(array):
    tile = (min(16, array.shape[-2]), min(128, array.shape[-1]))
    return pl.BlockSpec((1,) * (array.ndim - 2) + tile, lambda *args: (0,) * array.ndim)


def order_kernel(turn, where_ref, w_ref, dep_ref, own_ref, give_ref):
    block = w_ref[0].T if turn else w_ref[0]
    core = where_ref[2]
    for zz in range(4):
        even = block[2 * zz * COLS : (2 * zz + 1) * COLS]
        odd = block[(2 * zz + 1) * COLS : (2 * zz + 2) * COLS]
        apart = zz ^ where_ref[3]
        own_ref[0, 0, slot_of(apart, core)] = jnp.where(core == 0, even, odd)
        give_ref[0, 0, slot_of(apart, 1 - core)] = jnp.where(core == 0, odd, even)


def ordered_weights(weights, where, dep, turn):
    count = weights.shape[0]
    if turn:
        in_spec = pl.BlockSpec((1, HALF, WIDE), lambda i, h, s: (i, s[0], h))
    else:
        in_spec = pl.BlockSpec((1, WIDE, HALF), lambda i, h, s: (i, h, s[0]))
    out_spec = pl.BlockSpec((1, 1, 4, COLS, HALF), lambda i, h, s: (i, (h + s[1]) % 2, 0, 0, 0))
    shape = jax.ShapeDtypeStruct((count, 2, 4, COLS, HALF), BF)
    return pl.pallas_call(
        functools.partial(order_kernel, turn),
        grid_spec=pltpu.PrefetchScalarGridSpec(
            num_scalar_prefetch=1,
            grid=(count, 2),
            in_specs=[in_spec, order_spec(dep)],
            out_specs=[out_spec, out_spec],
        ),
        out_shape=[shape, shape],
        compiler_params=pltpu.CompilerParams(vmem_limit_bytes=SMALL),
        cost_estimate=NO_COST,
    )(where, weights, dep)


def join_kernel(own_ref, got_ref, dep_ref, out_ref):
    first = pl.program_id(0) == 0
    for hi in range(2):
        for slot in range(4):
            chunk = jnp.where(first, slot * 2 + hi, hi * 4 + slot)
            out_ref[0, chunk, :, :HALF] = own_ref[0, hi, slot]
            out_ref[0, chunk, :, HALF:] = got_ref[0, hi, slot]


def joined_weights(own, got, dep):
    count = own.shape[0]
    in_spec = pl.BlockSpec((1, 2, 4, COLS, HALF), lambda i: (i, 0, 0, 0, 0))
    out = pl.pallas_call(
        join_kernel,
        grid=(count,),
        in_specs=[in_spec, in_spec, order_spec(dep)],
        out_specs=pl.BlockSpec((1, 8, COLS, 2 * HALF), lambda i: (i, 0, 0, 0)),
        out_shape=jax.ShapeDtypeStruct((count, 8, COLS, 2 * HALF), BF),
        compiler_params=pltpu.CompilerParams(vmem_limit_bytes=12 * 1024 * 1024),
        cost_estimate=NO_COST,
    )(own, got, dep)
    return out.reshape(count, WIDE, 2 * HALF)


def pass_on(value, first, count, *deps):
    def kernel(value_ref, *refs):
        refs[-1][...] = value_ref[...]

    block = (1,) + value.shape[1:]
    return pl.pallas_call(
        kernel,
        grid=(count,),
        in_specs=[pl.BlockSpec(block, lambda i: (first + i,) + (0,) * (value.ndim - 1))]
        + [order_spec(dep) for dep in deps],
        out_specs=pl.BlockSpec(block, lambda i: (i,) + (0,) * (value.ndim - 1)),
        out_shape=jax.ShapeDtypeStruct((count,) + value.shape[1:], value.dtype),
        compiler_params=pltpu.CompilerParams(vmem_limit_bytes=SMALL),
        cost_estimate=NO_COST,
    )(value, *deps)


def pack_x(core, own, first, second, far, deps):
    def kernel(core_ref, own_ref, first_ref, second_ref, far_ref, *rest):
        out_ref = rest[-1]
        swap = core_ref[0] != 0
        out_ref[0, :, :ROWS] = own_ref[...]
        out_ref[1, :, :ROWS] = far_ref[...]
        out_ref[0, :, ROWS:] = jnp.where(swap, second_ref[...], first_ref[...])
        out_ref[1, :, ROWS:] = jnp.where(swap, first_ref[...], second_ref[...])

    return pl.pallas_call(
        kernel,
        grid=(1,),
        in_specs=[pl.BlockSpec(memory_space=pltpu.SMEM)]
        + [pl.BlockSpec(memory_space=pltpu.VMEM)] * 4
        + [order_spec(dep) for dep in deps],
        out_specs=pl.BlockSpec(memory_space=pltpu.VMEM),
        out_shape=jax.ShapeDtypeStruct((2, COLS, 2 * ROWS), BF),
        compiler_params=pltpu.CompilerParams(vmem_limit_bytes=SMALL),
        cost_estimate=NO_COST,
    )(core, own, first, second, far, *deps)


def pack_z(pieces, deps):
    def kernel(*refs):
        for k in range(4):
            refs[-1][k] = refs[k][...]

    return pl.pallas_call(
        kernel,
        grid=(1,),
        in_specs=[pl.BlockSpec(memory_space=pltpu.VMEM)] * 4 + [order_spec(dep) for dep in deps],
        out_specs=pl.BlockSpec(memory_space=pltpu.VMEM),
        out_shape=jax.ShapeDtypeStruct((4, COLS, ROWS), BF),
        compiler_params=pltpu.CompilerParams(vmem_limit_bytes=SMALL),
        cost_estimate=NO_COST,
    )(*pieces, *deps)


def sum_kernel(core_ref, own_ref, oth_ref, got_own_ref, got_oth_ref, two_ref, got_two_ref, *refs):
    own = own_ref[...] + got_own_ref[...].astype(F32)
    oth = oth_ref[...] + got_oth_ref[...].astype(F32)
    two = two_ref[...] + got_two_ref[...].astype(F32)
    swap = core_ref[0] != 0
    keep1_ref, first1_ref, second1_ref, far1_ref, keep2_ref, first2_ref, second2_ref, far2_ref = refs[-8:]
    keep1_ref[...] = own[0]
    first1_ref[...] = jnp.where(swap, oth[1], oth[0]).astype(BF)
    second1_ref[...] = jnp.where(swap, oth[0], oth[1]).astype(BF)
    far1_ref[...] = own[1].astype(BF)
    keep2_ref[...] = two[0]
    first2_ref[...] = two[1].astype(BF)
    second2_ref[...] = two[2].astype(BF)
    far2_ref[...] = two[3].astype(BF)


def heavy_sum(core, one, got1, two, got2, deps):
    def spec(lead, shift):
        return pl.BlockSpec((lead, COLS, 128), lambda j, c: (0, 0, j + shift))

    kept = jax.ShapeDtypeStruct((COLS, ROWS), F32)
    give = jax.ShapeDtypeStruct((COLS, ROWS), BF)
    out = pl.pallas_call(
        sum_kernel,
        grid_spec=pltpu.PrefetchScalarGridSpec(
            num_scalar_prefetch=1,
            grid=(4,),
            in_specs=[spec(2, 0), spec(2, 4), spec(2, 0), spec(2, 4), spec(4, 0), spec(4, 0)]
            + [order_spec(dep) for dep in deps],
            out_specs=[pl.BlockSpec((COLS, 128), lambda j, c: (0, j))] * 8,
        ),
        out_shape=[kept, give, give, give] * 2,
        compiler_params=pltpu.CompilerParams(vmem_limit_bytes=SMALL),
        cost_estimate=NO_COST,
    )(core, one, one, got1, got1, two, got2, *deps)
    return out[:4], out[4:]


def error_kernel(ids_ref, counts_ref, *refs):
    block = pl.program_id(0)
    scale = 1.0 / math.sqrt(4096)
    for k in range(2):
        recon = refs[4 * k][...]
        for got in refs[4 * k + 1 : 4 * k + 4]:
            recon = recon + got[...].astype(F32)
        live = jnp.where(block < counts_ref[k], 1.0, 0.0).astype(F32)
        refs[10 + k][...] = ((recon - refs[8 + k][0].astype(F32)) * live * scale).astype(BF)


def errors(ids, counts, one, two, targets):
    part = pl.BlockSpec((COLS, 128), lambda j, ids, counts: (0, j))
    out = jax.ShapeDtypeStruct((COLS, ROWS), BF)
    return pl.pallas_call(
        error_kernel,
        grid_spec=pltpu.PrefetchScalarGridSpec(
            num_scalar_prefetch=2,
            grid=(4,),
            in_specs=[part] * 8
            + [
                pl.BlockSpec((1, COLS, 128), lambda j, ids, counts: (ids[j], 0, 0)),
                pl.BlockSpec((1, COLS, 128), lambda j, ids, counts: (ids[4 + j], 0, 0)),
            ],
            out_specs=[part] * 2,
        ),
        out_shape=[out, out],
        compiler_params=pltpu.CompilerParams(vmem_limit_bytes=SMALL),
        cost_estimate=NO_COST,
    )(ids, counts, *one, *two, targets, targets)


def silu_kernel(part_ref, got_ref, live_ref, feat_ref):
    pre = part_ref[...] + got_ref[...].astype(F32)
    feat_ref[...] = (jax.nn.silu(pre) * live_ref[...]).astype(BF)


def silu_slope_kernel(part_ref, got_ref, live_ref, *refs):
    pre = part_ref[...] + got_ref[...].astype(F32)
    refs[-1][...] = (activation_slope(pre) * live_ref[...]).astype(BF)


def slope_kernel(part_ref, got_ref, slope_ref, *refs):
    out_ref, sum_ref = refs[-2:]
    grad = part_ref[...] + got_ref[...].astype(F32)
    grad = (grad * slope_ref[...].astype(F32)).astype(BF)
    out_ref[...] = grad
    sum_ref[...] = mm(jnp.ones((8, 2 * ROWS), BF), grad, 1, 1)


def with_other_core(kernel, part, got, extra, outs, with_sum=0, deps=()):
    tile = 128
    count = 2 * HALF // tile
    own = pl.BlockSpec((tile, 2 * ROWS), lambda i: (i, 0))
    swapped = pl.BlockSpec((tile, 2 * ROWS), lambda i: ((i + count // 2) % count, 0))
    return pl.pallas_call(
        kernel,
        grid=(count,),
        in_specs=[own, swapped]
        + [own if array.shape[0] > 1 else pl.BlockSpec((1, 2 * ROWS), lambda i: (0, 0)) for array in extra]
        + [order_spec(dep) for dep in deps],
        out_specs=[own] * len(outs) + [pl.BlockSpec((8, tile), lambda i: (0, i))] * with_sum,
        out_shape=[jax.ShapeDtypeStruct((2 * HALF, 2 * ROWS), kind) for kind in outs]
        + [jax.ShapeDtypeStruct((8, 2 * HALF), F32)] * with_sum,
        compiler_params=pltpu.CompilerParams(vmem_limit_bytes=SMALL),
        cost_estimate=NO_COST,
    )(part, got, *extra, *deps)


def term_views(terms):
    return [term.reshape((2, 4, COLS, 2 * HALF) if hi_first else (4, 2, COLS, 2 * HALF)) for term, hi_first in terms]


def term_specs(terms, place):
    def one(hi_first):
        def index(*args):
            hi, slot = place(*args)
            return (hi, slot, 0, 0) if hi_first else (slot, hi, 0, 0)

        return pl.BlockSpec((1, 1, COLS, 2 * HALF), index)

    return [one(hi_first) for _, hi_first in terms]


MORE = 16


def more_rows(sums):
    row = jnp.concatenate([ref[:, :HALF] for ref in sums], axis=1)
    return jnp.concatenate([row, row], axis=0)


def y_give(scalars, terms, deps=(), sums=()):
    count = len(terms)
    rows = COLS + (MORE if sums else 0)

    def kernel(s_ref, *refs):
        for k in range(count):
            refs[-1][0, k, 0, :COLS] = refs[k][0, 0]
        if sums:
            refs[-1][0, 0, 0, COLS:] = more_rows(refs[count : count + 2]).astype(BF)

    return pl.pallas_call(
        kernel,
        grid_spec=pltpu.PrefetchScalarGridSpec(
            num_scalar_prefetch=1,
            grid=(2, 2),
            in_specs=term_specs(terms, lambda i, hi, s: (hi, s[2 + i]))
            + [pl.BlockSpec((8, 2 * HALF), lambda i, hi, s: (0, 0))] * len(sums)
            + [order_spec(dep) for dep in deps],
            out_specs=pl.BlockSpec((1, count, 1, rows, 2 * HALF), lambda i, hi, s: (i, 0, hi, 0, 0)),
        ),
        out_shape=jax.ShapeDtypeStruct((2, count, 2, rows, 2 * HALF), BF),
        compiler_params=pltpu.CompilerParams(vmem_limit_bytes=SMALL),
        cost_estimate=NO_COST,
    )(scalars, *term_views(terms), *sums, *deps)


def y_near(scalars, terms, got, deps=(), sums=()):
    count = len(terms)
    rows = got.shape[3]

    def kernel(s_ref, *refs):
        got_ref = refs[2 * count]
        near_ref, keep_ref = refs[-2:]
        for k in range(count):
            first = refs[k][0, 0].astype(F32) + got_ref[1, k, 0, :COLS].astype(F32)
            near_ref[k, 0, :COLS] = first.astype(BF)
            keep = refs[count + k][0, 0].astype(F32) + got_ref[0, k, 0, :COLS].astype(F32)
            keep_ref[k, 0, :COLS] = keep.astype(BF)
        if sums:
            more = more_rows(refs[2 * count + 1 : 2 * count + 3])
            near_ref[0, 0, COLS:] = (more + got_ref[1, 0, 0, COLS:].astype(F32)).astype(BF)
            keep_ref[0, 0, COLS:] = (more + got_ref[0, 0, 0, COLS:].astype(F32)).astype(BF)

    out = pl.BlockSpec((count, 1, rows, 2 * HALF), lambda hi, s: (0, hi, 0, 0))
    shape = (count, 2, rows, 2 * HALF)
    return pl.pallas_call(
        kernel,
        grid_spec=pltpu.PrefetchScalarGridSpec(
            num_scalar_prefetch=1,
            grid=(2,),
            in_specs=term_specs(terms, lambda hi, s: (hi, s[1]))
            + term_specs(terms, lambda hi, s: (hi, s[0]))
            + [pl.BlockSpec((2, count, 1, rows, 2 * HALF), lambda hi, s: (0, 0, hi, 0, 0))]
            + [pl.BlockSpec((8, 2 * HALF), lambda hi, s: (0, 0))] * len(sums)
            + [order_spec(dep) for dep in deps],
            out_specs=[out, out],
        ),
        out_shape=[jax.ShapeDtypeStruct(shape, BF)] * 2,
        compiler_params=pltpu.CompilerParams(vmem_limit_bytes=SMALL),
        cost_estimate=NO_COST,
    )(scalars, *term_views(terms), *term_views(terms), got, *sums, *deps)


def y_quarters(scalars, keep, last, deps=()):
    count, _, rows, _ = keep.shape

    def kernel(s_ref, keep_ref, last_ref, *refs):
        outs = refs[len(deps) :]
        totals = [keep_ref[k, 0].astype(F32) + last_ref[k, 0].astype(F32) for k in range(count)]

        @pl.when(pl.program_id(0) == 0)
        def _():
            for k, total in enumerate(totals):
                outs[0][k] = total[:COLS, :HALF]
                outs[1][k] = total[:COLS, HALF:].astype(BF)
            if rows > COLS:
                outs[4][...] = totals[0][COLS:]

        @pl.when(pl.program_id(0) == 1)
        def _():
            for k, total in enumerate(totals):
                outs[2][k] = total[:COLS, :HALF].astype(BF)
                outs[3][k] = total[:COLS, HALF:].astype(BF)

    part = pl.BlockSpec((count, 1, rows, 2 * HALF), lambda i, s: (0, (i + s[4]) % 2, 0, 0))
    out = pl.BlockSpec((count, COLS, HALF), lambda i, s: (0, 0, 0))
    sent = jax.ShapeDtypeStruct((count, COLS, HALF), BF)
    more = rows - COLS
    same, core, mate, both, *sums = pl.pallas_call(
        kernel,
        grid_spec=pltpu.PrefetchScalarGridSpec(
            num_scalar_prefetch=1,
            grid=(2,),
            in_specs=[part, part] + [order_spec(dep) for dep in deps],
            out_specs=[out] * 4 + [pl.BlockSpec((MORE, 2 * HALF), lambda i, s: (0, 0))] * (more // MORE),
        ),
        out_shape=[jax.ShapeDtypeStruct((count, COLS, HALF), F32), sent, sent, sent]
        + [jax.ShapeDtypeStruct((MORE, 2 * HALF), F32)] * (more // MORE),
        compiler_params=pltpu.CompilerParams(vmem_limit_bytes=SMALL),
        cost_estimate=NO_COST,
    )(scalars, keep, last, *deps)
    return (same, to_other_core(core), to_mate(mate, 0), to_mate(both, 1)), sums


def write_out(place, groups, picks, deps=()):
    def kernel(place_ref, *refs):
        core, x_lo = place_ref[0], place_ref[1]
        for n, (group, k) in enumerate(picks):
            same, from_core, from_mate, from_both = [ref[k].astype(F32) for ref in refs[4 * group : 4 * group + 4]]

            def side(own, mate):
                return jnp.where(
                    x_lo == 0, jnp.concatenate([own, mate], axis=1), jnp.concatenate([mate, own], axis=1)
                )

            refs[-1][n, pl.ds(pl.multiple_of(core * COLS, 8), COLS), :] = side(same, from_mate)
            refs[-1][n, pl.ds(pl.multiple_of((1 - core) * COLS, 8), COLS), :] = side(from_core, from_both)

    flat = [array for group in groups for array in group]
    return pl.pallas_call(
        kernel,
        in_specs=[pl.BlockSpec(memory_space=pltpu.SMEM)] + [pl.BlockSpec(memory_space=pltpu.VMEM)] * len(flat + list(deps)),
        out_specs=pl.BlockSpec(memory_space=pltpu.VMEM),
        out_shape=jax.ShapeDtypeStruct((len(picks), 2 * COLS, 2 * HALF), F32),
        compiler_params=pltpu.CompilerParams(vmem_limit_bytes=SMALL),
        cost_estimate=NO_COST,
    )(place, *flat, *deps)


def per_device(cache_in, cache_out, read_list, live_blocks, encoder, enc_bias, decoder):
    t = lax.axis_index("tok")
    l = lax.axis_index("layer")
    x_lo, y = t // 4, t % 4
    x_hi, z, core = l // 8, (l // 2) % 4, l % 2
    is_core0 = core == 0
    block_ids = read_list[0]

    def picked(cache):
        rows = cache.at[block_ids].get(mode="promise_in_bounds")
        return rows.reshape(2, ROWS, COLS).transpose(0, 2, 1)

    core_ref = core.reshape(1)

    def gather_both(one, two, steps=None):
        far1, far2 = exchange_far(one, "x"), exchange_far(two, "z")
        got2 = exchange(two, "z", 0), exchange(two, "z", 1), far2
        got1 = exchange(one, "x", 0), exchange(one, "x", 1), far1
        arrived = got2[0]
        block2 = pack_z((two,) + got2, got1)
        block1 = pack_x(core_ref, one, *got1, got2)
        got1, got2 = exchange(block1, "z", 0), exchange(block2, "x", 0)
        if steps is not None:
            steps.extend([arrived, block1, got2])
        more1 = [exchange(block1, "z", 1), exchange(got1, "z", 1)]
        more2 = [exchange(block2, "x", 1), exchange(got2, "x", 1)]
        near = jnp.where(is_core0, got2, more2[0])
        away = jnp.where(is_core0, more2[0], got2)

        def rows(*parts):
            return tuple(p.reshape(WIDE // 4, 2 * ROWS) for p in parts)

        return (
            rows(block1, got1, *more1),
            (
                jnp.concatenate([block2, near], axis=2).reshape(WIDE // 2, 2 * ROWS),
                jnp.concatenate([more2[1], away], axis=2).reshape(WIDE // 2, 2 * ROWS),
            ),
        )

    own_in = picked(cache_in)
    steps = []
    in0, in1 = gather_both(own_in[0], own_in[1], steps)
    where = jnp.stack([x_lo, x_hi, core, z]).astype(jnp.int32)
    enc_own, enc_give = ordered_weights(encoder, where, steps[0], False)
    dec_own, dec_give = ordered_weights(decoder, where, steps[1], True)
    enc_w = joined_weights(enc_own, to_other_core(enc_give), steps[2])
    dec_w = joined_weights(dec_own, to_other_core(dec_give), steps[2])
    live_other = to_mate(live_blocks, 0)
    row_blocks = jnp.arange(ROWS, dtype=jnp.int32) // 128
    own_live = (row_blocks[None, :] < live_blocks[0][:, None]).astype(F32)
    other_live = (row_blocks[None, :] < live_other[0][:, None]).astype(F32)
    live = jnp.concatenate([own_live, other_live], axis=1)[:, None, :]
    bias_half = lax.dynamic_slice(
        enc_bias, (jnp.int32(0), x_lo * HALF), (2, HALF), allow_negative_indices=False
    )
    bias_mine = jnp.concatenate([bias_half, jnp.zeros_like(bias_half)], axis=1)[:, :, None]

    inputs = (in0, in1)
    mid = WIDE // 2

    def over_width(mat, parts):
        size = WIDE // len(parts)
        total = mm(mat[:size], parts[0], 0, 0)
        for i in range(1, len(parts)):
            total = total + mm(mat[i * size : (i + 1) * size], parts[i], 0, 0)
        return total

    def encode(k):
        total = over_width(enc_w[k], inputs[k]) + bias_mine[k]
        other = to_other_core(total.astype(BF))
        return with_other_core(silu_kernel, total, other, (live[k],), (BF,))[0], total, other

    feats, totals, others = zip(*[encode(k) for k in range(2)])

    low = mid // 2
    dec_hi = [dec_w[k].reshape(2, mid, 2 * HALF) for k in (1, 2)]

    def slot_term(k):
        return mm(dec_w[0][k * low : (k + 1) * low], feats[0], 1, 0)

    def quarter(hi, first):
        total = mm(at(dec_hi[0], hi), feats[0][:, first : first + ROWS], 1, 0)
        return total + mm(at(dec_hi[1], hi), feats[1][:, first : first + ROWS], 1, 0)

    got = [
        exchange(slot_term(3).astype(BF), "z", 1),
        exchange(quarter(1, 0).astype(BF), "x", 1),
        exchange(slot_term(2).astype(BF), "z", 1),
        exchange(quarter(1 - core, ROWS).astype(BF), "x", 1),
    ]
    slopes = [
        with_other_core(silu_slope_kernel, totals[k], others[k], (live[k],), (BF,), 0, (got[0],))[0]
        for k in range(2)
    ]
    give1 = (slot_term(1) + got[0].astype(F32)).astype(BF)
    give2 = (quarter(core, ROWS) + got[1].astype(F32)).astype(BF)
    block1 = (slot_term(0) + got[2].astype(F32)).reshape(2, COLS, 2 * ROWS)
    block2 = (quarter(0, 0) + got[3].astype(F32)).reshape(4, COLS, ROWS)
    got1, got2 = exchange(give1, "z", 0), exchange(give2, "x", 0)
    one, two = heavy_sum(
        core_ref, block1, got1.reshape(2, COLS, 2 * ROWS), block2, got2.reshape(4, COLS, ROWS), slopes
    )
    far1, far2 = exchange_far(one[3], "x"), exchange_far(two[3], "z")
    got2 = exchange(two[1], "z", 0), exchange(two[2], "z", 1), far2
    got1 = exchange(one[1], "x", 0), exchange(one[2], "x", 1), far1
    own_err = errors(
        block_ids, live_blocks[0], (one[0],) + got1, (two[0],) + got2, cache_out.transpose(0, 2, 1)
    )

    err0, err1 = gather_both(*own_err)

    err0, err1 = jnp.concatenate(err0), jnp.concatenate(err1)

    def width_grad(whole, other, hi_first):
        return mm(whole, other, 1, 1).astype(BF), hi_first

    m_first = jnp.where(is_core0, 1, 3)
    m_second = jnp.where(is_core0, 3, 1)
    scalars = jnp.stack([slot_of(z ^ y ^ m, core) for m in (0, m_first, m_second, 2)] + [x_lo ^ x_hi])
    scalars = scalars.astype(jnp.int32)
    place = jnp.stack([core, x_lo]).astype(jnp.int32)

    def backward(k, total, deps=()):
        other = to_other_core(total.astype(BF))
        return with_other_core(slope_kernel, total, other, (slopes[k],), (BF,), 1, deps)

    terms_a = [width_grad(err1, feats[0], True), width_grad(err1, feats[1], True)]
    give_a = y_give(scalars, terms_a)
    got_a = exchange(give_a, "y", 1)
    gpre1, sum1 = backward(1, mm(pass_on(dec_w, 2, 1, give_a)[0], err1, 0, 0))
    terms_b = [width_grad(err0, feats[0], False), width_grad(jnp.concatenate(in1), gpre1, True)]
    give_b = y_give(scalars, terms_b)
    got_b = exchange(give_b, "y", 1)
    near_a, keep_a = y_near(scalars, terms_a, got_a, (give_b,))
    last_a = exchange(near_a, "y", 0)
    back_w = pass_on(dec_w, 0, 2, give_b)
    gpre0, sum0 = backward(0, mm(back_w[1], err1, 0, 0) + mm(back_w[0], err0, 0, 0), (near_a,))
    terms_c = [width_grad(jnp.concatenate(in0), gpre0, False)]
    give_c = y_give(scalars, terms_c, (), (sum0, sum1))
    got_c = exchange(give_c, "y", 1)

    done_a, _ = y_quarters(scalars, keep_a, last_a, (give_c,))
    near_b, keep_b = y_near(scalars, terms_b, got_b, (done_a[0],))
    last_b = exchange(near_b, "y", 0)
    near_c, keep_c = y_near(scalars, terms_c, got_c, done_a, (sum0, sum1))
    last_c = exchange(near_c, "y", 0)
    done_b, _ = y_quarters(scalars, keep_b, last_b, (near_c,))
    done_c, sums = y_quarters(scalars, keep_c, last_c, done_b[:2])
    bias_out = at(sums[0][0].reshape(2, 4, 64), y, 1)
    dec_out = write_out(place, (done_a, done_b), ((1, 0), (0, 0), (0, 1)), done_c[:1]).transpose(0, 2, 1)
    enc_out = write_out(place, (done_b, done_c), ((1, 0), (0, 1)))
    return (enc_out, bias_out[:, None, :], dec_out)


def solution(mesh):
    return jax.shard_map(
        per_device,
        mesh=mesh,
        in_specs=(
            P("tok", None, "layer"),
            P("tok", None, "layer"),
            P("tok", None),
            P("tok", None),
            P(None, None, "layer"),
            P(None, "layer"),
            P(None, "layer", None),
        ),
        out_specs=(P(None, "tok", "layer"), P(None, "layer", "tok"), P(None, "layer", "tok")),
        check_vma=False,
    )
```

```python
import functools
import math

import jax
import jax.numpy as jnp
from jax import lax
from jax.experimental import pallas as pl
from jax.experimental.pallas import tpu as pltpu
from jax.sharding import PartitionSpec as P

AXES = ("tok", "layer")
BF = jnp.bfloat16
F32 = jnp.float32
ROWS = 512
COLS = 144
HALF = 256
WIDE = 8 * COLS
SMALL = 8 * 1024 * 1024
NO_COST = pl.CostEstimate(flops=0, bytes_accessed=0, transcendentals=0)


def device_index(x, y, z, c):
    return ((x % 2) * 4 + y) * 16 + (x // 2) * 8 + z * 2 + c


def pairs_of(partner):
    out = []
    for x in range(4):
        for y in range(4):
            for z in range(4):
                for c in range(2):
                    out.append((device_index(x, y, z, c), device_index(*partner(x, y, z, c))))
    return out


def mask(step, c):
    return 1 if (step + c) % 2 == 0 else 3


def exchange(value, axis, step):
    def partner(x, y, z, c):
        m = mask(step, c)
        return {"x": (x ^ m, y, z, c), "y": (x, y ^ m, z, c), "z": (x, y, z ^ m, c)}[axis]

    return lax.ppermute(value, AXES, pairs_of(partner))


def exchange_far(value, axis):
    def partner(x, y, z, c):
        return {"x": (x ^ 2, y, z, c), "z": (x, y, z ^ 2, c)}[axis]

    return lax.ppermute(value, AXES, pairs_of(partner))


def to_other_core(value):
    return lax.ppermute(value, AXES, pairs_of(lambda x, y, z, c: (x, y, z, 1 - c)))


def to_mate(value, flip):
    return lax.ppermute(value, AXES, pairs_of(lambda x, y, z, c: (x ^ 1, y, z, c ^ flip)))


def activation_slope(pre_act):
    sigma = jax.nn.sigmoid(pre_act)
    return sigma + pre_act * sigma * (1.0 - sigma)


def mm(a, b, ca, cb):
    return lax.dot_general(a, b, (((ca,), (cb,)), ((), ())), preferred_element_type=F32)


def at(array, index, dim=0):
    starts = [jnp.int32(0)] * array.ndim
    starts[dim] = index
    sizes = list(array.shape)
    sizes[dim] = 1
    piece = lax.dynamic_slice(array, starts, sizes, allow_negative_indices=False)
    return piece.reshape(array.shape[:dim] + array.shape[dim + 1 :])


def slot_of(apart, core):
    on_core0 = apart ^ (apart >> 1)
    on_core1 = (on_core0 & 1) * 2 + (on_core0 >> 1)
    return jnp.where(core == 0, on_core0, on_core1)


def order_spec(array):
    tile = (min(16, array.shape[-2]), min(128, array.shape[-1]))
    return pl.BlockSpec((1,) * (array.ndim - 2) + tile, lambda *args: (0,) * array.ndim)


def order_kernel(turn, where_ref, w_ref, dep_ref, own_ref, give_ref):
    block = w_ref[0].T if turn else w_ref[0]
    core = where_ref[2]
    for zz in range(4):
        even = block[2 * zz * COLS : (2 * zz + 1) * COLS]
        odd = block[(2 * zz + 1) * COLS : (2 * zz + 2) * COLS]
        apart = zz ^ where_ref[3]
        own_ref[0, 0, slot_of(apart, core)] = jnp.where(core == 0, even, odd)
        give_ref[0, 0, slot_of(apart, 1 - core)] = jnp.where(core == 0, odd, even)


def ordered_weights(weights, where, dep, turn):
    count = weights.shape[0]
    if turn:
        in_spec = pl.BlockSpec((1, HALF, WIDE), lambda i, h, s: (i, s[0], h))
    else:
        in_spec = pl.BlockSpec((1, WIDE, HALF), lambda i, h, s: (i, h, s[0]))
    out_spec = pl.BlockSpec((1, 1, 4, COLS, HALF), lambda i, h, s: (i, (h + s[1]) % 2, 0, 0, 0))
    shape = jax.ShapeDtypeStruct((count, 2, 4, COLS, HALF), BF)
    return pl.pallas_call(
        functools.partial(order_kernel, turn),
        grid_spec=pltpu.PrefetchScalarGridSpec(
            num_scalar_prefetch=1,
            grid=(count, 2),
            in_specs=[in_spec, order_spec(dep)],
            out_specs=[out_spec, out_spec],
        ),
        out_shape=[shape, shape],
        compiler_params=pltpu.CompilerParams(vmem_limit_bytes=SMALL),
        cost_estimate=NO_COST,
    )(where, weights, dep)


def join_kernel(own_ref, got_ref, dep_ref, out_ref):
    first = pl.program_id(0) == 0
    for hi in range(2):
        for slot in range(4):
            chunk = jnp.where(first, slot * 2 + hi, hi * 4 + slot)
            out_ref[0, chunk, :, :HALF] = own_ref[0, hi, slot]
            out_ref[0, chunk, :, HALF:] = got_ref[0, hi, slot]


def joined_weights(own, got, dep):
    count = own.shape[0]
    in_spec = pl.BlockSpec((1, 2, 4, COLS, HALF), lambda i: (i, 0, 0, 0, 0))
    out = pl.pallas_call(
        join_kernel,
        grid=(count,),
        in_specs=[in_spec, in_spec, order_spec(dep)],
        out_specs=pl.BlockSpec((1, 8, COLS, 2 * HALF), lambda i: (i, 0, 0, 0)),
        out_shape=jax.ShapeDtypeStruct((count, 8, COLS, 2 * HALF), BF),
        compiler_params=pltpu.CompilerParams(vmem_limit_bytes=12 * 1024 * 1024),
        cost_estimate=NO_COST,
    )(own, got, dep)
    return out.reshape(count, WIDE, 2 * HALF)


def pass_on(value, first, count, *deps):
    def kernel(value_ref, *refs):
        refs[-1][...] = value_ref[...]

    block = (1,) + value.shape[1:]
    return pl.pallas_call(
        kernel,
        grid=(count,),
        in_specs=[pl.BlockSpec(block, lambda i: (first + i,) + (0,) * (value.ndim - 1))]
        + [order_spec(dep) for dep in deps],
        out_specs=pl.BlockSpec(block, lambda i: (i,) + (0,) * (value.ndim - 1)),
        out_shape=jax.ShapeDtypeStruct((count,) + value.shape[1:], value.dtype),
        compiler_params=pltpu.CompilerParams(vmem_limit_bytes=SMALL),
        cost_estimate=NO_COST,
    )(value, *deps)


def pack_x(core, own, first, second, far, deps):
    def kernel(core_ref, own_ref, first_ref, second_ref, far_ref, *rest):
        out_ref = rest[-1]
        swap = core_ref[0] != 0
        out_ref[0, :, :ROWS] = own_ref[...]
        out_ref[1, :, :ROWS] = far_ref[...]
        out_ref[0, :, ROWS:] = jnp.where(swap, second_ref[...], first_ref[...])
        out_ref[1, :, ROWS:] = jnp.where(swap, first_ref[...], second_ref[...])

    return pl.pallas_call(
        kernel,
        grid=(1,),
        in_specs=[pl.BlockSpec(memory_space=pltpu.SMEM)]
        + [pl.BlockSpec(memory_space=pltpu.VMEM)] * 4
        + [order_spec(dep) for dep in deps],
        out_specs=pl.BlockSpec(memory_space=pltpu.VMEM),
        out_shape=jax.ShapeDtypeStruct((2, COLS, 2 * ROWS), BF),
        compiler_params=pltpu.CompilerParams(vmem_limit_bytes=SMALL),
        cost_estimate=NO_COST,
    )(core, own, first, second, far, *deps)


def pack_z(pieces, deps):
    def kernel(*refs):
        for k in range(4):
            refs[-1][k] = refs[k][...]

    return pl.pallas_call(
        kernel,
        grid=(1,),
        in_specs=[pl.BlockSpec(memory_space=pltpu.VMEM)] * 4 + [order_spec(dep) for dep in deps],
        out_specs=pl.BlockSpec(memory_space=pltpu.VMEM),
        out_shape=jax.ShapeDtypeStruct((4, COLS, ROWS), BF),
        compiler_params=pltpu.CompilerParams(vmem_limit_bytes=SMALL),
        cost_estimate=NO_COST,
    )(*pieces, *deps)


def sum_kernel(core_ref, own_ref, oth_ref, got_own_ref, got_oth_ref, two_ref, got_two_ref, *refs):
    own = own_ref[...] + got_own_ref[...].astype(F32)
    oth = oth_ref[...] + got_oth_ref[...].astype(F32)
    two = two_ref[...] + got_two_ref[...].astype(F32)
    swap = core_ref[0] != 0
    keep1_ref, first1_ref, second1_ref, far1_ref, keep2_ref, first2_ref, second2_ref, far2_ref = refs[-8:]
    keep1_ref[...] = own[0]
    first1_ref[...] = jnp.where(swap, oth[1], oth[0]).astype(BF)
    second1_ref[...] = jnp.where(swap, oth[0], oth[1]).astype(BF)
    far1_ref[...] = own[1].astype(BF)
    keep2_ref[...] = two[0]
    first2_ref[...] = two[1].astype(BF)
    second2_ref[...] = two[2].astype(BF)
    far2_ref[...] = two[3].astype(BF)


def heavy_sum(core, one, got1, two, got2, deps):
    def spec(lead, shift):
        return pl.BlockSpec((lead, COLS, 128), lambda j, c: (0, 0, j + shift))

    kept = jax.ShapeDtypeStruct((COLS, ROWS), F32)
    give = jax.ShapeDtypeStruct((COLS, ROWS), BF)
    out = pl.pallas_call(
        sum_kernel,
        grid_spec=pltpu.PrefetchScalarGridSpec(
            num_scalar_prefetch=1,
            grid=(4,),
            in_specs=[spec(2, 0), spec(2, 4), spec(2, 0), spec(2, 4), spec(4, 0), spec(4, 0)]
            + [order_spec(dep) for dep in deps],
            out_specs=[pl.BlockSpec((COLS, 128), lambda j, c: (0, j))] * 8,
        ),
        out_shape=[kept, give, give, give] * 2,
        compiler_params=pltpu.CompilerParams(vmem_limit_bytes=SMALL),
        cost_estimate=NO_COST,
    )(core, one, one, got1, got1, two, got2, *deps)
    return out[:4], out[4:]


def error_kernel(ids_ref, counts_ref, *refs):
    block = pl.program_id(0)
    scale = 1.0 / math.sqrt(4096)
    for k in range(2):
        recon = refs[4 * k][...]
        for got in refs[4 * k + 1 : 4 * k + 4]:
            recon = recon + got[...].astype(F32)
        live = jnp.where(block < counts_ref[k], 1.0, 0.0).astype(F32)
        refs[10 + k][...] = ((recon - refs[8 + k][0].astype(F32)) * live * scale).astype(BF)


def errors(ids, counts, one, two, targets):
    part = pl.BlockSpec((COLS, 128), lambda j, ids, counts: (0, j))
    out = jax.ShapeDtypeStruct((COLS, ROWS), BF)
    return pl.pallas_call(
        error_kernel,
        grid_spec=pltpu.PrefetchScalarGridSpec(
            num_scalar_prefetch=2,
            grid=(4,),
            in_specs=[part] * 8
            + [
                pl.BlockSpec((1, COLS, 128), lambda j, ids, counts: (ids[j], 0, 0)),
                pl.BlockSpec((1, COLS, 128), lambda j, ids, counts: (ids[4 + j], 0, 0)),
            ],
            out_specs=[part] * 2,
        ),
        out_shape=[out, out],
        compiler_params=pltpu.CompilerParams(vmem_limit_bytes=SMALL),
        cost_estimate=NO_COST,
    )(ids, counts, *one, *two, targets, targets)


def silu_kernel(part_ref, got_ref, live_ref, feat_ref):
    pre = part_ref[...] + got_ref[...].astype(F32)
    feat_ref[...] = (jax.nn.silu(pre) * live_ref[...]).astype(BF)


def silu_slope_kernel(part_ref, got_ref, live_ref, *refs):
    pre = part_ref[...] + got_ref[...].astype(F32)
    refs[-1][...] = (activation_slope(pre) * live_ref[...]).astype(BF)


def slope_kernel(part_ref, got_ref, slope_ref, *refs):
    out_ref, sum_ref = refs[-2:]
    grad = part_ref[...] + got_ref[...].astype(F32)
    grad = (grad * slope_ref[...].astype(F32)).astype(BF)
    out_ref[...] = grad
    sum_ref[...] = mm(jnp.ones((8, 2 * ROWS), BF), grad, 1, 1)


def with_other_core(kernel, part, got, extra, outs, with_sum=0, deps=()):
    tile = 128
    count = 2 * HALF // tile
    own = pl.BlockSpec((tile, 2 * ROWS), lambda i: (i, 0))
    swapped = pl.BlockSpec((tile, 2 * ROWS), lambda i: ((i + count // 2) % count, 0))
    return pl.pallas_call(
        kernel,
        grid=(count,),
        in_specs=[own, swapped]
        + [own if array.shape[0] > 1 else pl.BlockSpec((1, 2 * ROWS), lambda i: (0, 0)) for array in extra]
        + [order_spec(dep) for dep in deps],
        out_specs=[own] * len(outs) + [pl.BlockSpec((8, tile), lambda i: (0, i))] * with_sum,
        out_shape=[jax.ShapeDtypeStruct((2 * HALF, 2 * ROWS), kind) for kind in outs]
        + [jax.ShapeDtypeStruct((8, 2 * HALF), F32)] * with_sum,
        compiler_params=pltpu.CompilerParams(vmem_limit_bytes=SMALL),
        cost_estimate=NO_COST,
    )(part, got, *extra, *deps)


def term_views(terms):
    return [term.reshape((2, 4, COLS, 2 * HALF) if hi_first else (4, 2, COLS, 2 * HALF)) for term, hi_first in terms]


def term_specs(terms, place):
    def one(hi_first):
        def index(*args):
            hi, slot = place(*args)
            return (hi, slot, 0, 0) if hi_first else (slot, hi, 0, 0)

        return pl.BlockSpec((1, 1, COLS, 2 * HALF), index)

    return [one(hi_first) for _, hi_first in terms]


MORE = 16


def more_rows(sums):
    row = jnp.concatenate([ref[:, :HALF] for ref in sums], axis=1)
    return jnp.concatenate([row, row], axis=0)


def y_give(scalars, terms, deps=(), sums=()):
    count = len(terms)
    rows = COLS + (MORE if sums else 0)

    def kernel(s_ref, *refs):
        for k in range(count):
            refs[-1][0, k, 0, :COLS] = refs[k][0, 0]
        if sums:
            refs[-1][0, 0, 0, COLS:] = more_rows(refs[count : count + 2]).astype(BF)

    return pl.pallas_call(
        kernel,
        grid_spec=pltpu.PrefetchScalarGridSpec(
            num_scalar_prefetch=1,
            grid=(2, 2),
            in_specs=term_specs(terms, lambda i, hi, s: (hi, s[2 + i]))
            + [pl.BlockSpec((8, 2 * HALF), lambda i, hi, s: (0, 0))] * len(sums)
            + [order_spec(dep) for dep in deps],
            out_specs=pl.BlockSpec((1, count, 1, rows, 2 * HALF), lambda i, hi, s: (i, 0, hi, 0, 0)),
        ),
        out_shape=jax.ShapeDtypeStruct((2, count, 2, rows, 2 * HALF), BF),
        compiler_params=pltpu.CompilerParams(vmem_limit_bytes=SMALL),
        cost_estimate=NO_COST,
    )(scalars, *term_views(terms), *sums, *deps)


def y_near(scalars, terms, got, deps=(), sums=()):
    count = len(terms)
    rows = got.shape[3]

    def kernel(s_ref, *refs):
        got_ref = refs[2 * count]
        near_ref, keep_ref = refs[-2:]
        for k in range(count):
            first = refs[k][0, 0].astype(F32) + got_ref[1, k, 0, :COLS].astype(F32)
            near_ref[k, 0, :COLS] = first.astype(BF)
            keep = refs[count + k][0, 0].astype(F32) + got_ref[0, k, 0, :COLS].astype(F32)
            keep_ref[k, 0, :COLS] = keep.astype(BF)
        if sums:
            more = more_rows(refs[2 * count + 1 : 2 * count + 3])
            near_ref[0, 0, COLS:] = (more + got_ref[1, 0, 0, COLS:].astype(F32)).astype(BF)
            keep_ref[0, 0, COLS:] = (more + got_ref[0, 0, 0, COLS:].astype(F32)).astype(BF)

    out = pl.BlockSpec((count, 1, rows, 2 * HALF), lambda hi, s: (0, hi, 0, 0))
    shape = (count, 2, rows, 2 * HALF)
    return pl.pallas_call(
        kernel,
        grid_spec=pltpu.PrefetchScalarGridSpec(
            num_scalar_prefetch=1,
            grid=(2,),
            in_specs=term_specs(terms, lambda hi, s: (hi, s[1]))
            + term_specs(terms, lambda hi, s: (hi, s[0]))
            + [pl.BlockSpec((2, count, 1, rows, 2 * HALF), lambda hi, s: (0, 0, hi, 0, 0))]
            + [pl.BlockSpec((8, 2 * HALF), lambda hi, s: (0, 0))] * len(sums)
            + [order_spec(dep) for dep in deps],
            out_specs=[out, out],
        ),
        out_shape=[jax.ShapeDtypeStruct(shape, BF)] * 2,
        compiler_params=pltpu.CompilerParams(vmem_limit_bytes=SMALL),
        cost_estimate=NO_COST,
    )(scalars, *term_views(terms), *term_views(terms), got, *sums, *deps)


def y_quarters(scalars, keep, last, deps=()):
    count, _, rows, _ = keep.shape

    def kernel(s_ref, keep_ref, last_ref, *refs):
        outs = refs[len(deps) :]
        totals = [keep_ref[k, 0].astype(F32) + last_ref[k, 0].astype(F32) for k in range(count)]

        @pl.when(pl.program_id(0) == 0)
        def _():
            for k, total in enumerate(totals):
                outs[0][k] = total[:COLS, :HALF]
                outs[1][k] = total[:COLS, HALF:].astype(BF)
            if rows > COLS:
                outs[4][...] = totals[0][COLS:]

        @pl.when(pl.program_id(0) == 1)
        def _():
            for k, total in enumerate(totals):
                outs[2][k] = total[:COLS, :HALF].astype(BF)
                outs[3][k] = total[:COLS, HALF:].astype(BF)

    part = pl.BlockSpec((count, 1, rows, 2 * HALF), lambda i, s: (0, (i + s[4]) % 2, 0, 0))
    out = pl.BlockSpec((count, COLS, HALF), lambda i, s: (0, 0, 0))
    sent = jax.ShapeDtypeStruct((count, COLS, HALF), BF)
    more = rows - COLS
    same, core, mate, both, *sums = pl.pallas_call(
        kernel,
        grid_spec=pltpu.PrefetchScalarGridSpec(
            num_scalar_prefetch=1,
            grid=(2,),
            in_specs=[part, part] + [order_spec(dep) for dep in deps],
            out_specs=[out] * 4 + [pl.BlockSpec((MORE, 2 * HALF), lambda i, s: (0, 0))] * (more // MORE),
        ),
        out_shape=[jax.ShapeDtypeStruct((count, COLS, HALF), F32), sent, sent, sent]
        + [jax.ShapeDtypeStruct((MORE, 2 * HALF), F32)] * (more // MORE),
        compiler_params=pltpu.CompilerParams(vmem_limit_bytes=SMALL),
        cost_estimate=NO_COST,
    )(scalars, keep, last, *deps)
    return (same, to_other_core(core), to_mate(mate, 0), to_mate(both, 1)), sums


def write_out(place, groups, picks, deps=()):
    def kernel(place_ref, *refs):
        core, x_lo = place_ref[0], place_ref[1]
        for n, (group, k) in enumerate(picks):
            same, from_core, from_mate, from_both = [ref[k].astype(F32) for ref in refs[4 * group : 4 * group + 4]]

            def side(own, mate):
                return jnp.where(
                    x_lo == 0, jnp.concatenate([own, mate], axis=1), jnp.concatenate([mate, own], axis=1)
                )

            refs[-1][n, pl.ds(pl.multiple_of(core * COLS, 8), COLS), :] = side(same, from_mate)
            refs[-1][n, pl.ds(pl.multiple_of((1 - core) * COLS, 8), COLS), :] = side(from_core, from_both)

    flat = [array for group in groups for array in group]
    return pl.pallas_call(
        kernel,
        in_specs=[pl.BlockSpec(memory_space=pltpu.SMEM)] + [pl.BlockSpec(memory_space=pltpu.VMEM)] * len(flat + list(deps)),
        out_specs=pl.BlockSpec(memory_space=pltpu.VMEM),
        out_shape=jax.ShapeDtypeStruct((len(picks), 2 * COLS, 2 * HALF), F32),
        compiler_params=pltpu.CompilerParams(vmem_limit_bytes=SMALL),
        cost_estimate=NO_COST,
    )(place, *flat, *deps)


def per_device(cache_in, cache_out, read_list, live_blocks, encoder, enc_bias, decoder):
    t = lax.axis_index("tok")
    l = lax.axis_index("layer")
    x_lo, y = t // 4, t % 4
    x_hi, z, core = l // 8, (l // 2) % 4, l % 2
    is_core0 = core == 0
    block_ids = read_list[0]

    def picked(cache):
        rows = cache.at[block_ids].get(mode="promise_in_bounds")
        return rows.reshape(2, ROWS, COLS).transpose(0, 2, 1)

    core_ref = core.reshape(1)

    def gather_both(one, two, steps=None):
        far1, far2 = exchange_far(one, "x"), exchange_far(two, "z")
        got2 = exchange(two, "z", 0), exchange(two, "z", 1), far2
        got1 = exchange(one, "x", 0), exchange(one, "x", 1), far1
        arrived = got2[0]
        block2 = pack_z((two,) + got2, got1)
        block1 = pack_x(core_ref, one, *got1, got2)
        got1, got2 = exchange(block1, "z", 0), exchange(block2, "x", 0)
        if steps is not None:
            steps.extend([arrived, block1, got2])
        more1 = [exchange(block1, "z", 1), exchange(got1, "z", 1)]
        more2 = [exchange(block2, "x", 1), exchange(got2, "x", 1)]
        near = jnp.where(is_core0, got2, more2[0])
        away = jnp.where(is_core0, more2[0], got2)

        def rows(*parts):
            return tuple(p.reshape(WIDE // 4, 2 * ROWS) for p in parts)

        return (
            rows(block1, got1, *more1),
            (
                jnp.concatenate([block2, near], axis=2).reshape(WIDE // 2, 2 * ROWS),
                jnp.concatenate([more2[1], away], axis=2).reshape(WIDE // 2, 2 * ROWS),
            ),
        )

    own_in = picked(cache_in)
    steps = []
    in0, in1 = gather_both(own_in[0], own_in[1], steps)
    where = jnp.stack([x_lo, x_hi, core, z]).astype(jnp.int32)
    enc_own, enc_give = ordered_weights(encoder, where, steps[0], False)
    dec_own, dec_give = ordered_weights(decoder, where, steps[1], True)
    enc_w = joined_weights(enc_own, to_other_core(enc_give), steps[2])
    dec_w = joined_weights(dec_own, to_other_core(dec_give), steps[2])
    live_other = to_mate(pass_on(live_blocks, 0, 1, steps[2]), 0)
    row_blocks = jnp.arange(ROWS, dtype=jnp.int32) // 128
    own_live = (row_blocks[None, :] < live_blocks[0][:, None]).astype(F32)
    other_live = (row_blocks[None, :] < live_other[0][:, None]).astype(F32)
    live = jnp.concatenate([own_live, other_live], axis=1)[:, None, :]
    bias_half = lax.dynamic_slice(
        enc_bias, (jnp.int32(0), x_lo * HALF), (2, HALF), allow_negative_indices=False
    )
    bias_mine = jnp.concatenate([bias_half, jnp.zeros_like(bias_half)], axis=1)[:, :, None]

    inputs = (in0, in1)
    mid = WIDE // 2

    def over_width(mat, parts):
        size = WIDE // len(parts)
        total = mm(mat[:size], parts[0], 0, 0)
        for i in range(1, len(parts)):
            total = total + mm(mat[i * size : (i + 1) * size], parts[i], 0, 0)
        return total

    def encode(k):
        total = over_width(enc_w[k], inputs[k]) + bias_mine[k]
        other = to_other_core(total.astype(BF))
        return with_other_core(silu_kernel, total, other, (live[k],), (BF,))[0], total, other

    feats, totals, others = zip(*[encode(k) for k in range(2)])

    low = mid // 2
    dec_hi = [dec_w[k].reshape(2, mid, 2 * HALF) for k in (1, 2)]

    def slot_term(k):
        return mm(dec_w[0][k * low : (k + 1) * low], feats[0], 1, 0)

    def quarter(hi, first):
        total = mm(at(dec_hi[0], hi), feats[0][:, first : first + ROWS], 1, 0)
        return total + mm(at(dec_hi[1], hi), feats[1][:, first : first + ROWS], 1, 0)

    got = [
        exchange(slot_term(3).astype(BF), "z", 1),
        exchange(quarter(1, 0).astype(BF), "x", 1),
        exchange(slot_term(2).astype(BF), "z", 1),
        exchange(quarter(1 - core, ROWS).astype(BF), "x", 1),
    ]
    slopes = [
        with_other_core(silu_slope_kernel, totals[k], others[k], (live[k],), (BF,), 0, (got[0],))[0]
        for k in range(2)
    ]
    give1 = (slot_term(1) + got[0].astype(F32)).astype(BF)
    give2 = (quarter(core, ROWS) + got[1].astype(F32)).astype(BF)
    block1 = (slot_term(0) + got[2].astype(F32)).reshape(2, COLS, 2 * ROWS)
    block2 = (quarter(0, 0) + got[3].astype(F32)).reshape(4, COLS, ROWS)
    got1, got2 = exchange(give1, "z", 0), exchange(give2, "x", 0)
    one, two = heavy_sum(
        core_ref, block1, got1.reshape(2, COLS, 2 * ROWS), block2, got2.reshape(4, COLS, ROWS), slopes
    )
    far1, far2 = exchange_far(one[3], "x"), exchange_far(two[3], "z")
    got2 = exchange(two[1], "z", 0), exchange(two[2], "z", 1), far2
    got1 = exchange(one[1], "x", 0), exchange(one[2], "x", 1), far1
    own_err = errors(
        block_ids, live_blocks[0], (one[0],) + got1, (two[0],) + got2, cache_out.transpose(0, 2, 1)
    )

    err0, err1 = gather_both(*own_err)

    err0, err1 = jnp.concatenate(err0), jnp.concatenate(err1)

    def width_grad(whole, other, hi_first):
        return mm(whole, other, 1, 1).astype(BF), hi_first

    m_first = jnp.where(is_core0, 1, 3)
    m_second = jnp.where(is_core0, 3, 1)
    scalars = jnp.stack([slot_of(z ^ y ^ m, core) for m in (0, m_first, m_second, 2)] + [x_lo ^ x_hi])
    scalars = scalars.astype(jnp.int32)
    place = jnp.stack([core, x_lo]).astype(jnp.int32)

    def backward(k, total, deps=()):
        other = to_other_core(total.astype(BF))
        return with_other_core(slope_kernel, total, other, (slopes[k],), (BF,), 1, deps)

    terms_a = [width_grad(err1, feats[0], True), width_grad(err1, feats[1], True)]
    give_a = y_give(scalars, terms_a)
    got_a = exchange(give_a, "y", 1)
    gpre1, sum1 = backward(1, mm(pass_on(dec_w, 2, 1, give_a)[0], err1, 0, 0))
    terms_b = [width_grad(err0, feats[0], False), width_grad(jnp.concatenate(in1), gpre1, True)]
    give_b = y_give(scalars, terms_b)
    got_b = exchange(give_b, "y", 1)
    near_a, keep_a = y_near(scalars, terms_a, got_a, (give_b,))
    last_a = exchange(near_a, "y", 0)
    back_w = pass_on(dec_w, 0, 2, give_b)
    gpre0, sum0 = backward(0, mm(back_w[1], err1, 0, 0) + mm(back_w[0], err0, 0, 0), (near_a,))
    terms_c = [width_grad(jnp.concatenate(in0), gpre0, False)]
    give_c = y_give(scalars, terms_c, (), (sum0, sum1))
    got_c = exchange(give_c, "y", 1)

    done_a, _ = y_quarters(scalars, keep_a, last_a, (give_c,))
    near_b, keep_b = y_near(scalars, terms_b, got_b, (done_a[0],))
    last_b = exchange(near_b, "y", 0)
    near_c, keep_c = y_near(scalars, terms_c, got_c, done_a, (sum0, sum1))
    last_c = exchange(near_c, "y", 0)
    done_b, _ = y_quarters(scalars, keep_b, last_b, (near_c,))
    done_c, sums = y_quarters(scalars, keep_c, last_c, done_b[:2])
    bias_out = at(sums[0][0].reshape(2, 4, 64), y, 1)
    dec_out = write_out(place, (done_a, done_b), ((1, 0), (0, 0), (0, 1)), done_c[:1]).transpose(0, 2, 1)
    enc_out = write_out(place, (done_b, done_c), ((1, 0), (0, 1)))
    return (enc_out, bias_out[:, None, :], dec_out)


def solution(mesh):
    return jax.shard_map(
        per_device,
        mesh=mesh,
        in_specs=(
            P("tok", None, "layer"),
            P("tok", None, "layer"),
            P("tok", None),
            P("tok", None),
            P(None, None, "layer"),
            P(None, "layer"),
            P(None, "layer", None),
        ),
        out_specs=(P(None, "tok", "layer"), P(None, "layer", "tok"), P(None, "layer", "tok")),
        check_vma=False,
    )
```
